128 devices in a mesh: ctx: 16 (over z, y), ep: 8 (over x, core).
Axes of the slice: x: 4, y: 4, z: 4, core: 2. Of those that a mesh axis runs over, the one named last changes fastest.
Arguments:
- queries: bfloat16 [4096, 8192], P('ctx', 'ep'), may hold values from -0.625 to 0.625
- keys: bfloat16 [4096, 8192], P('ctx', 'ep'), may hold values from -0.625 to 0.625
- values: bfloat16 [4096, 8192], P('ctx', 'ep'), may hold values from -0.625 to 0.625
- out_grad: bfloat16 [4096, 8192], P('ctx', 'ep'), may hold values from -0.625 to 0.625
- log_decay: float32 [64, 4096], P('ep', 'ctx'), may hold values from -1 to 0
- doc_ids: int32 [4096], P('ctx'), may hold values from 0 to 2, never falling along the last dimension, each value on 1 to 2048 neighbouring positions
- moe_input: bfloat16 [4096, 3072], P('ctx', 'ep'), may hold values from -6 to 6
- moe_cotangent: bfloat16 [4096, 3072], P('ctx', 'ep'), may hold values from -6 to 6
- router_weights: float32 [4096, 2], P('ctx'), may hold values from 0.1 to 0.9
- expert_ids: int32 [4096, 2], P('ctx'), may hold values from 0 to 15, all different within a row; in each aligned block of 256 rows (0 to 255, 256 to 511, ...) at most 40 rows name the same one
- w_gate: bfloat16 [16, 3072, 5120], P('ctx', None, 'ep'), may hold values from -0.109375 to 0.109375
- w_up: bfloat16 [16, 3072, 5120], P('ctx', None, 'ep'), may hold values from -0.109375 to 0.109375
- w_down: bfloat16 [16, 5120, 3072], P('ctx', 'ep'), may hold values from -0.078125 to 0.078125
Outputs:
- grad_q: bfloat16 [4096, 8192], P('ctx', 'ep')
- grad_k: bfloat16 [4096, 8192], P('ctx', 'ep')
- grad_v: bfloat16 [4096, 8192], P('ctx', 'ep')
- grad_moe_input: bfloat16 [4096, 3072], P('ctx', 'ep')
The draws below stay inside these ranges and needn't reach their ends.
Inputs may be any that keep to these rules, and one draw needn't show every extreme that they name: `doc_ids`: document numbers never fall along the sequence; a document holds 1 to 2048 tokens, one exactly that many. `expert_ids`: A token names two different experts. In the rows of one device no expert is named more than 40 times, a bound that some block reaches.
All inputs are finite; a program needn't handle non-finite values.
Results may differ from the reference program's by a relative error of at most 0.0057.
Values may be sent and summed in bfloat16 or wider, within the bound.
No kernel may reach another device: no remote copies, remote signals or barrier semaphores. Data moves between devices by JAX's collectives and lax.ppermute only.
A program may use at most 128 MiB of HBM per device.

```python
import math
import jax
import jax.numpy as jnp
import numpy as np
from jax import lax

HEAD_COUNT = 64
HEAD_DIM = 128
WIDTH = 3072
EXP_HIDDEN = 5120
TOK_DEV = 256
TOKEN_COUNT = 4096
EXPERTS = 16
CAPACITY = 40
N_CTX = 16


def draw_log_decay(key, part):
    key = jax.random.fold_in(key, 7)
    key_sequence = jax.random.split(key, 7)
    fast_share = 0.5
    fast_heads = jax.random.uniform(key_sequence[0], (HEAD_COUNT, 1)) < fast_share
    fast_rate = jnp.exp(jax.random.uniform(key_sequence[1], (HEAD_COUNT, 1), minval=math.log(1.0 / 50.0), maxval=math.log(1.0 / 30.0)))
    slow_rate = jax.random.uniform(key_sequence[2], (HEAD_COUNT, 1), minval=0.2, maxval=0.6) / TOKEN_COUNT
    baseline_rate = jnp.where(fast_heads, fast_rate, slow_rate)
    block_count = TOKEN_COUNT // TOK_DEV
    block_multiplier = jnp.exp(jax.random.uniform(key_sequence[3], (HEAD_COUNT, block_count, 1), minval=-0.7, maxval=0.7))
    block_multiplier = jnp.broadcast_to(block_multiplier, (HEAD_COUNT, block_count, TOK_DEV)).reshape(HEAD_COUNT, TOKEN_COUNT)
    token_multiplier = jnp.exp(jax.random.uniform(key_sequence[4], (HEAD_COUNT, TOKEN_COUNT), minval=-0.35, maxval=0.35))
    surge_locations = jax.random.randint(key_sequence[5], (HEAD_COUNT, 2, 1), 0, TOKEN_COUNT)
    surge_match = jnp.any(surge_locations == jnp.arange(TOKEN_COUNT)[None, None, :], axis=1)
    surge_extent = jax.random.uniform(key_sequence[6], (HEAD_COUNT, TOKEN_COUNT), minval=0.22, maxval=0.69)
    return -(baseline_rate * block_multiplier * token_multiplier) - jnp.where(surge_match, surge_extent, 0.0)


def block_scale(key, dims, cuts, low, largest):
    def one(axis_at, shards_of):
        heights = jax.random.uniform(jax.random.fold_in(jax.random.fold_in(key, 6), axis_at), (shards_of,), jnp.float32, low / len(cuts), largest / len(cuts))
        return jnp.repeat(jnp.exp(heights), dims[axis_at] // shards_of).reshape((-1,) + (1,) * (len(dims) - axis_at - 1))

    factor_of = one(*cuts[0])
    for cut in cuts[1:]:
        factor_of = factor_of * one(*cut)
    return factor_of


def length_profile(count, total, bound, lean):
    weights = [(1 << 20) // math.isqrt(standing ** lean) + 1 for standing in range(2, count + 1)]
    surplus, counts = total - bound - (count - 1), [1] * (count - 1)
    while surplus > 0:
        movable = [i for i in range(count - 1) if counts[i] < bound]
        pool, remaining = sum([weights[i] for i in movable]), surplus
        for i in movable:
            extra = min(bound - counts[i], max(1, remaining * weights[i] // pool), surplus)
            counts[i] = counts[i] + extra
            surplus = surplus - extra
    return np.array([bound] + counts)


def ragged(own_key, count, total, reach, slope):
    if count == 2:
        one = jax.random.randint(own_key, (), max(1, total - reach), min(reach, total - 1) + 1)
        return jnp.stack([one, total - one])
    tallies = jnp.asarray(length_profile(count, total, reach, slope), jnp.int32)
    pairs = (count - 1) // 2
    source_of, sink = tallies[1:1 + 2 * pairs:2], tallies[2:2 + 2 * pairs:2]
    room = jnp.minimum(source_of - 1, reach - sink)
    passed = jax.random.randint(jax.random.fold_in(own_key, 1), (pairs,), 0, 1 << 20) % (room + 1)
    tallies = tallies.at[1:1 + 2 * pairs:2].set(source_of - passed).at[2:2 + 2 * pairs:2].set(sink + passed)
    return tallies[jax.random.permutation(jax.random.fold_in(own_key, 2), count)]


def shared_out(stream_key, own, number, rows, number_of, top, most, skew):
    sequence = jax.random.permutation(stream_key, number_of)
    crowded, usual = shares(number_of, rows * top, most, skew, True), shares(number_of, rows * top, most, skew, False)
    places = jnp.arange(number_of)

    def named(lengths, rotation):
        used = int((lengths > 0).sum())
        fixed = max(1, used // 4)
        shifted = fixed + (places - fixed + rotation * (used - fixed)) % max(1, number_of - fixed)
        return jnp.zeros((number_of,), jnp.int32).at[sequence[jnp.where(places < fixed, places, shifted)]].set(jnp.asarray(lengths, jnp.int32))

    lengths = jnp.where(number % 4 == 0, named(crowded, number // 4), named(usual, number - number // 4 - 1))
    mixed = jax.random.permutation(jax.random.fold_in(own, 3), number_of)
    giver, receiver = mixed[0:number_of // 2 * 2:2], mixed[1:number_of // 2 * 2:2]
    margin = jnp.minimum(lengths[giver] - 1, most - lengths[receiver]) // 2
    margin = jnp.where((giver == sequence[0]) | (receiver == sequence[0]) | (lengths[receiver] == 0), 0, jnp.maximum(margin, 0))
    shifted = jax.random.randint(jax.random.fold_in(own, 4), (number_of // 2,), 0, 1 << 20) % (margin + 1)
    lengths = lengths.at[giver].add(-shifted).at[receiver].add(shifted)
    labels = jnp.searchsorted(jnp.cumsum(lengths), jnp.arange(rows * top), side="right").astype(jnp.int32)
    table = labels.reshape(top, rows).T
    table = table[jax.random.permutation(jax.random.fold_in(own, 1), rows)]
    rotation = jax.random.randint(jax.random.fold_in(own, 2), (rows, 1), 0, top)
    return jnp.take_along_axis(table, (jnp.arange(top)[None, :] + rotation) % top, axis=1)


def shares(amount, total, reach, skew, full):
    loads = [(1 << 20) // math.isqrt(grade ** skew) + 1 for grade in range(1, amount + 1)]
    largest = reach if full else min(reach, max(-(-total // amount), total * loads[0] // sum(loads)))
    least = 1 if total - largest >= amount - 1 else 0
    counts, surplus = [largest] + [least] * (amount - 1), total - largest - least * (amount - 1)
    while surplus > 0:
        candidates = [i for i in range(1, amount) if counts[i] < largest] or [i for i in range(1, amount) if counts[i] < reach]
        pool, left = sum([loads[i] for i in candidates]), surplus
        for i in candidates:
            more = min(reach - counts[i], max(1, left * loads[i] // pool), surplus)
            counts[i] = counts[i] + more
            surplus = surplus - more
    return np.array(counts)


def gaussian(stream_key, shape, scale, most, cuts=(), kind=jnp.bfloat16):
    drawn = jax.random.normal(stream_key, shape, jnp.float32) * scale
    if len(cuts) > 0:
        drawn = block_scale(stream_key, shape, cuts, -0.22, 0.18) * drawn
    return jnp.clip(drawn, min=-most, max=most).astype(kind)


def setup_inputs(seed: int = 0) -> dict:
    splits = jax.random.split(jax.random.key(seed), 14)
    queries = gaussian(splits[0], (TOKEN_COUNT, HEAD_COUNT * HEAD_DIM), 0.1, 0.625, ((0, 16), (1, 8)))
    keys = gaussian(splits[1], (TOKEN_COUNT, HEAD_COUNT * HEAD_DIM), 0.1, 0.625, ((0, 16), (1, 8)))
    values = gaussian(splits[2], (TOKEN_COUNT, HEAD_COUNT * HEAD_DIM), 0.1, 0.625, ((0, 16), (1, 8)))
    out_grad = gaussian(splits[3], (TOKEN_COUNT, HEAD_COUNT * HEAD_DIM), 0.1, 0.625, ((0, 16), (1, 8)))
    log_decay = draw_log_decay(jax.random.fold_in(splits[13], 71), 0)
    doc_ids = jnp.searchsorted(jnp.cumsum(ragged(splits[5], 3, TOKEN_COUNT, TOKEN_COUNT // 2, 2)), jnp.arange(TOKEN_COUNT), side="right").astype(jnp.int32)
    moe_input = gaussian(splits[6], (TOKEN_COUNT, WIDTH), 1.0, 6.0, ((0, 16), (1, 8)))
    moe_cotangent = gaussian(splits[7], (TOKEN_COUNT, WIDTH), 1.0, 6.0, ((0, 16), (1, 8)))
    router_weights = jnp.clip(0.1 + 0.79999997 * jax.random.uniform(splits[8], (TOKEN_COUNT, 2), jnp.float32) ** block_scale(splits[8], (TOKEN_COUNT, 2), ((0, 16),), -0.2, 0.2), 0.1, 0.9)
    expert_ids_keys = jax.random.split(jax.random.fold_in(splits[9], 1), TOKEN_COUNT // TOK_DEV)
    expert_ids_turns = jax.random.permutation(jax.random.fold_in(splits[9], 3), TOKEN_COUNT // TOK_DEV)
    expert_ids = jax.vmap(lambda own, number: shared_out(jax.random.fold_in(splits[9], 2), own, number, TOK_DEV, EXPERTS, 2, CAPACITY, 2))(expert_ids_keys, expert_ids_turns).reshape((TOKEN_COUNT, 2))
    w_gate = gaussian(splits[10], (EXPERTS, WIDTH, EXP_HIDDEN), WIDTH ** -0.5, 0.109375, ((0, 16), (2, 8)))
    w_up = gaussian(splits[11], (EXPERTS, WIDTH, EXP_HIDDEN), WIDTH ** -0.5, 0.109375, ((0, 16), (2, 8)))
    w_down = gaussian(splits[12], (EXPERTS, EXP_HIDDEN, WIDTH), EXP_HIDDEN ** -0.5, 0.078125, ((0, 16), (1, 8)))
    return {"queries": queries, "keys": keys, "values": values, "out_grad": out_grad, "log_decay": log_decay, "doc_ids": doc_ids, "moe_input": moe_input, "moe_cotangent": moe_cotangent, "router_weights": router_weights, "expert_ids": expert_ids, "w_gate": w_gate, "w_up": w_up, "w_down": w_down}


def rounded(values):
    return lax.optimization_barrier(values.astype(jnp.bfloat16)).astype(jnp.float32)


def reference(queries, keys, values, out_grad, log_decay, doc_ids, moe_input, moe_cotangent, router_weights, expert_ids, w_gate, w_up, w_down):
    highest = lax.Precision.HIGHEST
    block_count = TOKEN_COUNT // TOK_DEV

    def split_blocks(source):
        return source.reshape(block_count, TOK_DEV, HEAD_COUNT, HEAD_DIM).astype(jnp.float32)

    query_b = split_blocks(queries)
    key_b = split_blocks(keys)
    value_b = split_blocks(values)
    grad_b = split_blocks(out_grad)
    cum_decay = jnp.cumsum(log_decay.reshape(HEAD_COUNT, block_count, TOK_DEV).transpose(1, 0, 2), axis=2)
    doc_blocks = doc_ids.reshape(block_count, TOK_DEV)
    last_doc = doc_blocks[:, -1]
    prev_doc = jnp.concatenate([jnp.full((1,), -1, jnp.int32), last_doc[:-1]])
    log_total = cum_decay[:, :, -1]
    start_weight = jnp.where(doc_blocks[:, None, :] == prev_doc[:, None, None], jnp.exp(cum_decay), 0.0)
    end_weight = jnp.where(doc_blocks[:, None, :] == last_doc[:, None, None], jnp.exp(log_total[:, :, None] - cum_decay), 0.0)
    carry_rate = jnp.where((prev_doc == last_doc)[:, None], jnp.exp(log_total), 0.0)
    keys_end = rounded(jnp.transpose(end_weight, (0, 2, 1))[..., None] * key_b)
    queries_start = rounded(jnp.transpose(start_weight, (0, 2, 1))[..., None] * query_b)
    block_state = jnp.einsum('bthd,bthe->bhde', keys_end, value_b, precision=highest)
    block_adjoint = jnp.einsum('bthd,bthe->bhde', queries_start, grad_b, precision=highest)

    def advance(state_sum, carried):
        factor, summand = carried
        return factor[:, None, None] * state_sum + summand, state_sum

    zero_state = jnp.zeros((HEAD_COUNT, HEAD_DIM, HEAD_DIM), jnp.float32)
    _, incoming = lax.scan(advance, zero_state, (carry_rate, block_state))
    _, adjoint = lax.scan(advance, zero_state, (carry_rate, block_adjoint), reverse=True)
    positions = jnp.arange(TOK_DEV)
    causal = positions[:, None] >= positions[None, :]

    def block_out(carried):
        query_f, key_f, value_f, grad_f, cum_f, start_f, end_f, doc_f, incoming_f, adjoint_f = carried
        same_doc = causal & (doc_f[:, None] == doc_f[None, :])
        spread = jnp.where(causal[None], cum_f[:, :, None] - cum_f[:, None, :], 0.0)
        decay_mask = jnp.where(same_doc[None], jnp.exp(spread), 0.0)
        score_do = jnp.einsum('ihd,jhd->hij', grad_f, value_f, precision=highest)
        score_qk = jnp.einsum('ihd,jhd->hij', query_f, key_f, precision=highest)
        weighted_do = rounded(decay_mask * score_do)
        weighted_qk = rounded(decay_mask * score_qk)
        incoming_low = rounded(incoming_f)
        adjoint_low = rounded(adjoint_f)
        grad_query = jnp.einsum('hij,jhd->ihd', weighted_do, key_f, precision=highest) + start_f.T[:, :, None] * jnp.einsum('ihe,hde->ihd', grad_f, incoming_low, precision=highest)
        grad_key = jnp.einsum('hij,ihd->jhd', weighted_do, query_f, precision=highest) + end_f.T[:, :, None] * jnp.einsum('jhe,hde->jhd', value_f, adjoint_low, precision=highest)
        grad_value = jnp.einsum('hij,ihe->jhe', weighted_qk, grad_f, precision=highest) + end_f.T[:, :, None] * jnp.einsum('jhd,hde->jhe', key_f, adjoint_low, precision=highest)
        return (grad_query.astype(jnp.bfloat16), grad_key.astype(jnp.bfloat16), grad_value.astype(jnp.bfloat16))

    grad_query, grad_key, grad_value = lax.map(block_out, (query_b, key_b, value_b, grad_b, cum_decay, start_weight, end_weight, doc_blocks, incoming, adjoint))
    grad_q = grad_query.reshape(TOKEN_COUNT, HEAD_COUNT * HEAD_DIM)
    grad_k = grad_key.reshape(TOKEN_COUNT, HEAD_COUNT * HEAD_DIM)
    grad_v = grad_value.reshape(TOKEN_COUNT, HEAD_COUNT * HEAD_DIM)

    flat_expert = expert_ids.reshape(-1)
    flat_token = jnp.arange(2 * TOKEN_COUNT, dtype=jnp.int32) // 2
    flat_weight = router_weights.reshape(-1)
    limit = N_CTX * CAPACITY

    def expert_step(grad_sum, carried):
        number, gate_mat, up_mat, down_mat = carried
        chosen = flat_expert == number
        row_ids = jnp.nonzero(chosen, size=limit, fill_value=0)[0].astype(jnp.int32)
        live_row = jnp.arange(limit, dtype=jnp.int32) < jnp.sum(chosen.astype(jnp.int32))
        token_ids = flat_token[row_ids]
        x_rows = moe_input[token_ids].astype(jnp.float32)
        d_rows = moe_cotangent[token_ids].astype(jnp.float32)
        gate_f = gate_mat.astype(jnp.float32)
        up_f = up_mat.astype(jnp.float32)
        down_f = down_mat.astype(jnp.float32)
        gate_pre = jnp.dot(x_rows, gate_f, precision=highest)
        up_pre = jnp.dot(x_rows, up_f, precision=highest)
        hidden_grad = jnp.dot(d_rows, down_f.T, precision=highest)
        sigmoid_gate = jax.nn.sigmoid(gate_pre)
        gate_grad = rounded(hidden_grad * up_pre * sigmoid_gate * (1.0 + gate_pre * (1.0 - sigmoid_gate)))
        up_grad = rounded(hidden_grad * gate_pre * sigmoid_gate)
        expert_grad = jnp.dot(gate_grad, gate_f.T, precision=highest) + jnp.dot(up_grad, up_f.T, precision=highest)
        weight_rows = jnp.where(live_row, flat_weight[row_ids], 0.0)
        return grad_sum.at[token_ids].add(weight_rows[:, None] * expert_grad), None

    grad_sum, _ = lax.scan(expert_step, jnp.zeros((TOKEN_COUNT, WIDTH), jnp.float32), (jnp.arange(EXPERTS, dtype=jnp.int32), w_gate, w_up, w_down))
    return (grad_q, grad_k, grad_v, grad_sum.astype(jnp.bfloat16))
```

```python
import jax
import jax.numpy as jnp
from jax import lax
from jax.experimental import pallas as pl
from jax.experimental.pallas import tpu as pltpu
from jax.sharding import Mesh, PartitionSpec as P

BF = jnp.bfloat16
F32 = jnp.float32
I32 = jnp.int32
TOK = 256
HEADS = 8
HD = 128
HALF = HD // 2
CTX = 16
CAP = 40
ROWS = CTX * CAP
FEAT = 384
HID = 640
MARKS = 16
RINGX = 4
RIGHT = [(i, (i + 1) % RINGX) for i in range(RINGX)]
LEFT = [(i, (i - 1) % RINGX) for i in range(RINGX)]
SWAP = [(0, 1), (1, 0)]
MIB = 1 << 20

NT = (((1,), (1,)), ((), ()))
TN = (((0,), (0,)), ((), ()))


def vmem():
    return pl.BlockSpec(memory_space=pltpu.VMEM)


def anywhere():
    return pl.BlockSpec(memory_space=pl.ANY)


def call(kernel, outs, ins, scratch=(), flops=0, size=0, limit=32):
    return pl.pallas_call(
        kernel,
        out_shape=outs,
        in_specs=ins,
        out_specs=jax.tree.map(lambda _: vmem(), outs),
        scratch_shapes=scratch,
        compiler_params=pltpu.CompilerParams(vmem_limit_bytes=limit * MIB),
        cost_estimate=pl.CostEstimate(flops=flops, bytes_accessed=size, transcendentals=0),
    )


def mm(a, b, dims=(((1,), (0,)), ((), ()))):
    return lax.dot_general(a, b, dims, preferred_element_type=F32)


def onehot(slot):
    row = lax.broadcasted_iota(I32, (ROWS, TOK), 0)
    return row == slot


def pack_kernel(ids_ref, x_ref, d_ref, rows_ref, slots_ref):
    ids = ids_ref[...]
    expert = lax.broadcasted_iota(I32, (CTX, TOK), 0)
    first, second = ids[0:1] == expert, ids[1:2] == expert
    hits = jnp.where(first | second, 1.0, 0.0).astype(BF)
    before = lax.broadcasted_iota(I32, (TOK, TOK), 0) < lax.broadcasted_iota(I32, (TOK, TOK), 1)
    rank = mm(hits, jnp.where(before, 1.0, 0.0).astype(BF))
    slot0 = ids[0:1] * CAP + jnp.sum(jnp.where(first, rank, 0.0), axis=0, keepdims=True).astype(I32)
    slot1 = ids[1:2] * CAP + jnp.sum(jnp.where(second, rank, 0.0), axis=0, keepdims=True).astype(I32)
    slots_ref[0:1, :] = slot0
    slots_ref[1:2, :] = slot1
    pick = jnp.where(onehot(slot0) | onehot(slot1), 1.0, 0.0).astype(BF)
    rows_ref[:, :FEAT] = mm(pick, x_ref[...]).astype(BF)
    rows_ref[:, FEAT:] = mm(pick, d_ref[...]).astype(BF)


def combine_kernel(rows_ref, slots_ref, weights_ref, out_ref):
    rows = rows_ref[...]
    columns = jnp.concatenate([weights_ref[...], jnp.zeros((6, TOK), F32)], axis=0).T
    total = jnp.zeros((TOK, FEAT), F32)
    for k in range(2):
        pick = jnp.where(onehot(slots_ref[k : k + 1, :]), 1.0, 0.0).astype(BF)
        total += columns[:, k : k + 1] * mm(pick, rows, TN)
    out_ref[...] = total.astype(BF)


def state_kernel(q_ref, k_ref, v_ref, g_ref, decay_ref, doc_ref, out_ref, row_ref, col_ref):
    upto = lax.broadcasted_iota(I32, (TOK, TOK), 0) <= lax.broadcasted_iota(I32, (TOK, TOK), 1)
    cum = lax.dot_general(
        decay_ref[...],
        jnp.where(upto, 1.0, 0.0),
        (((1,), (0,)), ((), ())),
        precision=lax.Precision.HIGHEST,
        preferred_element_type=F32,
    )
    doc = jnp.broadcast_to(doc_ref[...].astype(F32), (HEADS, TOK))
    both = jnp.concatenate([cum, doc], axis=0)
    row_ref[...] = both
    turned = both.T
    cum_c, doc_c = turned[:, :HEADS], turned[:, HEADS:]
    total, first, last = cum_c[TOK - 1 :], doc_c[0:1], doc_c[TOK - 1 :]
    end_w = jnp.where(doc_c == last, jnp.exp(total - cum_c), 0.0)
    first_w = jnp.where(doc_c == first, jnp.exp(cum_c), 0.0)
    col_ref[:, 0:8] = cum_c
    col_ref[:, 8:16] = doc_c
    col_ref[:, 16:24] = first_w
    col_ref[:, 24:32] = end_w
    line = lax.broadcasted_iota(I32, (MARKS, HD), 0)
    for h in range(HEADS):
        cols = slice(h * HD, (h + 1) * HD)
        keys_end = (end_w[:, h : h + 1] * k_ref[:, cols].astype(F32)).astype(BF)
        queries_first = (first_w[:, h : h + 1] * q_ref[:, cols].astype(F32)).astype(BF)
        state = mm(keys_end, v_ref[:, cols], TN).astype(BF)
        adjoint = mm(queries_first, g_ref[:, cols], TN).astype(BF)
        sum_h = jnp.broadcast_to(total[:, h : h + 1], (MARKS, HD))
        high = sum_h.astype(BF).astype(F32)
        mid = (sum_h - high).astype(BF).astype(F32)
        low = sum_h - high - mid
        marks = jnp.where(line == 0, high, jnp.where(line == 1, mid, jnp.where(line == 2, low, 0.0)))
        marks = jnp.where(line == 3, first[:, h : h + 1], jnp.where(line == 4, last[:, h : h + 1], marks))
        for part in range(2):
            lines = slice(part * HALF, (part + 1) * HALF)
            out_ref[2 * h + part, 0:HALF, :] = state[lines]
            out_ref[2 * h + part, HALF:HD, :] = adjoint[lines]
            out_ref[2 * h + part, HD:, :] = marks.astype(BF)


def scan_kernel(in_ref, out_ref):
    rates, live = [], []
    prev = jnp.full((1, HD), -1.0, F32)
    for b in range(CTX):
        marks = in_ref[b, HD:, :].astype(F32)
        first, last = marks[3:4], marks[4:5]
        rates.append(jnp.where(prev == last, jnp.exp(marks[0:1] + marks[1:2] + marks[2:3]), 0.0))
        live.append(prev == first)
        prev = last
    total = jnp.zeros((HALF, HD), F32)
    for b in range(CTX):
        out_ref[b, 0:HALF, :] = jnp.where(live[b], total, 0.0).astype(BF)
        total = rates[b] * total + in_ref[b, 0:HALF, :].astype(F32)
    total = jnp.zeros((HALF, HD), F32)
    for b in reversed(range(CTX)):
        out_ref[b, HALF:, :] = total.astype(BF)
        total = rates[b] * total + jnp.where(live[b], in_ref[b, HALF:HD, :].astype(F32), 0.0)


def attention_kernel(q_ref, k_ref, v_ref, g_ref, row_ref, col_ref, carried_ref, gq_ref, gk_ref, gv_ref):
    seen = lax.broadcasted_iota(I32, (TOK, TOK), 0) >= lax.broadcasted_iota(I32, (TOK, TOK), 1)
    same = seen & (col_ref[:, 8:9] == row_ref[8:9, :])
    for h in range(HEADS):
        cols = slice(h * HD, (h + 1) * HD)
        q, k, v, g = q_ref[:, cols], k_ref[:, cols], v_ref[:, cols], g_ref[:, cols]
        spread = jnp.where(same, col_ref[:, h : h + 1] - row_ref[h : h + 1, :], -1e30)
        decay = jnp.exp(spread)
        weighted_do = (decay * mm(g, v, NT)).astype(BF)
        weighted_qk = (decay * mm(q, k, NT)).astype(BF)
        incoming = jnp.concatenate([carried_ref[2 * h, 0:HALF, :], carried_ref[2 * h + 1, 0:HALF, :]], axis=0)
        adjoint = jnp.concatenate([carried_ref[2 * h, HALF:, :], carried_ref[2 * h + 1, HALF:, :]], axis=0)
        start = col_ref[:, 16 + h : 17 + h]
        end = col_ref[:, 24 + h : 25 + h]
        gq_ref[:, cols] = (mm(weighted_do, k) + start * mm(g, incoming, NT)).astype(BF)
        gk_ref[:, cols] = (mm(weighted_do, q, TN) + end * mm(v, adjoint, NT)).astype(BF)
        gv_ref[:, cols] = (mm(weighted_qk, g, TN) + end * mm(k, adjoint)).astype(BF)


def feature_block(place, offset, sibling):
    core = place[1]
    core = 1 - core if sibling else core
    return pl.multiple_of((((place[0] + offset) % RINGX) * 2 + core) * FEAT, FEAT)


def first_layer(place, offsets, chunks, weights, xs, ds, gate_w, up_w, down_w, sems):
    groups = ([], [], [])
    n = 0
    for i, (offset, sibling) in enumerate(offsets):
        block = feature_block(place, offset, sibling)
        side = pl.ds(i * FEAT, FEAT)
        x_src, d_src = chunks[i]
        moves = (
            (0, x_src, xs.at[:, side]),
            (0, weights[0].at[0, pl.ds(block, FEAT), :], gate_w.at[side, :]),
            (1, weights[1].at[0, pl.ds(block, FEAT), :], up_w.at[side, :]),
            (2, d_src, ds.at[:, side]),
            (2, weights[2].at[0, :, pl.ds(block, FEAT)], down_w.at[:, side]),
        )
        for group, src, dst in moves:
            groups[group].append(pltpu.make_async_copy(src, dst, sems.at[n]))
            n += 1
    for group in groups:
        for copy in group:
            copy.start()
    return groups


A_OFFSETS = ((0, False), (0, True), (-1, False), (1, False), (-1, True), (1, True))


def expert_a_kernel(place, a0, a1, a2, a3, a4, a5, wg, wu, wd, gate_ref, up_ref, hid_ref, xs, ds, gate_w, up_w, down_w, sems):
    chunks = [(a.at[:, pl.ds(0, FEAT)], a.at[:, pl.ds(FEAT, FEAT)]) for a in (a0, a1, a2, a3, a4, a5)]
    groups = first_layer(place, A_OFFSETS, chunks, (wg, wu, wd), xs, ds, gate_w, up_w, down_w, sems)
    for copy in groups[0]:
        copy.wait()
    gate_ref[...] = mm(xs[...], gate_w[...])
    for copy in groups[1]:
        copy.wait()
    up_ref[...] = mm(xs[...], up_w[...])
    for copy in groups[2]:
        copy.wait()
    hid_ref[...] = mm(ds[...], down_w[...], NT)


def out_weights(place, sibling, wg, wu, cat, sems, at):
    copies = []
    for i, offset in enumerate(OUT_OFFSETS):
        block = feature_block(place, offset, sibling)
        side = pl.ds(i * FEAT, FEAT)
        copies.append(pltpu.make_async_copy(wg.at[0, pl.ds(block, FEAT), :], cat.at[side, pl.ds(0, HID)], sems.at[at + 2 * i]))
        copies.append(pltpu.make_async_copy(wu.at[0, pl.ds(block, FEAT), :], cat.at[side, pl.ds(HID, HID)], sems.at[at + 2 * i + 1]))
    for copy in copies:
        copy.start()
    return copies


B_OFFSETS = ((2, False), (2, True))
OUT_OFFSETS = (2, 1, -1, 0)


def expert_b_kernel(place, gate_ref, up_ref, hid_ref, x0, d0, x1, d1, wg, wu, wd, mid_ref, out_ref, xs, ds, gate_w, up_w, down_w, cat, sems):
    chunks = [(x0, d0), (x1, d1)]
    groups = first_layer(place, B_OFFSETS, chunks, (wg, wu, wd), xs, ds, gate_w, up_w, down_w, sems)
    late = out_weights(place, True, wg, wu, cat, sems, 10)
    for group in groups:
        for copy in group:
            copy.wait()
    gate = gate_ref[...] + mm(xs[...], gate_w[...])
    up = up_ref[...] + mm(xs[...], up_w[...])
    hid = hid_ref[...] + mm(ds[...], down_w[...], NT)
    s = 1.0 / (1.0 + jnp.exp(-gate))
    mid_ref[:, :HID] = (hid * up * s * (1.0 + gate * (1.0 - s))).astype(BF)
    mid_ref[:, HID:] = (hid * gate * s).astype(BF)
    for copy in late:
        copy.wait()
    for i in range(RINGX):
        out_ref[i] = mm(mid_ref[...], cat[i * FEAT : (i + 1) * FEAT, :], NT).astype(BF)


def expert_c_kernel(place, mid_ref, wg, wu, out_ref, cat, sems):
    for copy in out_weights(place, False, wg, wu, cat, sems, 0):
        copy.wait()
    for i in range(RINGX):
        out_ref[i] = mm(mid_ref[...], cat[i * FEAT : (i + 1) * FEAT, :], NT)


def local(
    queries, keys, values, out_grad, log_decay, doc_ids, moe_input, moe_cotangent, router_weights, expert_ids, w_gate, w_up, w_down
):
    S = jax.ShapeDtypeStruct
    place = jnp.stack([lax.axis_index("x"), lax.axis_index("core")]).astype(I32)
    smem = pl.BlockSpec(memory_space=pltpu.SMEM)

    def ring(value, way):
        return lax.ppermute(value, "x", way)

    def swap(value):
        return lax.ppermute(value, "core", SWAP)

    rows, slots = call(
        pack_kernel,
        (S((ROWS, 2 * FEAT), BF), S((2, TOK), I32)),
        [vmem()] * 3,
        flops=2 * ROWS * TOK * 2 * FEAT,
        size=2 * MIB,
    )(expert_ids.T, moe_input, moe_cotangent)
    own = lax.all_to_all(rows.reshape(CTX, CAP, 2 * FEAT), "ctx", 0, 0, tiled=True).reshape(ROWS, 2 * FEAT)
    from_left, from_right = ring(own, RIGHT), ring(own, LEFT)
    x_opp, d_opp = ring(from_left[:, :FEAT], RIGHT), ring(from_right[:, FEAT:], LEFT)
    own_s, left_s, right_s = swap(own), swap(from_left), swap(from_right)
    x_opp_s, d_opp_s = swap(x_opp), swap(d_opp)

    message, lines, columns = call(
        state_kernel,
        (S((CTX, HD + MARKS, HD), BF), S((2 * HEADS, TOK), F32), S((TOK, 4 * HEADS), F32)),
        [vmem()] * 6,
        flops=4 * HEADS * TOK * HD * HD,
        size=3 * MIB,
    )(queries, keys, values, out_grad, log_decay, doc_ids.reshape(1, TOK))
    message = lax.all_to_all(message, "ctx", 0, 0, tiled=True)
    carried = call(scan_kernel, S((CTX, HD, HD), BF), [vmem()], flops=MIB, size=MIB)(message)
    carried = lax.all_to_all(carried, "ctx", 0, 0, tiled=True)
    grads = call(
        attention_kernel,
        (S((TOK, HEADS * HD), BF),) * 3,
        [vmem()] * 7,
        flops=16 * HEADS * TOK * TOK * HD,
        size=4 * MIB,
    )(queries, keys, values, out_grad, lines, columns, carried)

    square = S((ROWS, HID), F32)
    n = len(A_OFFSETS)
    gate, up, hid = call(
        expert_a_kernel,
        (square,) * 3,
        [smem] + [anywhere()] * 9,
        [
            pltpu.VMEM((ROWS, n * FEAT), BF),
            pltpu.VMEM((ROWS, n * FEAT), BF),
            pltpu.VMEM((n * FEAT, HID), BF),
            pltpu.VMEM((n * FEAT, HID), BF),
            pltpu.VMEM((HID, n * FEAT), BF),
            pltpu.SemaphoreType.DMA((5 * n,)),
        ],
        flops=6 * ROWS * HID * n * FEAT,
        size=18 * MIB,
    )(place, own, own_s, from_left, from_right, left_s, right_s, w_gate, w_up, w_down)
    n = len(B_OFFSETS)
    mid, away = call(
        expert_b_kernel,
        (S((ROWS, 2 * HID), BF), S((RINGX, ROWS, FEAT), BF)),
        [smem] + [vmem()] * 3 + [anywhere()] * 7,
        [
            pltpu.VMEM((ROWS, n * FEAT), BF),
            pltpu.VMEM((ROWS, n * FEAT), BF),
            pltpu.VMEM((n * FEAT, HID), BF),
            pltpu.VMEM((n * FEAT, HID), BF),
            pltpu.VMEM((HID, n * FEAT), BF),
            pltpu.VMEM((RINGX * FEAT, 2 * HID), BF),
            pltpu.SemaphoreType.DMA((5 * n + 8,)),
        ],
        flops=10 * ROWS * HID * RINGX * FEAT,
        size=14 * MIB,
        limit=48,
    )(place, gate, up, hid, x_opp, d_opp, x_opp_s, d_opp_s, w_gate, w_up, w_down)
    away = swap(away)
    mine = call(
        expert_c_kernel,
        S((RINGX, ROWS, FEAT), F32),
        [smem, vmem()] + [anywhere()] * 2,
        [pltpu.VMEM((RINGX * FEAT, 2 * HID), BF), pltpu.SemaphoreType.DMA((8,))],
        flops=4 * ROWS * HID * RINGX * FEAT,
        size=8 * MIB,
    )(place, mid, w_gate, w_up)

    chip = mine + away.astype(F32)
    cut = ROWS // 2
    via_right = ring(chip[0, :cut].astype(BF), RIGHT).astype(F32)
    via_left = ring(chip[0, cut:].astype(BF), LEFT).astype(F32)
    to_right = jnp.concatenate([chip[1, :cut] + via_right, chip[1, cut:]], axis=0).astype(BF)
    to_left = jnp.concatenate([chip[2, :cut], chip[2, cut:] + via_left], axis=0).astype(BF)
    summed = chip[3] + ring(to_right, RIGHT).astype(F32) + ring(to_left, LEFT).astype(F32)
    back = lax.all_to_all(summed.astype(BF).reshape(CTX, CAP, FEAT), "ctx", 0, 0, tiled=True)
    grad_moe = call(
        combine_kernel,
        S((TOK, FEAT), BF),
        [vmem()] * 3,
        flops=4 * ROWS * TOK * FEAT,
        size=MIB,
    )(back.reshape(ROWS, FEAT), slots, router_weights.T)
    return (*grads, grad_moe)


def solution(mesh):
    fine = Mesh(mesh.devices.reshape(CTX, RINGX, 2), ("ctx", "x", "core"))
    ep = ("x", "core")
    row = P("ctx", ep)
    in_specs = (row, row, row, row, P(ep, "ctx"), P("ctx"), row, row, P("ctx", None), P("ctx", None))
    in_specs += (P("ctx", None, ep), P("ctx", None, ep), P("ctx", ep, None))
    return jax.shard_map(local, mesh=fine, in_specs=in_specs, out_specs=(row,) * 4, check_vma=False)
```

```python
import jax
import jax.numpy as jnp
from jax import lax
from jax.experimental import pallas as pl
from jax.experimental.pallas import tpu as pltpu
from jax.sharding import Mesh, PartitionSpec as P

BF = jnp.bfloat16
F32 = jnp.float32
I32 = jnp.int32
TOK = 256
HEADS = 8
HD = 128
HALF = HD // 2
CTX = 16
CAP = 40
ROWS = CTX * CAP
FEAT = 384
HID = 640
MARKS = 16
RINGX = 4
RIGHT = [(i, (i + 1) % RINGX) for i in range(RINGX)]
LEFT = [(i, (i - 1) % RINGX) for i in range(RINGX)]
SWAP = [(0, 1), (1, 0)]
MIB = 1 << 20

NT = (((1,), (1,)), ((), ()))
TN = (((0,), (0,)), ((), ()))


def vmem():
    return pl.BlockSpec(memory_space=pltpu.VMEM)


def anywhere():
    return pl.BlockSpec(memory_space=pl.ANY)


def hbm():
    return pl.BlockSpec(memory_space=pltpu.HBM)


def call(kernel, outs, ins, scratch=(), flops=0, size=0, limit=32):
    return pl.pallas_call(
        kernel,
        out_shape=outs,
        in_specs=ins,
        out_specs=jax.tree.map(lambda _: vmem(), outs),
        scratch_shapes=scratch,
        compiler_params=pltpu.CompilerParams(vmem_limit_bytes=limit * MIB),
        cost_estimate=pl.CostEstimate(flops=flops, bytes_accessed=size, transcendentals=0),
    )


def mm(a, b, dims=(((1,), (0,)), ((), ()))):
    return lax.dot_general(a, b, dims, preferred_element_type=F32)


def onehot(slot):
    row = lax.broadcasted_iota(I32, (ROWS, TOK), 0)
    return row == slot


def pack_kernel(ids_hbm, x_hbm, d_hbm, rows_ref, slots_ref, ids_ref, x_ref, d_ref, sems):
    copies = [
        pltpu.make_async_copy(src, dst, sems.at[i])
        for i, (src, dst) in enumerate(((ids_hbm, ids_ref), (x_hbm, x_ref), (d_hbm, d_ref)))
    ]
    for copy in copies:
        copy.start()
    copies[0].wait()
    ids = ids_ref[...]
    expert = lax.broadcasted_iota(I32, (CTX, TOK), 0)
    first, second = ids[0:1] == expert, ids[1:2] == expert
    hits = jnp.where(first | second, 1.0, 0.0).astype(BF)
    before = lax.broadcasted_iota(I32, (TOK, TOK), 0) < lax.broadcasted_iota(I32, (TOK, TOK), 1)
    rank = mm(hits, jnp.where(before, 1.0, 0.0).astype(BF))
    slot0 = ids[0:1] * CAP + jnp.sum(jnp.where(first, rank, 0.0), axis=0, keepdims=True).astype(I32)
    slot1 = ids[1:2] * CAP + jnp.sum(jnp.where(second, rank, 0.0), axis=0, keepdims=True).astype(I32)
    slots_ref[0:1, :] = slot0
    slots_ref[1:2, :] = slot1
    pick = jnp.where(onehot(slot0) | onehot(slot1), 1.0, 0.0).astype(BF)
    copies[1].wait()
    copies[2].wait()
    rows_ref[:, :FEAT] = mm(pick, x_ref[...]).astype(BF)
    rows_ref[:, FEAT:] = mm(pick, d_ref[...]).astype(BF)


def combine_kernel(rows_ref, slots_ref, weights_ref, out_ref):
    rows = rows_ref[...]
    columns = jnp.concatenate([weights_ref[...], jnp.zeros((6, TOK), F32)], axis=0).T
    total = jnp.zeros((TOK, FEAT), F32)
    for k in range(2):
        pick = jnp.where(onehot(slots_ref[k : k + 1, :]), 1.0, 0.0).astype(BF)
        total += columns[:, k : k + 1] * mm(pick, rows, TN)
    out_ref[...] = total.astype(BF)


def state_kernel(q_ref, k_ref, v_ref, g_ref, decay_ref, doc_ref, token, out_ref, row_ref, col_ref):
    upto = lax.broadcasted_iota(I32, (TOK, TOK), 0) <= lax.broadcasted_iota(I32, (TOK, TOK), 1)
    cum = lax.dot_general(
        decay_ref[...],
        jnp.where(upto, 1.0, 0.0),
        (((1,), (0,)), ((), ())),
        precision=lax.Precision.HIGHEST,
        preferred_element_type=F32,
    )
    doc = jnp.broadcast_to(doc_ref[...].astype(F32), (HEADS, TOK))
    both = jnp.concatenate([cum, doc], axis=0)
    row_ref[...] = both
    turned = both.T
    cum_c, doc_c = turned[:, :HEADS], turned[:, HEADS:]
    total, first, last = cum_c[TOK - 1 :], doc_c[0:1], doc_c[TOK - 1 :]
    end_w = jnp.where(doc_c == last, jnp.exp(total - cum_c), 0.0)
    first_w = jnp.where(doc_c == first, jnp.exp(cum_c), 0.0)
    col_ref[:, 0:8] = cum_c
    col_ref[:, 8:16] = doc_c
    col_ref[:, 16:24] = first_w
    col_ref[:, 24:32] = end_w
    line = lax.broadcasted_iota(I32, (MARKS, HD), 0)
    for h in range(HEADS):
        cols = slice(h * HD, (h + 1) * HD)
        keys_end = (end_w[:, h : h + 1] * k_ref[:, cols].astype(F32)).astype(BF)
        queries_first = (first_w[:, h : h + 1] * q_ref[:, cols].astype(F32)).astype(BF)
        state = mm(keys_end, v_ref[:, cols], TN).astype(BF)
        adjoint = mm(queries_first, g_ref[:, cols], TN).astype(BF)
        sum_h = jnp.broadcast_to(total[:, h : h + 1], (MARKS, HD))
        high = sum_h.astype(BF).astype(F32)
        mid = (sum_h - high).astype(BF).astype(F32)
        low = sum_h - high - mid
        marks = jnp.where(line == 0, high, jnp.where(line == 1, mid, jnp.where(line == 2, low, 0.0)))
        marks = jnp.where(line == 3, first[:, h : h + 1], jnp.where(line == 4, last[:, h : h + 1], marks))
        for part in range(2):
            lines = slice(part * HALF, (part + 1) * HALF)
            out_ref[2 * h + part, 0:HALF, :] = state[lines]
            out_ref[2 * h + part, HALF:HD, :] = adjoint[lines]
            out_ref[2 * h + part, HD:, :] = marks.astype(BF)


def scan_kernel(in_ref, out_ref):
    rates, live = [], []
    prev = jnp.full((1, HD), -1.0, F32)
    for b in range(CTX):
        marks = in_ref[b, HD:, :].astype(F32)
        first, last = marks[3:4], marks[4:5]
        rates.append(jnp.where(prev == last, jnp.exp(marks[0:1] + marks[1:2] + marks[2:3]), 0.0))
        live.append(prev == first)
        prev = last
    total = jnp.zeros((HALF, HD), F32)
    for b in range(CTX):
        out_ref[b, 0:HALF, :] = jnp.where(live[b], total, 0.0).astype(BF)
        total = rates[b] * total + in_ref[b, 0:HALF, :].astype(F32)
    total = jnp.zeros((HALF, HD), F32)
    for b in reversed(range(CTX)):
        out_ref[b, HALF:, :] = total.astype(BF)
        total = rates[b] * total + jnp.where(live[b], in_ref[b, HALF:HD, :].astype(F32), 0.0)


def attention_kernel(q_ref, k_ref, v_ref, g_ref, row_ref, col_ref, carried_ref, gq_ref, gk_ref, gv_ref):
    seen = lax.broadcasted_iota(I32, (TOK, TOK), 0) >= lax.broadcasted_iota(I32, (TOK, TOK), 1)
    same = seen & (col_ref[:, 8:9] == row_ref[8:9, :])
    for h in range(HEADS):
        cols = slice(h * HD, (h + 1) * HD)
        q, k, v, g = q_ref[:, cols], k_ref[:, cols], v_ref[:, cols], g_ref[:, cols]
        spread = jnp.where(same, col_ref[:, h : h + 1] - row_ref[h : h + 1, :], -1e30)
        decay = jnp.exp(spread)
        weighted_do = (decay * mm(g, v, NT)).astype(BF)
        weighted_qk = (decay * mm(q, k, NT)).astype(BF)
        incoming = jnp.concatenate([carried_ref[2 * h, 0:HALF, :], carried_ref[2 * h + 1, 0:HALF, :]], axis=0)
        adjoint = jnp.concatenate([carried_ref[2 * h, HALF:, :], carried_ref[2 * h + 1, HALF:, :]], axis=0)
        start = col_ref[:, 16 + h : 17 + h]
        end = col_ref[:, 24 + h : 25 + h]
        gq_ref[:, cols] = (mm(weighted_do, k) + start * mm(g, incoming, NT)).astype(BF)
        gk_ref[:, cols] = (mm(weighted_do, q, TN) + end * mm(v, adjoint, NT)).astype(BF)
        gv_ref[:, cols] = (mm(weighted_qk, g, TN) + end * mm(k, adjoint)).astype(BF)


def feature_block(place, offset, sibling):
    core = place[1]
    core = 1 - core if sibling else core
    return pl.multiple_of((((place[0] + offset) % RINGX) * 2 + core) * FEAT, FEAT)


ORDER = ((0, 0), (0, 1), (-1, 0), (1, 0), (-1, 1), (1, 1), (2, 0), (2, 1))
EARLY = 6
OUT_ORDER = (2, 1, -1, 0)


def weights_kernel(place, wg, wu, wd, token, cat, down, sems):
    copies = []
    for i, (offset, sibling) in enumerate(ORDER):
        block = feature_block(place, offset, sibling)
        side = pl.ds(i * FEAT, FEAT)
        for j, (src, dst) in enumerate(
            (
                (wg.at[0, pl.ds(block, FEAT), :], cat.at[side, pl.ds(0, HID)]),
                (wu.at[0, pl.ds(block, FEAT), :], cat.at[side, pl.ds(HID, HID)]),
                (wd.at[0, :, pl.ds(block, FEAT)], down.at[:, side]),
            )
        ):
            copies.append(pltpu.make_async_copy(src, dst, sems.at[3 * i + j]))
    for copy in copies:
        copy.start()
    for copy in copies:
        copy.wait()


def expert_x_kernel(a0, a1, a2, a3, a4, a5, cat, token, out_ref, xs):
    for i, a in enumerate((a0, a1, a2, a3, a4, a5)):
        xs[:, i * FEAT : (i + 1) * FEAT] = a[:, :FEAT]
    out_ref[...] = mm(xs[...], cat[: EARLY * FEAT, :])


def expert_d_kernel(a0, a1, a2, a3, a4, a5, down, out_ref, ds):
    for i, a in enumerate((a0, a1, a2, a3, a4, a5)):
        ds[:, i * FEAT : (i + 1) * FEAT] = a[:, FEAT:]
    out_ref[...] = mm(ds[...], down[:, : EARLY * FEAT], NT)


def expert_mid_kernel(gu_ref, hid_ref, x0, d0, x1, d1, cat, down, mid_ref, o0, o1, o2, o3):
    late = slice(EARLY * FEAT, None)
    xs = jnp.concatenate([x0[...], x1[...]], axis=1)
    ds = jnp.concatenate([d0[...], d1[...]], axis=1)
    pre = gu_ref[...] + mm(xs, cat[late, :])
    hid = hid_ref[...] + mm(ds, down[:, late], NT)
    gate, up = pre[:, :HID], pre[:, HID:]
    s = 1.0 / (1.0 + jnp.exp(-gate))
    mid_ref[:, :HID] = (hid * up * s * (1.0 + gate * (1.0 - s))).astype(BF)
    mid_ref[:, HID:] = (hid * gate * s).astype(BF)
    out_blocks(mid_ref, cat, 1, (o0, o1, o2, o3))


def out_blocks(mid_ref, cat, sibling, outs):
    for offset, out in zip(OUT_ORDER, outs):
        at = ORDER.index((offset, sibling)) * FEAT
        out[...] = mm(mid_ref[...], cat[at : at + FEAT, :], NT).astype(out.dtype)


def expert_out_kernel(mid_ref, cat, o0, o1, o2, o3):
    out_blocks(mid_ref, cat, 0, (o0, o1, o2, o3))


def local(
    queries, keys, values, out_grad, log_decay, doc_ids, moe_input, moe_cotangent, router_weights, expert_ids, w_gate, w_up, w_down
):
    S = jax.ShapeDtypeStruct
    place = jnp.stack([lax.axis_index("x"), lax.axis_index("core")]).astype(I32)
    smem = pl.BlockSpec(memory_space=pltpu.SMEM)

    def ring(value, way):
        return lax.ppermute(value, "x", way)

    def swap(value):
        return lax.ppermute(value, "core", SWAP)

    rows, slots = call(
        pack_kernel,
        (S((ROWS, 2 * FEAT), BF), S((2, TOK), I32)),
        [hbm()] * 3,
        [pltpu.VMEM((2, TOK), I32)] + [pltpu.VMEM((TOK, FEAT), BF)] * 2 + [pltpu.SemaphoreType.DMA((3,))],
        flops=2 * ROWS * TOK * 2 * FEAT,
        size=2 * MIB,
        limit=6,
    )(expert_ids.T, moe_input, moe_cotangent)
    own = lax.all_to_all(rows.reshape(CTX, CAP, 2 * FEAT), "ctx", 0, 0, tiled=True).reshape(ROWS, 2 * FEAT)
    from_left, from_right = ring(own, RIGHT), ring(own, LEFT)
    x_opp, d_opp = ring(from_left[:, :FEAT], RIGHT), ring(from_right[:, FEAT:], LEFT)
    own_s, left_s, right_s = swap(own), swap(from_left), swap(from_right)
    x_opp_s, d_opp_s = swap(x_opp), swap(d_opp)

    cat, down = call(
        weights_kernel,
        (S((RINGX * 2 * FEAT, 2 * HID), BF), S((HID, RINGX * 2 * FEAT), BF)),
        [smem] + [hbm()] * 3 + [anywhere()],
        [pltpu.SemaphoreType.DMA((3 * len(ORDER),))],
        size=24 * MIB,
        limit=14,
    )(place, w_gate, w_up, w_down, own)

    message, lines, columns = call(
        state_kernel,
        (S((CTX, HD + MARKS, HD), BF), S((2 * HEADS, TOK), F32), S((TOK, 4 * HEADS), F32)),
        [vmem()] * 6 + [anywhere()],
        flops=4 * HEADS * TOK * HD * HD,
        size=3 * MIB,
        limit=8,
    )(queries, keys, values, out_grad, log_decay, doc_ids.reshape(1, TOK), own)
    message = lax.all_to_all(message, "ctx", 0, 0, tiled=True)
    scanned = call(scan_kernel, S((CTX, HD, HD), BF), [vmem()], flops=MIB, size=MIB, limit=4)(message)
    carried = lax.all_to_all(scanned, "ctx", 0, 0, tiled=True)
    grads = call(
        attention_kernel,
        (S((TOK, HEADS * HD), BF),) * 3,
        [vmem()] * 7,
        flops=16 * HEADS * TOK * TOK * HD,
        size=4 * MIB,
        limit=12,
    )(queries, keys, values, out_grad, lines, columns, carried)

    n = EARLY * FEAT
    early = (own, own_s, from_left, from_right, left_s, right_s)
    pre = call(
        expert_x_kernel,
        S((ROWS, 2 * HID), F32),
        [vmem()] * 7 + [anywhere()],
        [pltpu.VMEM((ROWS, n), BF)],
        flops=4 * ROWS * HID * n,
        size=18 * MIB,
        limit=26,
    )(*early, cat, scanned)
    hid = call(
        expert_d_kernel,
        S((ROWS, HID), F32),
        [vmem()] * 7,
        [pltpu.VMEM((ROWS, n), BF)],
        flops=2 * ROWS * HID * n,
        size=14 * MIB,
        limit=20,
    )(*early, down)
    block = S((ROWS, FEAT), BF)
    mid, *away = call(
        expert_mid_kernel,
        (S((ROWS, 2 * HID), BF),) + (block,) * RINGX,
        [vmem()] * 8,
        flops=10 * ROWS * HID * RINGX * FEAT,
        size=14 * MIB,
        limit=32,
    )(pre, hid, x_opp, d_opp, x_opp_s, d_opp_s, cat, down)
    away = [swap(a) for a in away]
    mine = call(
        expert_out_kernel,
        (S((ROWS, FEAT), F32),) * RINGX,
        [vmem()] * 2,
        flops=4 * ROWS * HID * RINGX * FEAT,
        size=8 * MIB,
        limit=18,
    )(mid, cat)

    cut = ROWS // 2
    opp, right, left, here = [(m, a.astype(F32)) for m, a in zip(mine, away)]
    via_right = ring((opp[0][:cut] + opp[1][:cut]).astype(BF), RIGHT).astype(F32)
    via_left = ring((opp[0][cut:] + opp[1][cut:]).astype(BF), LEFT).astype(F32)
    none = jnp.zeros((cut, FEAT), F32)
    to_right = (right[0] + right[1] + jnp.concatenate([via_right, none], axis=0)).astype(BF)
    to_left = (left[0] + left[1] + jnp.concatenate([none, via_left], axis=0)).astype(BF)
    summed = here[0] + here[1] + ring(to_right, RIGHT).astype(F32) + ring(to_left, LEFT).astype(F32)
    back = lax.all_to_all(summed.astype(BF).reshape(CTX, CAP, FEAT), "ctx", 0, 0, tiled=True)
    grad_moe = call(
        combine_kernel,
        S((TOK, FEAT), BF),
        [vmem()] * 3,
        flops=4 * ROWS * TOK * FEAT,
        size=MIB,
        limit=8,
    )(back.reshape(ROWS, FEAT), slots, router_weights.T)
    return (*grads, grad_moe)


def solution(mesh):
    fine = Mesh(mesh.devices.reshape(CTX, RINGX, 2), ("ctx", "x", "core"))
    ep = ("x", "core")
    row = P("ctx", ep)
    in_specs = (row, row, row, row, P(ep, "ctx"), P("ctx"), row, row, P("ctx", None), P("ctx", None))
    in_specs += (P("ctx", None, ep), P("ctx", None, ep), P("ctx", ep, None))
    return jax.shard_map(local, mesh=fine, in_specs=in_specs, out_specs=(row,) * 4, check_vma=False)
```

```python
import jax
import jax.numpy as jnp
from jax import lax
from jax.experimental import pallas as pl
from jax.experimental.pallas import tpu as pltpu
from jax.sharding import Mesh, PartitionSpec as P

BF = jnp.bfloat16
F32 = jnp.float32
I32 = jnp.int32
TOK = 256
HEADS = 8
HD = 128
HALF = HD // 2
CTX = 16
CAP = 40
PARTS = (24, 16)
BASES = (0, 24)
FEAT = 384
HID = 640
MARKS = 16
RINGX = 4
RIGHT = [(i, (i + 1) % RINGX) for i in range(RINGX)]
LEFT = [(i, (i - 1) % RINGX) for i in range(RINGX)]
SWAP = [(0, 1), (1, 0)]
MIB = 1 << 20

NT = (((1,), (1,)), ((), ()))
TN = (((0,), (0,)), ((), ()))


def vmem():
    return pl.BlockSpec(memory_space=pltpu.VMEM)


def anywhere():
    return pl.BlockSpec(memory_space=pl.ANY)


def in_hbm(value):
    return pltpu.with_memory_space_constraint(value, pltpu.HBM)


def call(kernel, outs, ins, scratch=(), flops=0, size=0, limit=32):
    return pl.pallas_call(
        kernel,
        out_shape=outs,
        in_specs=ins,
        out_specs=jax.tree.map(lambda o: vmem() if isinstance(o, jax.ShapeDtypeStruct) else anywhere(), outs),
        scratch_shapes=scratch,
        compiler_params=pltpu.CompilerParams(vmem_limit_bytes=limit * MIB),
        cost_estimate=pl.CostEstimate(flops=flops, bytes_accessed=size, transcendentals=0),
    )


def fetch(pairs, sems):
    copies = [pltpu.make_async_copy(src, dst, sems.at[i]) for i, (src, dst) in enumerate(pairs)]
    for copy in copies:
        copy.start()
    return copies


def mm(a, b, dims=(((1,), (0,)), ((), ()))):
    return lax.dot_general(a, b, dims, preferred_element_type=F32)


def onehot(slot, rows):
    return lax.broadcasted_iota(I32, (rows, TOK), 0) == slot


def part_slots(ids):
    expert = lax.broadcasted_iota(I32, (CTX, TOK), 0)
    named = [ids[k : k + 1] == expert for k in range(2)]
    hits = jnp.where(named[0] | named[1], 1.0, 0.0).astype(BF)
    before = lax.broadcasted_iota(I32, (TOK, TOK), 0) < lax.broadcasted_iota(I32, (TOK, TOK), 1)
    rank = mm(hits, jnp.where(before, 1.0, 0.0).astype(BF))
    places = [jnp.sum(jnp.where(m, rank, 0.0), axis=0, keepdims=True).astype(I32) for m in named]
    found = []
    for cap, base in zip(PARTS, BASES):
        at = [place - base for place in places]
        found.append([jnp.where((at[k] >= 0) & (at[k] < cap), ids[k : k + 1] * cap + at[k], -1) for k in range(2)])
    return found


def pack_kernel(ids_hbm, x_hbm, d_hbm, rows0_ref, rows1_ref, ids_ref, x_ref, d_ref, sems):
    copies = fetch(((ids_hbm, ids_ref), (x_hbm, x_ref), (d_hbm, d_ref)), sems)
    copies[0].wait()
    picks = []
    for cap, slots in zip(PARTS, part_slots(ids_ref[...])):
        picks.append(jnp.where(onehot(slots[0], CTX * cap) | onehot(slots[1], CTX * cap), 1.0, 0.0).astype(BF))
    copies[1].wait()
    copies[2].wait()
    for pick, out in zip(picks, (rows0_ref, rows1_ref)):
        out[:, :FEAT] = mm(pick, x_ref[...]).astype(BF)
        out[:, FEAT:] = mm(pick, d_ref[...]).astype(BF)


def combine_kernel(rows0_ref, rows1_ref, ids_hbm, weights_hbm, out_ref, ids_ref, weights_ref, sems):
    for copy in fetch(((ids_hbm, ids_ref), (weights_hbm, weights_ref)), sems):
        copy.wait()
    slots = part_slots(ids_ref[...])
    columns = jnp.concatenate([weights_ref[...], jnp.zeros((6, TOK), F32)], axis=0).T
    total = jnp.zeros((TOK, FEAT), F32)
    for k in range(2):
        for p, rows_ref in enumerate((rows0_ref, rows1_ref)):
            pick = jnp.where(onehot(slots[p][k], CTX * PARTS[p]), 1.0, 0.0).astype(BF)
            total += columns[:, k : k + 1] * mm(pick, rows_ref[...], TN)
    out_ref[...] = total.astype(BF)


def sums_of_decay(decay, doc):
    upto = lax.broadcasted_iota(I32, (TOK, TOK), 0) <= lax.broadcasted_iota(I32, (TOK, TOK), 1)
    cum = lax.dot_general(
        decay,
        jnp.where(upto, 1.0, 0.0),
        (((1,), (0,)), ((), ())),
        precision=lax.Precision.HIGHEST,
        preferred_element_type=F32,
    )
    both = jnp.concatenate([cum, jnp.broadcast_to(doc.astype(F32), (HEADS, TOK))], axis=0)
    return both, both.T


def weights_of(turned):
    cum, doc = turned[:, :HEADS], turned[:, HEADS:]
    first_w = jnp.where(doc == doc[0:1], jnp.exp(cum), 0.0)
    end_w = jnp.where(doc == doc[TOK - 1 :], jnp.exp(cum[TOK - 1 :] - cum), 0.0)
    return cum, doc, first_w, end_w


def state_kernel(*refs):
    sources, out_ref, (decay_ref, doc_ref, q_ref, k_ref, v_ref, g_ref), sems = refs[:6], refs[7], refs[8:14], refs[14]
    copies = fetch(tuple(zip(sources, refs[8:14])), sems)
    copies[0].wait()
    copies[1].wait()
    _, turned = sums_of_decay(decay_ref[...], doc_ref[...])
    cum_c, doc_c, first_w, end_w = weights_of(turned)
    total, first, last = cum_c[TOK - 1 :], doc_c[0:1], doc_c[TOK - 1 :]
    line = lax.broadcasted_iota(I32, (MARKS, HD), 0)
    for copy in copies[2:]:
        copy.wait()
    for h in range(HEADS):
        cols = slice(h * HD, (h + 1) * HD)
        keys_end = (end_w[:, h : h + 1] * k_ref[:, cols].astype(F32)).astype(BF)
        queries_first = (first_w[:, h : h + 1] * q_ref[:, cols].astype(F32)).astype(BF)
        state = mm(keys_end, v_ref[:, cols], TN).astype(BF)
        adjoint = mm(queries_first, g_ref[:, cols], TN).astype(BF)
        sum_h = jnp.broadcast_to(total[:, h : h + 1], (MARKS, HD))
        high = sum_h.astype(BF).astype(F32)
        mid = (sum_h - high).astype(BF).astype(F32)
        low = sum_h - high - mid
        marks = jnp.where(line == 0, high, jnp.where(line == 1, mid, jnp.where(line == 2, low, 0.0)))
        marks = jnp.where(line == 3, first[:, h : h + 1], jnp.where(line == 4, last[:, h : h + 1], marks))
        for part in range(2):
            lines = slice(part * HALF, (part + 1) * HALF)
            out_ref[2 * h + part, 0:HALF, :] = state[lines]
            out_ref[2 * h + part, HALF:HD, :] = adjoint[lines]
            out_ref[2 * h + part, HD:, :] = marks.astype(BF)


def scan_kernel(in_ref, out_ref):
    rates, live = [], []
    prev = jnp.full((1, HD), -1.0, F32)
    for b in range(CTX):
        marks = in_ref[b, HD:, :].astype(F32)
        first, last = marks[3:4], marks[4:5]
        rates.append(jnp.where(prev == last, jnp.exp(marks[0:1] + marks[1:2] + marks[2:3]), 0.0))
        live.append(prev == first)
        prev = last
    total = jnp.zeros((HALF, HD), F32)
    for b in range(CTX):
        out_ref[b, 0:HALF, :] = jnp.where(live[b], total, 0.0).astype(BF)
        total = rates[b] * total + in_ref[b, 0:HALF, :].astype(F32)
    total = jnp.zeros((HALF, HD), F32)
    for b in reversed(range(CTX)):
        out_ref[b, HALF:, :] = total.astype(BF)
        total = rates[b] * total + jnp.where(live[b], in_ref[b, HALF:HD, :].astype(F32), 0.0)


def attention_kernel(*refs):
    sources, carried_ref, (gq_ref, gk_ref, gv_ref), (decay_ref, doc_ref, q_ref, k_ref, v_ref, g_ref), sems = (
        refs[:6], refs[6], refs[7:10], refs[10:16], refs[16]
    )
    copies = fetch(tuple(zip(sources, refs[10:16])), sems)
    copies[0].wait()
    copies[1].wait()
    row, turned = sums_of_decay(decay_ref[...], doc_ref[...])
    cum_c, doc_c, first_w, end_w = weights_of(turned)
    seen = lax.broadcasted_iota(I32, (TOK, TOK), 0) >= lax.broadcasted_iota(I32, (TOK, TOK), 1)
    same = seen & (doc_c[:, 0:1] == row[HEADS : HEADS + 1])
    for copy in copies[2:]:
        copy.wait()
    for h in range(HEADS):
        cols = slice(h * HD, (h + 1) * HD)
        q, k, v, g = q_ref[:, cols], k_ref[:, cols], v_ref[:, cols], g_ref[:, cols]
        spread = jnp.where(same, cum_c[:, h : h + 1] - row[h : h + 1], -1e30)
        decay = jnp.exp(spread)
        weighted_do = (decay * mm(g, v, NT)).astype(BF)
        weighted_qk = (decay * mm(q, k, NT)).astype(BF)
        incoming = jnp.concatenate([carried_ref[2 * h, 0:HALF, :], carried_ref[2 * h + 1, 0:HALF, :]], axis=0)
        adjoint = jnp.concatenate([carried_ref[2 * h, HALF:, :], carried_ref[2 * h + 1, HALF:, :]], axis=0)
        start = first_w[:, h : h + 1]
        end = end_w[:, h : h + 1]
        gq_ref[:, cols] = (mm(weighted_do, k) + start * mm(g, incoming, NT)).astype(BF)
        gk_ref[:, cols] = (mm(weighted_do, q, TN) + end * mm(v, adjoint, NT)).astype(BF)
        gv_ref[:, cols] = (mm(weighted_qk, g, TN) + end * mm(k, adjoint)).astype(BF)


def feature_block(place, offset, sibling):
    core = place[1]
    core = 1 - core if sibling else core
    return pl.multiple_of((((place[0] + offset) % RINGX) * 2 + core) * FEAT, FEAT)


ORDER = ((0, 0), (0, 1), (-1, 0), (-1, 1), (1, 0), (1, 1), (2, 0), (2, 1))
ALL = len(ORDER) * FEAT
OUT_ORDER = (2, -1, 1, 0)


def expert_kernel(place, *refs):
    chunks, (wg, wu, wd) = refs[:8], refs[8:11]
    (away_hbm, mine_hbm), (xs, ds, gate_w, up_w, down_w, gate_mid, up_mid, away, mine, sems, out_sems) = refs[-13:-11], refs[-11:]
    stages = ([], [], [])
    for i, (offset, sibling) in enumerate(ORDER):
        block = feature_block(place, offset, sibling)
        side = pl.ds(i * FEAT, FEAT)
        stages[0].append((wd.at[0, :, pl.ds(block, FEAT)], down_w.at[:, side]))
        stages[0].append((chunks[i].at[:, pl.ds(FEAT, FEAT)], ds.at[:, side]))
        stages[1].append((wg.at[0, pl.ds(block, FEAT), :], gate_w.at[side, :]))
        stages[1].append((chunks[i].at[:, pl.ds(0, FEAT)], xs.at[:, side]))
        stages[2].append((wu.at[0, pl.ds(block, FEAT), :], up_w.at[side, :]))
    copies = fetch(stages[0] + stages[1] + stages[2], sems)

    def ready(n):
        for _ in range(n):
            copies.pop(0).wait()

    ready(len(stages[0]))
    hid = mm(ds[...], down_w[...], NT)
    ready(len(stages[1]))
    gate = mm(xs[...], gate_w[...])
    ready(len(stages[2]))
    up = mm(xs[...], up_w[...])
    s = 1.0 / (1.0 + jnp.exp(-gate))
    gate_mid[...] = (hid * up * s * (1.0 + gate * (1.0 - s))).astype(BF)
    up_mid[...] = (hid * gate * s).astype(BF)
    leaving = []
    for sibling, buffer, out in ((1, away, away_hbm), (0, mine, mine_hbm)):
        for i, offset in enumerate(OUT_ORDER):
            at = slice(ORDER.index((offset, sibling)) * FEAT, (ORDER.index((offset, sibling)) + 1) * FEAT)
            buffer[i] = (mm(gate_mid[...], gate_w[at, :], NT) + mm(up_mid[...], up_w[at, :], NT)).astype(out.dtype)
            leaving.append(pltpu.make_async_copy(buffer.at[i], out.at[i], out_sems.at[len(leaving)]))
            leaving[-1].start()
    for copy in leaving:
        copy.wait()


def add_kernel(mine_hbm, away, *refs):
    outs, (mine, sems) = refs[-6:-2], refs[-2:]
    copies = fetch([(mine_hbm.at[i], mine.at[i]) for i in range(RINGX)], sems)
    for i, out in enumerate(outs):
        copies[i].wait()
        out[...] = (mine[i] + away[i].astype(F32)).astype(out.dtype)


def local(
    queries, keys, values, out_grad, log_decay, doc_ids, moe_input, moe_cotangent, router_weights, expert_ids, w_gate, w_up, w_down
):
    S = jax.ShapeDtypeStruct
    place = jnp.stack([lax.axis_index("x"), lax.axis_index("core")]).astype(I32)
    smem = pl.BlockSpec(memory_space=pltpu.SMEM)

    def ring(value, way):
        return lax.ppermute(value, "x", way)

    def swap(value):
        return lax.ppermute(value, "core", SWAP)

    ids = in_hbm(expert_ids.T)
    rows = call(
        pack_kernel,
        tuple(S((CTX * cap, 2 * FEAT), BF) for cap in PARTS),
        [anywhere()] * 3,
        [pltpu.VMEM((2, TOK), I32)] + [pltpu.VMEM((TOK, FEAT), BF)] * 2 + [pltpu.SemaphoreType.DMA((3,))],
        flops=2 * CTX * CAP * TOK * 2 * FEAT,
        size=2 * MIB,
        limit=6,
    )(ids, in_hbm(moe_input), in_hbm(moe_cotangent))
    own = [
        lax.all_to_all(r.reshape(CTX, cap, 2 * FEAT), "ctx", 0, 0, tiled=True).reshape(CTX * cap, 2 * FEAT)
        for r, cap in zip(rows, PARTS)
    ]
    chunks = []
    for p in range(2):
        from_left, from_right = ring(own[p], RIGHT), ring(own[p], LEFT)
        far = ring(from_left, RIGHT) if p == 0 else ring(from_right, LEFT)
        chunks.append([c for a in (own[p], from_left, from_right, far) for c in (a, swap(a))])
    branch = [in_hbm(a) for a in (log_decay, doc_ids.reshape(1, TOK), queries, keys, values, out_grad)]
    held = [pltpu.VMEM((HEADS, TOK), F32), pltpu.VMEM((1, TOK), I32)] + [pltpu.VMEM((TOK, HEADS * HD), BF)] * 4
    held += [pltpu.SemaphoreType.DMA((6,))]
    message = call(
        state_kernel,
        S((CTX, HD + MARKS, HD), BF),
        [anywhere()] * 7,
        held,
        flops=4 * HEADS * TOK * HD * HD,
        size=3 * MIB,
        limit=8,
    )(*branch, own[0])
    arrived = lax.all_to_all(message, "ctx", 0, 0, tiled=True)
    scanned = call(scan_kernel, S((CTX, HD, HD), BF), [vmem()], flops=MIB, size=MIB, limit=4)(arrived)
    carried = lax.all_to_all(scanned, "ctx", 0, 0, tiled=True)
    grads = call(
        attention_kernel,
        (S((TOK, HEADS * HD), BF),) * 3,
        [anywhere()] * 6 + [vmem()],
        held,
        flops=16 * HEADS * TOK * TOK * HD,
        size=4 * MIB,
        limit=12,
    )(*branch, carried)

    weights = [in_hbm(w) for w in (w_gate, w_up, w_down)]
    back, before, between = [], [message, chunks[1][2], chunks[1][6]], []
    for p, cap in enumerate(PARTS):
        r = CTX * cap
        block, wide = S((r, FEAT), BF), S((r, FEAT), F32)
        away, mine = call(
            expert_kernel,
            (pltpu.HBM((RINGX, r, FEAT), BF), pltpu.HBM((RINGX, r, FEAT), F32)),
            [smem] + [anywhere()] * (11 + len(before)),
            [pltpu.VMEM((r, ALL), BF)] * 2
            + [pltpu.VMEM((ALL, HID), BF)] * 2
            + [pltpu.VMEM((HID, ALL), BF)]
            + [pltpu.VMEM((r, HID), BF)] * 2
            + [pltpu.VMEM((RINGX, r, FEAT), BF), pltpu.VMEM((RINGX, r, FEAT), F32)]
            + [pltpu.SemaphoreType.DMA((5 * len(ORDER),)), pltpu.SemaphoreType.DMA((2 * RINGX,))],
            flops=10 * r * HID * ALL,
            size=20 * MIB,
            limit=40,
        )(place, *[in_hbm(c) for c in chunks[p]], *weights, *before)
        away = swap(away)
        sides = (block, wide) if p == 0 else (wide, block)
        far, left, right, here = call(
            add_kernel,
            (block, *sides, wide),
            [anywhere(), vmem()] + [anywhere()] * len(between),
            [pltpu.VMEM((RINGX, r, FEAT), F32), pltpu.SemaphoreType.DMA((RINGX,))],
            flops=r * FEAT * 4,
            size=4 * MIB,
            limit=10,
        )(in_hbm(mine), away, *between)
        before = [far, scanned]
        if p == 0:
            right = (right + ring(far, RIGHT).astype(F32)).astype(BF)
        else:
            left = (left + ring(far, LEFT).astype(F32)).astype(BF)
        summed = (here + ring(right, RIGHT).astype(F32) + ring(left, LEFT).astype(F32)).astype(BF)
        between = [summed]
        got = lax.all_to_all(summed.reshape(CTX, cap, FEAT), "ctx", 0, 0, tiled=True)
        back.append(got.reshape(r, FEAT))
    grad_moe = call(
        combine_kernel,
        S((TOK, FEAT), BF),
        [vmem()] * 2 + [anywhere()] * 2,
        [pltpu.VMEM((2, TOK), I32), pltpu.VMEM((2, TOK), F32), pltpu.SemaphoreType.DMA((2,))],
        flops=4 * CTX * CAP * TOK * FEAT,
        size=MIB,
        limit=8,
    )(*back, ids, in_hbm(router_weights.T))
    return (*grads, grad_moe)


def solution(mesh):
    fine = Mesh(mesh.devices.reshape(CTX, RINGX, 2), ("ctx", "x", "core"))
    ep = ("x", "core")
    row = P("ctx", ep)
    in_specs = (row, row, row, row, P(ep, "ctx"), P("ctx"), row, row, P("ctx", None), P("ctx", None))
    in_specs += (P("ctx", None, ep), P("ctx", None, ep), P("ctx", ep, None))
    return jax.shard_map(local, mesh=fine, in_specs=in_specs, out_specs=(row,) * 4, check_vma=False)
```

```python
import jax
import jax.numpy as jnp
from jax import lax
from jax.experimental import pallas as pl
from jax.experimental.pallas import tpu as pltpu
from jax.sharding import Mesh, PartitionSpec as P

BF = jnp.bfloat16
F32 = jnp.float32
I32 = jnp.int32
TOK = 256
HEADS = 8
HD = 128
HALF = HD // 2
CTX = 16
CAP = 40
ROWS = CTX * CAP
CUT = ROWS // 2
FEAT = 384
HID = 640
MARKS = 16
RINGX = 4
RIGHT = [(i, (i + 1) % RINGX) for i in range(RINGX)]
LEFT = [(i, (i - 1) % RINGX) for i in range(RINGX)]
SWAP = [(0, 1), (1, 0)]
MIB = 1 << 20

NT = (((1,), (1,)), ((), ()))
TN = (((0,), (0,)), ((), ()))


def vmem():
    return pl.BlockSpec(memory_space=pltpu.VMEM)


def anywhere():
    return pl.BlockSpec(memory_space=pl.ANY)


def in_hbm(value):
    return pltpu.with_memory_space_constraint(value, pltpu.HBM)


def call(kernel, outs, ins, scratch=(), flops=0, size=0, limit=32):
    return pl.pallas_call(
        kernel,
        out_shape=outs,
        in_specs=ins,
        out_specs=jax.tree.map(lambda o: vmem() if isinstance(o, jax.ShapeDtypeStruct) else anywhere(), outs),
        scratch_shapes=scratch,
        compiler_params=pltpu.CompilerParams(vmem_limit_bytes=limit * MIB),
        cost_estimate=pl.CostEstimate(flops=flops, bytes_accessed=size, transcendentals=0),
    )


def fetch(pairs, sems):
    copies = [pltpu.make_async_copy(src, dst, sems.at[i]) for i, (src, dst) in enumerate(pairs)]
    for copy in copies:
        copy.start()
    return copies


def mm(a, b, dims=(((1,), (0,)), ((), ()))):
    return lax.dot_general(a, b, dims, preferred_element_type=F32)


def onehot(slot):
    return lax.broadcasted_iota(I32, (ROWS, TOK), 0) == slot


def slots_of(ids):
    expert = lax.broadcasted_iota(I32, (CTX, TOK), 0)
    named = [ids[k : k + 1] == expert for k in range(2)]
    hits = jnp.where(named[0] | named[1], 1.0, 0.0).astype(BF)
    before = lax.broadcasted_iota(I32, (TOK, TOK), 0) < lax.broadcasted_iota(I32, (TOK, TOK), 1)
    rank = mm(hits, jnp.where(before, 1.0, 0.0).astype(BF))
    places = [jnp.sum(jnp.where(m, rank, 0.0), axis=0, keepdims=True).astype(I32) for m in named]
    return [ids[k : k + 1] * CAP + places[k] for k in range(2)]


def pack_kernel(ids_hbm, x_hbm, d_hbm, rows_ref, ids_ref, x_ref, d_ref, sems):
    copies = fetch(((ids_hbm, ids_ref), (x_hbm, x_ref), (d_hbm, d_ref)), sems)
    copies[0].wait()
    slots = slots_of(ids_ref[...])
    pick = jnp.where(onehot(slots[0]) | onehot(slots[1]), 1.0, 0.0).astype(BF)
    copies[1].wait()
    rows_ref[:, :FEAT] = mm(pick, x_ref[...]).astype(BF)
    copies[2].wait()
    rows_ref[:, FEAT:] = mm(pick, d_ref[...]).astype(BF)


def combine_kernel(rows_ref, ids_hbm, weights_hbm, out_ref, ids_ref, weights_ref, sems):
    for copy in fetch(((ids_hbm, ids_ref), (weights_hbm, weights_ref)), sems):
        copy.wait()
    columns = jnp.concatenate([weights_ref[...], jnp.zeros((6, TOK), F32)], axis=0).T
    total = jnp.zeros((TOK, FEAT), F32)
    for k, slot in enumerate(slots_of(ids_ref[...])):
        pick = jnp.where(onehot(slot), 1.0, 0.0).astype(BF)
        total += columns[:, k : k + 1] * mm(pick, rows_ref[...], TN)
    out_ref[...] = total.astype(BF)


def sums_of_decay(decay, doc):
    upto = lax.broadcasted_iota(I32, (TOK, TOK), 0) <= lax.broadcasted_iota(I32, (TOK, TOK), 1)
    cum = lax.dot_general(
        decay,
        jnp.where(upto, 1.0, 0.0),
        (((1,), (0,)), ((), ())),
        precision=lax.Precision.HIGHEST,
        preferred_element_type=F32,
    )
    both = jnp.concatenate([cum, jnp.broadcast_to(doc.astype(F32), (HEADS, TOK))], axis=0)
    return both, both.T


def weights_of(turned):
    cum, doc = turned[:, :HEADS], turned[:, HEADS:]
    first_w = jnp.where(doc == doc[0:1], jnp.exp(cum), 0.0)
    end_w = jnp.where(doc == doc[TOK - 1 :], jnp.exp(cum[TOK - 1 :] - cum), 0.0)
    return cum, doc, first_w, end_w


def state_kernel(*refs):
    sources, out_ref, (decay_ref, doc_ref, q_ref, k_ref, v_ref, g_ref), sems = refs[:6], refs[7], refs[8:14], refs[14]
    copies = fetch(tuple(zip(sources, refs[8:14])), sems)
    copies[0].wait()
    copies[1].wait()
    _, turned = sums_of_decay(decay_ref[...], doc_ref[...])
    cum_c, doc_c, first_w, end_w = weights_of(turned)
    total, first, last = cum_c[TOK - 1 :], doc_c[0:1], doc_c[TOK - 1 :]
    line = lax.broadcasted_iota(I32, (MARKS, HD), 0)
    for copy in copies[2:]:
        copy.wait()
    for h in range(HEADS):
        cols = slice(h * HD, (h + 1) * HD)
        keys_end = (end_w[:, h : h + 1] * k_ref[:, cols].astype(F32)).astype(BF)
        queries_first = (first_w[:, h : h + 1] * q_ref[:, cols].astype(F32)).astype(BF)
        state = mm(keys_end, v_ref[:, cols], TN).astype(BF)
        adjoint = mm(queries_first, g_ref[:, cols], TN).astype(BF)
        sum_h = jnp.broadcast_to(total[:, h : h + 1], (MARKS, HD))
        high = sum_h.astype(BF).astype(F32)
        mid = (sum_h - high).astype(BF).astype(F32)
        low = sum_h - high - mid
        marks = jnp.where(line == 0, high, jnp.where(line == 1, mid, jnp.where(line == 2, low, 0.0)))
        marks = jnp.where(line == 3, first[:, h : h + 1], jnp.where(line == 4, last[:, h : h + 1], marks))
        for part in range(2):
            lines = slice(part * HALF, (part + 1) * HALF)
            out_ref[2 * h + part, 0:HALF, :] = state[lines]
            out_ref[2 * h + part, HALF:HD, :] = adjoint[lines]
            out_ref[2 * h + part, HD:, :] = marks.astype(BF)


def scan_kernel(in_ref, out_ref):
    rates, live = [], []
    prev = jnp.full((1, HD), -1.0, F32)
    for b in range(CTX):
        marks = in_ref[b, HD:, :].astype(F32)
        first, last = marks[3:4], marks[4:5]
        rates.append(jnp.where(prev == last, jnp.exp(marks[0:1] + marks[1:2] + marks[2:3]), 0.0))
        live.append(prev == first)
        prev = last
    total = jnp.zeros((HALF, HD), F32)
    for b in range(CTX):
        out_ref[b, 0:HALF, :] = jnp.where(live[b], total, 0.0).astype(BF)
        total = rates[b] * total + in_ref[b, 0:HALF, :].astype(F32)
    total = jnp.zeros((HALF, HD), F32)
    for b in reversed(range(CTX)):
        out_ref[b, HALF:, :] = total.astype(BF)
        total = rates[b] * total + jnp.where(live[b], in_ref[b, HALF:HD, :].astype(F32), 0.0)


def attention_kernel(*refs):
    sources, carried_ref, (gq_ref, gk_ref, gv_ref), (decay_ref, doc_ref, q_ref, k_ref, v_ref, g_ref), sems = (
        refs[:6], refs[6], refs[7:10], refs[10:16], refs[16]
    )
    copies = fetch(tuple(zip(sources, refs[10:16])), sems)
    copies[0].wait()
    copies[1].wait()
    row, turned = sums_of_decay(decay_ref[...], doc_ref[...])
    cum_c, doc_c, first_w, end_w = weights_of(turned)
    seen = lax.broadcasted_iota(I32, (TOK, TOK), 0) >= lax.broadcasted_iota(I32, (TOK, TOK), 1)
    same = seen & (doc_c[:, 0:1] == row[HEADS : HEADS + 1])
    for copy in copies[2:]:
        copy.wait()
    for h in range(HEADS):
        cols = slice(h * HD, (h + 1) * HD)
        q, k, v, g = q_ref[:, cols], k_ref[:, cols], v_ref[:, cols], g_ref[:, cols]
        spread = jnp.where(same, cum_c[:, h : h + 1] - row[h : h + 1], -1e30)
        decay = jnp.exp(spread)
        weighted_do = (decay * mm(g, v, NT)).astype(BF)
        weighted_qk = (decay * mm(q, k, NT)).astype(BF)
        incoming = jnp.concatenate([carried_ref[2 * h, 0:HALF, :], carried_ref[2 * h + 1, 0:HALF, :]], axis=0)
        adjoint = jnp.concatenate([carried_ref[2 * h, HALF:, :], carried_ref[2 * h + 1, HALF:, :]], axis=0)
        start = first_w[:, h : h + 1]
        end = end_w[:, h : h + 1]
        gq_ref[:, cols] = (mm(weighted_do, k) + start * mm(g, incoming, NT)).astype(BF)
        gk_ref[:, cols] = (mm(weighted_do, q, TN) + end * mm(v, adjoint, NT)).astype(BF)
        gv_ref[:, cols] = (mm(weighted_qk, g, TN) + end * mm(k, adjoint)).astype(BF)


def feature_block(place, offset, sibling):
    core = place[1]
    core = 1 - core if sibling else core
    return pl.multiple_of((((place[0] + offset) % RINGX) * 2 + core) * FEAT, FEAT)


ORDER = ((0, 0), (0, 1), (-1, 0), (-1, 1), (1, 0), (1, 1), (2, 0), (2, 1))
ALL = len(ORDER) * FEAT
EARLY = 6
OUT_ORDER = (2, -1, 1, 0)


def forward_kernel(from_left, from_right, token, x_ref, d_ref, sems):
    pairs = ((from_left.at[:, pl.ds(0, FEAT)], x_ref), (from_right.at[:, pl.ds(FEAT, FEAT)], d_ref))
    for copy in fetch(pairs, sems):
        copy.wait()


def expert_early_kernel(place, *refs):
    chunks, (wg, wu, wd) = refs[:EARLY], refs[EARLY : EARLY + 3]
    (pre, hid, cat, down_late), (xs, ds, down_w, sems) = refs[-8:-4], refs[-4:]
    stages = ([], [], [], [])
    for i, (offset, sibling) in enumerate(ORDER):
        block = feature_block(place, offset, sibling)
        side = pl.ds(i * FEAT, FEAT)
        late = i >= EARLY
        if not late:
            stages[0].append((wd.at[0, :, pl.ds(block, FEAT)], down_w.at[:, side]))
            stages[0].append((chunks[i].at[:, pl.ds(FEAT, FEAT)], ds.at[:, side]))
            stages[1].append((chunks[i].at[:, pl.ds(0, FEAT)], xs.at[:, side]))
        else:
            stages[3].append((wd.at[0, :, pl.ds(block, FEAT)], down_late.at[:, pl.ds((i - EARLY) * FEAT, FEAT)]))
        stages[3 if late else 1].append((wg.at[0, pl.ds(block, FEAT), :], cat.at[side, pl.ds(0, HID)]))
        stages[3 if late else 2].append((wu.at[0, pl.ds(block, FEAT), :], cat.at[side, pl.ds(HID, HID)]))
    copies = fetch(stages[0] + stages[1] + stages[2] + stages[3], sems)

    def ready(n):
        for _ in range(n):
            copies.pop(0).wait()

    ready(len(stages[0]))
    hid[...] = mm(ds[...], down_w[...], NT)
    ready(len(stages[1]))
    pre[:, :HID] = mm(xs[...], cat[: EARLY * FEAT, :HID])
    ready(len(stages[2]))
    pre[:, HID:] = mm(xs[...], cat[: EARLY * FEAT, HID:])
    ready(len(stages[3]))


def out_block(mid_ref, cat, offset, sibling):
    at = ORDER.index((offset, sibling)) * FEAT
    return mm(mid_ref[...], cat[at : at + FEAT, :], NT)


def expert_mid_kernel(pre, hid_ref, x0, d0, x1, d1, cat, down_late, mid_ref, far_ref, rest_ref):
    late = slice(EARLY * FEAT, None)
    hid = hid_ref[...] + mm(jnp.concatenate([d0[...], d1[...]], axis=1), down_late[...], NT)
    both = pre[...] + mm(jnp.concatenate([x0[...], x1[...]], axis=1), cat[late, :])
    gate, up = both[:, :HID], both[:, HID:]
    s = 1.0 / (1.0 + jnp.exp(-gate))
    mid_ref[:, :HID] = (hid * up * s * (1.0 + gate * (1.0 - s))).astype(BF)
    mid_ref[:, HID:] = (hid * gate * s).astype(BF)
    far_ref[...] = out_block(mid_ref, cat, OUT_ORDER[0], 1).astype(BF)
    for i, offset in enumerate(OUT_ORDER[1:]):
        rest_ref[i] = out_block(mid_ref, cat, offset, 1).astype(BF)


def expert_out_kernel(mid_ref, cat, far_ref, rest_ref):
    far_ref[...] = out_block(mid_ref, cat, OUT_ORDER[0], 0)
    for i, offset in enumerate(OUT_ORDER[1:]):
        rest_ref[i] = out_block(mid_ref, cat, offset, 0)


def far_kernel(mine, away, right_ref, left_ref):
    right_ref[...] = (mine[:CUT] + away[:CUT].astype(F32)).astype(BF)
    left_ref[...] = (mine[CUT:] + away[CUT:].astype(F32)).astype(BF)


def near_kernel(mine, away, via_right, via_left, left_ref, right_ref, here_ref):
    left_ref[:CUT] = (mine[0, :CUT] + away[0, :CUT].astype(F32)).astype(BF)
    left_ref[CUT:] = (mine[0, CUT:] + away[0, CUT:].astype(F32) + via_left[...].astype(F32)).astype(BF)
    right_ref[:CUT] = (mine[1, :CUT] + away[1, :CUT].astype(F32) + via_right[...].astype(F32)).astype(BF)
    right_ref[CUT:] = (mine[1, CUT:] + away[1, CUT:].astype(F32)).astype(BF)
    here_ref[...] = mine[2] + away[2].astype(F32)


def local(
    queries, keys, values, out_grad, log_decay, doc_ids, moe_input, moe_cotangent, router_weights, expert_ids, w_gate, w_up, w_down
):
    S = jax.ShapeDtypeStruct
    place = jnp.stack([lax.axis_index("x"), lax.axis_index("core")]).astype(I32)
    smem = pl.BlockSpec(memory_space=pltpu.SMEM)
    block = S((ROWS, FEAT), BF)

    def ring(value, way):
        return lax.ppermute(value, "x", way)

    def swap(value):
        return lax.ppermute(value, "core", SWAP)

    ids = in_hbm(expert_ids.T)
    rows = call(
        pack_kernel,
        S((ROWS, 2 * FEAT), BF),
        [anywhere()] * 3,
        [pltpu.VMEM((2, TOK), I32)] + [pltpu.VMEM((TOK, FEAT), BF)] * 2 + [pltpu.SemaphoreType.DMA((3,))],
        flops=2 * ROWS * TOK * 2 * FEAT,
        size=2 * MIB,
        limit=6,
    )(ids, in_hbm(moe_input), in_hbm(moe_cotangent))
    own = lax.all_to_all(rows.reshape(CTX, CAP, 2 * FEAT), "ctx", 0, 0, tiled=True).reshape(ROWS, 2 * FEAT)
    from_left, from_right = ring(own, RIGHT), ring(own, LEFT)

    branch = [in_hbm(a) for a in (log_decay, doc_ids.reshape(1, TOK), queries, keys, values, out_grad)]
    held = [pltpu.VMEM((HEADS, TOK), F32), pltpu.VMEM((1, TOK), I32)] + [pltpu.VMEM((TOK, HEADS * HD), BF)] * 4
    held += [pltpu.SemaphoreType.DMA((6,))]
    message = call(
        state_kernel,
        S((CTX, HD + MARKS, HD), BF),
        [anywhere()] * 7,
        held,
        flops=4 * HEADS * TOK * HD * HD,
        size=3 * MIB,
        limit=8,
    )(*branch, own)
    arrived = lax.all_to_all(message, "ctx", 0, 0, tiled=True)

    x_far, d_far = call(
        forward_kernel,
        (block, block),
        [anywhere()] * 3,
        [pltpu.SemaphoreType.DMA((2,))],
        size=2 * MIB,
        limit=4,
    )(from_left, from_right, arrived)
    x_far, d_far = ring(x_far, RIGHT), ring(d_far, LEFT)
    early = [c for a in (own, from_left, from_right) for c in (a, swap(a))]

    scanned = call(scan_kernel, S((CTX, HD, HD), BF), [vmem()], flops=MIB, size=MIB, limit=4)(arrived)
    carried = lax.all_to_all(scanned, "ctx", 0, 0, tiled=True)
    grads = call(
        attention_kernel,
        (S((TOK, HEADS * HD), BF),) * 3,
        [anywhere()] * 6 + [vmem()],
        held,
        flops=16 * HEADS * TOK * TOK * HD,
        size=4 * MIB,
        limit=12,
    )(*branch, carried)

    n = EARLY * FEAT
    pre, hid, cat, down_late = call(
        expert_early_kernel,
        (S((ROWS, 2 * HID), F32), S((ROWS, HID), F32), S((ALL, 2 * HID), BF), S((HID, ALL - n), BF)),
        [smem] + [anywhere()] * (EARLY + 4),
        [pltpu.VMEM((ROWS, n), BF)] * 2 + [pltpu.VMEM((HID, n), BF), pltpu.SemaphoreType.DMA((36,))],
        flops=6 * ROWS * HID * n,
        size=24 * MIB,
        limit=28,
    )(place, *early, *[in_hbm(w) for w in (w_gate, w_up, w_down)], scanned)
    x_far, d_far, pre = lax.optimization_barrier((x_far, d_far, pre))
    mid, away_far, away_rest = call(
        expert_mid_kernel,
        (S((ROWS, 2 * HID), BF), block, S((RINGX - 1, ROWS, FEAT), BF)),
        [vmem()] * 8,
        flops=10 * ROWS * HID * RINGX * FEAT,
        size=14 * MIB,
        limit=32,
    )(pre, hid, x_far, d_far, swap(x_far), swap(d_far), cat, down_late)
    away_far, away_rest = swap(away_far), swap(away_rest)
    mine_far, mine_rest = call(
        expert_out_kernel,
        (S((ROWS, FEAT), F32), S((RINGX - 1, ROWS, FEAT), F32)),
        [vmem()] * 2,
        flops=4 * ROWS * HID * RINGX * FEAT,
        size=8 * MIB,
        limit=18,
    )(mid, cat)

    half = S((CUT, FEAT), BF)
    to_right, to_left = call(far_kernel, (half, half), [vmem()] * 2, size=2 * MIB, flops=MIB, limit=8)(mine_far, away_far)
    via_right, via_left = ring(to_right, RIGHT), ring(to_left, LEFT)
    to_left, to_right, here = call(
        near_kernel, (block, block, S((ROWS, FEAT), F32)), [vmem()] * 4, size=5 * MIB, flops=MIB, limit=16
    )(mine_rest, away_rest, via_right, via_left)
    summed = (here + ring(to_right, RIGHT).astype(F32) + ring(to_left, LEFT).astype(F32)).astype(BF)
    back = lax.all_to_all(summed.reshape(CTX, CAP, FEAT), "ctx", 0, 0, tiled=True)
    grad_moe = call(
        combine_kernel,
        S((TOK, FEAT), BF),
        [vmem()] + [anywhere()] * 2,
        [pltpu.VMEM((2, TOK), I32), pltpu.VMEM((2, TOK), F32), pltpu.SemaphoreType.DMA((2,))],
        flops=4 * ROWS * TOK * FEAT,
        size=MIB,
        limit=8,
    )(back.reshape(ROWS, FEAT), ids, in_hbm(router_weights.T))
    return (*grads, grad_moe)


def solution(mesh):
    fine = Mesh(mesh.devices.reshape(CTX, RINGX, 2), ("ctx", "x", "core"))
    ep = ("x", "core")
    row = P("ctx", ep)
    in_specs = (row, row, row, row, P(ep, "ctx"), P("ctx"), row, row, P("ctx", None), P("ctx", None))
    in_specs += (P("ctx", None, ep), P("ctx", None, ep), P("ctx", ep, None))
    return jax.shard_map(local, mesh=fine, in_specs=in_specs, out_specs=(row,) * 4, check_vma=False)
```

```python
import jax
import jax.numpy as jnp
from jax import lax
from jax.experimental import pallas as pl
from jax.experimental.pallas import tpu as pltpu
from jax.sharding import Mesh, PartitionSpec as P

BF = jnp.bfloat16
F32 = jnp.float32
I32 = jnp.int32
TOK = 256
HEADS = 8
HD = 128
HALF = HD // 2
CTX = 16
CAP = 40
ROWS = CTX * CAP
CUT = ROWS // 2
FEAT = 384
HID = 640
MARKS = 16
RINGX = 4
RIGHT = [(i, (i + 1) % RINGX) for i in range(RINGX)]
LEFT = [(i, (i - 1) % RINGX) for i in range(RINGX)]
SWAP = [(0, 1), (1, 0)]
MIB = 1 << 20

NT = (((1,), (1,)), ((), ()))
TN = (((0,), (0,)), ((), ()))


def vmem():
    return pl.BlockSpec(memory_space=pltpu.VMEM)


def anywhere():
    return pl.BlockSpec(memory_space=pl.ANY)


def in_hbm(value):
    return pltpu.with_memory_space_constraint(value, pltpu.HBM)


def call(kernel, outs, ins, scratch=(), flops=0, size=0, limit=32):
    return pl.pallas_call(
        kernel,
        out_shape=outs,
        in_specs=ins,
        out_specs=jax.tree.map(lambda o: vmem() if isinstance(o, jax.ShapeDtypeStruct) else anywhere(), outs),
        scratch_shapes=scratch,
        compiler_params=pltpu.CompilerParams(vmem_limit_bytes=limit * MIB),
        cost_estimate=pl.CostEstimate(flops=flops, bytes_accessed=size, transcendentals=0),
    )


def fetch(pairs, sems):
    copies = [pltpu.make_async_copy(src, dst, sems.at[i]) for i, (src, dst) in enumerate(pairs)]
    for copy in copies:
        copy.start()
    return copies


def mm(a, b, dims=(((1,), (0,)), ((), ()))):
    return lax.dot_general(a, b, dims, preferred_element_type=F32)


def onehot(slot):
    return lax.broadcasted_iota(I32, (ROWS, TOK), 0) == slot


def slots_of(ids):
    expert = lax.broadcasted_iota(I32, (CTX, TOK), 0)
    named = [ids[k : k + 1] == expert for k in range(2)]
    hits = jnp.where(named[0] | named[1], 1.0, 0.0).astype(BF)
    before = lax.broadcasted_iota(I32, (TOK, TOK), 0) < lax.broadcasted_iota(I32, (TOK, TOK), 1)
    rank = mm(hits, jnp.where(before, 1.0, 0.0).astype(BF))
    places = [jnp.sum(jnp.where(m, rank, 0.0), axis=0, keepdims=True).astype(I32) for m in named]
    return [ids[k : k + 1] * CAP + places[k] for k in range(2)]


def pack_kernel(ids_hbm, x_hbm, d_hbm, rows_ref, slots_hbm, ids_ref, x_ref, d_ref, slots_ref, sems):
    copies = fetch(((ids_hbm, ids_ref), (x_hbm, x_ref), (d_hbm, d_ref)), sems)
    copies[0].wait()
    slots = slots_of(ids_ref[...])
    slots_ref[0:1, :], slots_ref[1:2, :] = slots
    leaving = pltpu.make_async_copy(slots_ref, slots_hbm, sems.at[3])
    leaving.start()
    pick = jnp.where(onehot(slots[0]) | onehot(slots[1]), 1.0, 0.0).astype(BF)
    copies[1].wait()
    rows_ref[:, :FEAT] = mm(pick, x_ref[...]).astype(BF)
    copies[2].wait()
    rows_ref[:, FEAT:] = mm(pick, d_ref[...]).astype(BF)
    leaving.wait()


def combine_kernel(rows_ref, slots_hbm, weights_hbm, out_ref, slots_ref, weights_ref, sems):
    for copy in fetch(((slots_hbm, slots_ref), (weights_hbm, weights_ref)), sems):
        copy.wait()
    columns = jnp.concatenate([weights_ref[...], jnp.zeros((6, TOK), F32)], axis=0).T
    total = jnp.zeros((TOK, FEAT), F32)
    for k in range(2):
        pick = jnp.where(onehot(slots_ref[k : k + 1, :]), 1.0, 0.0).astype(BF)
        total += columns[:, k : k + 1] * mm(pick, rows_ref[...], TN)
    out_ref[...] = total.astype(BF)


def sums_of_decay(decay, doc):
    upto = lax.broadcasted_iota(I32, (TOK, TOK), 0) <= lax.broadcasted_iota(I32, (TOK, TOK), 1)
    cum = lax.dot_general(
        decay,
        jnp.where(upto, 1.0, 0.0),
        (((1,), (0,)), ((), ())),
        precision=lax.Precision.HIGHEST,
        preferred_element_type=F32,
    )
    both = jnp.concatenate([cum, jnp.broadcast_to(doc.astype(F32), (HEADS, TOK))], axis=0)
    return both, both.T


def weights_of(turned):
    cum, doc = turned[:, :HEADS], turned[:, HEADS:]
    first_w = jnp.where(doc == doc[0:1], jnp.exp(cum), 0.0)
    end_w = jnp.where(doc == doc[TOK - 1 :], jnp.exp(cum[TOK - 1 :] - cum), 0.0)
    return cum, doc, first_w, end_w


def state_kernel(*refs):
    sources, out_ref, (decay_ref, doc_ref, q_ref, k_ref, v_ref, g_ref), sems = refs[:6], refs[7], refs[8:14], refs[14]
    copies = fetch(tuple(zip(sources, refs[8:14])), sems)
    copies[0].wait()
    copies[1].wait()
    _, turned = sums_of_decay(decay_ref[...], doc_ref[...])
    cum_c, doc_c, first_w, end_w = weights_of(turned)
    total, first, last = cum_c[TOK - 1 :], doc_c[0:1], doc_c[TOK - 1 :]
    line = lax.broadcasted_iota(I32, (MARKS, HD), 0)
    for copy in copies[2:]:
        copy.wait()
    for h in range(HEADS):
        cols = slice(h * HD, (h + 1) * HD)
        keys_end = (end_w[:, h : h + 1] * k_ref[:, cols].astype(F32)).astype(BF)
        queries_first = (first_w[:, h : h + 1] * q_ref[:, cols].astype(F32)).astype(BF)
        state = mm(keys_end, v_ref[:, cols], TN).astype(BF)
        adjoint = mm(queries_first, g_ref[:, cols], TN).astype(BF)
        sum_h = jnp.broadcast_to(total[:, h : h + 1], (MARKS, HD))
        high = sum_h.astype(BF).astype(F32)
        mid = (sum_h - high).astype(BF).astype(F32)
        low = sum_h - high - mid
        marks = jnp.where(line == 0, high, jnp.where(line == 1, mid, jnp.where(line == 2, low, 0.0)))
        marks = jnp.where(line == 3, first[:, h : h + 1], jnp.where(line == 4, last[:, h : h + 1], marks))
        for part in range(2):
            lines = slice(part * HALF, (part + 1) * HALF)
            out_ref[2 * h + part, 0:HALF, :] = state[lines]
            out_ref[2 * h + part, HALF:HD, :] = adjoint[lines]
            out_ref[2 * h + part, HD:, :] = marks.astype(BF)


def scan_kernel(in_ref, out_ref):
    rates, live = [], []
    prev = jnp.full((1, HD), -1.0, F32)
    for b in range(CTX):
        marks = in_ref[b, HD:, :].astype(F32)
        first, last = marks[3:4], marks[4:5]
        rates.append(jnp.where(prev == last, jnp.exp(marks[0:1] + marks[1:2] + marks[2:3]), 0.0))
        live.append(prev == first)
        prev = last
    total = jnp.zeros((HALF, HD), F32)
    for b in range(CTX):
        out_ref[b, 0:HALF, :] = jnp.where(live[b], total, 0.0).astype(BF)
        total = rates[b] * total + in_ref[b, 0:HALF, :].astype(F32)
    total = jnp.zeros((HALF, HD), F32)
    for b in reversed(range(CTX)):
        out_ref[b, HALF:, :] = total.astype(BF)
        total = rates[b] * total + jnp.where(live[b], in_ref[b, HALF:HD, :].astype(F32), 0.0)


def attention_kernel(*refs):
    sources, carried_ref, (gq_ref, gk_ref, gv_ref), (decay_ref, doc_ref, q_ref, k_ref, v_ref, g_ref), sems = (
        refs[:6], refs[6], refs[7:10], refs[10:16], refs[16]
    )
    copies = fetch(tuple(zip(sources, refs[10:16])), sems)
    copies[0].wait()
    copies[1].wait()
    row, turned = sums_of_decay(decay_ref[...], doc_ref[...])
    cum_c, doc_c, first_w, end_w = weights_of(turned)
    seen = lax.broadcasted_iota(I32, (TOK, TOK), 0) >= lax.broadcasted_iota(I32, (TOK, TOK), 1)
    same = seen & (doc_c[:, 0:1] == row[HEADS : HEADS + 1])
    for copy in copies[2:]:
        copy.wait()
    for h in range(HEADS):
        cols = slice(h * HD, (h + 1) * HD)
        q, k, v, g = q_ref[:, cols], k_ref[:, cols], v_ref[:, cols], g_ref[:, cols]
        spread = jnp.where(same, cum_c[:, h : h + 1] - row[h : h + 1], -1e30)
        decay = jnp.exp(spread)
        weighted_do = (decay * mm(g, v, NT)).astype(BF)
        weighted_qk = (decay * mm(q, k, NT)).astype(BF)
        incoming = jnp.concatenate([carried_ref[2 * h, 0:HALF, :], carried_ref[2 * h + 1, 0:HALF, :]], axis=0)
        adjoint = jnp.concatenate([carried_ref[2 * h, HALF:, :], carried_ref[2 * h + 1, HALF:, :]], axis=0)
        start = first_w[:, h : h + 1]
        end = end_w[:, h : h + 1]
        gq_ref[:, cols] = (mm(weighted_do, k) + start * mm(g, incoming, NT)).astype(BF)
        gk_ref[:, cols] = (mm(weighted_do, q, TN) + end * mm(v, adjoint, NT)).astype(BF)
        gv_ref[:, cols] = (mm(weighted_qk, g, TN) + end * mm(k, adjoint)).astype(BF)


def feature_block(place, offset, sibling):
    core = place[1]
    core = 1 - core if sibling else core
    return pl.multiple_of((((place[0] + offset) % RINGX) * 2 + core) * FEAT, FEAT)


ORDER = ((0, 0), (0, 1), (-1, 0), (-1, 1), (1, 0), (1, 1), (2, 0), (2, 1))
ALL = len(ORDER) * FEAT
EARLY = 6
OUT_ORDER = (2, -1, 1, 0)


def forward_kernel(from_left, from_right, x_ref, d_ref, sems):
    pairs = ((from_left.at[:, pl.ds(0, FEAT)], x_ref), (from_right.at[:, pl.ds(FEAT, FEAT)], d_ref))
    for copy in fetch(pairs, sems):
        copy.wait()


def expert_early_kernel(place, *refs):
    chunks, (wg, wu, wd) = refs[:EARLY], refs[EARLY : EARLY + 3]
    (pre, hid, cat, down_late), (xs, ds, down_w, sems) = refs[-8:-4], refs[-4:]
    stages = ([], [], [], [])
    for i, (offset, sibling) in enumerate(ORDER):
        block = feature_block(place, offset, sibling)
        side = pl.ds(i * FEAT, FEAT)
        late = i >= EARLY
        if not late:
            stages[0].append((wd.at[0, :, pl.ds(block, FEAT)], down_w.at[:, side]))
            stages[0].append((chunks[i].at[:, pl.ds(FEAT, FEAT)], ds.at[:, side]))
            stages[1].append((chunks[i].at[:, pl.ds(0, FEAT)], xs.at[:, side]))
        else:
            stages[3].append((wd.at[0, :, pl.ds(block, FEAT)], down_late.at[:, pl.ds((i - EARLY) * FEAT, FEAT)]))
        stages[3 if late else 1].append((wg.at[0, pl.ds(block, FEAT), :], cat.at[side, pl.ds(0, HID)]))
        stages[3 if late else 2].append((wu.at[0, pl.ds(block, FEAT), :], cat.at[side, pl.ds(HID, HID)]))
    copies = fetch(stages[0] + stages[1] + stages[2] + stages[3], sems)

    def ready(n):
        for _ in range(n):
            copies.pop(0).wait()

    ready(len(stages[0]))
    hid[...] = mm(ds[...], down_w[...], NT)
    ready(len(stages[1]))
    pre[:, :HID] = mm(xs[...], cat[: EARLY * FEAT, :HID])
    ready(len(stages[2]))
    pre[:, HID:] = mm(xs[...], cat[: EARLY * FEAT, HID:])
    ready(len(stages[3]))


def out_block(mid_ref, cat, offset, sibling):
    at = ORDER.index((offset, sibling)) * FEAT
    return mm(mid_ref[...], cat[at : at + FEAT, :], NT)


def expert_mid_kernel(pre, hid_ref, x0, d0, x1, d1, cat, down_late, mid_ref, far_ref):
    late = slice(EARLY * FEAT, None)
    hid = hid_ref[...] + mm(jnp.concatenate([d0[...], d1[...]], axis=1), down_late[...], NT)
    both = pre[...] + mm(jnp.concatenate([x0[...], x1[...]], axis=1), cat[late, :])
    gate, up = both[:, :HID], both[:, HID:]
    s = 1.0 / (1.0 + jnp.exp(-gate))
    mid_ref[:, :HID] = (hid * up * s * (1.0 + gate * (1.0 - s))).astype(BF)
    mid_ref[:, HID:] = (hid * gate * s).astype(BF)
    far_ref[...] = out_block(mid_ref, cat, OUT_ORDER[0], 1).astype(BF)


def expert_out_kernel(mid_ref, cat, far_ref, rest_ref):
    far_ref[...] = out_block(mid_ref, cat, OUT_ORDER[0], 0)
    for i, offset in enumerate(OUT_ORDER[1:]):
        rest_ref[i] = out_block(mid_ref, cat, offset, 1).astype(BF)


def expert_rest_kernel(mid_ref, cat, rest_ref):
    for i, offset in enumerate(OUT_ORDER[1:]):
        rest_ref[i] = out_block(mid_ref, cat, offset, 0)


def far_kernel(mine, away, right_ref, left_ref):
    right_ref[...] = (mine[:CUT] + away[:CUT].astype(F32)).astype(BF)
    left_ref[...] = (mine[CUT:] + away[CUT:].astype(F32)).astype(BF)


def near_kernel(mine, away, via_right, via_left, left_ref, right_ref, here_ref):
    left_ref[:CUT] = (mine[0, :CUT] + away[0, :CUT].astype(F32)).astype(BF)
    left_ref[CUT:] = (mine[0, CUT:] + away[0, CUT:].astype(F32) + via_left[...].astype(F32)).astype(BF)
    right_ref[:CUT] = (mine[1, :CUT] + away[1, :CUT].astype(F32) + via_right[...].astype(F32)).astype(BF)
    right_ref[CUT:] = (mine[1, CUT:] + away[1, CUT:].astype(F32)).astype(BF)
    here_ref[...] = mine[2] + away[2].astype(F32)


def local(
    queries, keys, values, out_grad, log_decay, doc_ids, moe_input, moe_cotangent, router_weights, expert_ids, w_gate, w_up, w_down
):
    S = jax.ShapeDtypeStruct
    place = jnp.stack([lax.axis_index("x"), lax.axis_index("core")]).astype(I32)
    smem = pl.BlockSpec(memory_space=pltpu.SMEM)
    block = S((ROWS, FEAT), BF)

    def ring(value, way):
        return lax.ppermute(value, "x", way)

    def swap(value):
        return lax.ppermute(value, "core", SWAP)

    rows, slots = call(
        pack_kernel,
        (S((ROWS, 2 * FEAT), BF), pltpu.HBM((2, TOK), I32)),
        [anywhere()] * 3,
        [pltpu.VMEM((2, TOK), I32)] + [pltpu.VMEM((TOK, FEAT), BF)] * 2 + [pltpu.VMEM((2, TOK), I32), pltpu.SemaphoreType.DMA((4,))],
        flops=2 * ROWS * TOK * 2 * FEAT,
        size=2 * MIB,
        limit=6,
    )(in_hbm(expert_ids.T), in_hbm(moe_input), in_hbm(moe_cotangent))
    own = lax.all_to_all(rows.reshape(CTX, CAP, 2 * FEAT), "ctx", 0, 0, tiled=True).reshape(ROWS, 2 * FEAT)
    from_left, from_right = ring(own, RIGHT), ring(own, LEFT)

    branch = [in_hbm(a) for a in (log_decay, doc_ids.reshape(1, TOK), queries, keys, values, out_grad)]
    held = [pltpu.VMEM((HEADS, TOK), F32), pltpu.VMEM((1, TOK), I32)] + [pltpu.VMEM((TOK, HEADS * HD), BF)] * 4
    held += [pltpu.SemaphoreType.DMA((6,))]
    message = call(
        state_kernel,
        S((CTX, HD + MARKS, HD), BF),
        [anywhere()] * 7,
        held,
        flops=4 * HEADS * TOK * HD * HD,
        size=3 * MIB,
        limit=8,
    )(*branch, own)
    arrived = lax.all_to_all(message, "ctx", 0, 0, tiled=True)
    from_left, from_right, arrived = lax.optimization_barrier((from_left, from_right, arrived))

    x_far, d_far = call(
        forward_kernel,
        (block, block),
        [anywhere()] * 2,
        [pltpu.SemaphoreType.DMA((2,))],
        size=2 * MIB,
        limit=4,
    )(from_left, from_right)
    x_far, d_far = ring(x_far, RIGHT), ring(d_far, LEFT)
    early = [c for a in (own, from_left, from_right) for c in (a, swap(a))]

    scanned = call(scan_kernel, S((CTX, HD, HD), BF), [vmem()], flops=MIB, size=MIB, limit=4)(arrived)
    carried = lax.all_to_all(scanned, "ctx", 0, 0, tiled=True)
    grads = call(
        attention_kernel,
        (S((TOK, HEADS * HD), BF),) * 3,
        [anywhere()] * 6 + [vmem()],
        held,
        flops=16 * HEADS * TOK * TOK * HD,
        size=4 * MIB,
        limit=12,
    )(*branch, carried)

    n = EARLY * FEAT
    pre, hid, cat, down_late = call(
        expert_early_kernel,
        (S((ROWS, 2 * HID), F32), S((ROWS, HID), F32), S((ALL, 2 * HID), BF), S((HID, ALL - n), BF)),
        [smem] + [anywhere()] * (EARLY + 4),
        [pltpu.VMEM((ROWS, n), BF)] * 2 + [pltpu.VMEM((HID, n), BF), pltpu.SemaphoreType.DMA((36,))],
        flops=6 * ROWS * HID * n,
        size=24 * MIB,
        limit=28,
    )(place, *early, *[in_hbm(w) for w in (w_gate, w_up, w_down)], scanned)
    x_far, d_far, pre = lax.optimization_barrier((x_far, d_far, pre))
    rest = (RINGX - 1, ROWS, FEAT)
    mid, away_far = call(
        expert_mid_kernel,
        (S((ROWS, 2 * HID), BF), block),
        [vmem()] * 8,
        flops=8 * ROWS * HID * 2 * FEAT,
        size=12 * MIB,
        limit=32,
    )(pre, hid, x_far, d_far, swap(x_far), swap(d_far), cat, down_late)
    away_far = swap(away_far)
    mine_far, away_rest = call(
        expert_out_kernel,
        (S((ROWS, FEAT), F32), S(rest, BF)),
        [vmem()] * 2,
        flops=4 * ROWS * HID * RINGX * FEAT,
        size=8 * MIB,
        limit=18,
    )(mid, cat)

    half = S((CUT, FEAT), BF)
    to_right, to_left = call(far_kernel, (half, half), [vmem()] * 2, size=2 * MIB, flops=MIB, limit=8)(mine_far, away_far)
    mid, away_rest, to_right, to_left = lax.optimization_barrier((mid, away_rest, to_right, to_left))
    away_rest = swap(away_rest)
    mine_rest = call(
        expert_rest_kernel,
        S(rest, F32),
        [vmem()] * 2,
        flops=3 * ROWS * HID * RINGX * FEAT,
        size=8 * MIB,
        limit=18,
    )(mid, cat)
    via_right, via_left = ring(to_right, RIGHT), ring(to_left, LEFT)
    to_left, to_right, here = call(
        near_kernel, (block, block, S((ROWS, FEAT), F32)), [vmem()] * 4, size=5 * MIB, flops=MIB, limit=16
    )(mine_rest, away_rest, via_right, via_left)
    summed = (here + ring(to_right, RIGHT).astype(F32) + ring(to_left, LEFT).astype(F32)).astype(BF)
    back = lax.all_to_all(summed.reshape(CTX, CAP, FEAT), "ctx", 0, 0, tiled=True)
    grad_moe = call(
        combine_kernel,
        S((TOK, FEAT), BF),
        [vmem()] + [anywhere()] * 2,
        [pltpu.VMEM((2, TOK), I32), pltpu.VMEM((2, TOK), F32), pltpu.SemaphoreType.DMA((2,))],
        flops=4 * ROWS * TOK * FEAT,
        size=MIB,
        limit=8,
    )(back.reshape(ROWS, FEAT), in_hbm(slots), in_hbm(router_weights.T))
    return (*grads, grad_moe)


def solution(mesh):
    fine = Mesh(mesh.devices.reshape(CTX, RINGX, 2), ("ctx", "x", "core"))
    ep = ("x", "core")
    row = P("ctx", ep)
    in_specs = (row, row, row, row, P(ep, "ctx"), P("ctx"), row, row, P("ctx", None), P("ctx", None))
    in_specs += (P("ctx", None, ep), P("ctx", None, ep), P("ctx", ep, None))
    return jax.shard_map(local, mesh=fine, in_specs=in_specs, out_specs=(row,) * 4, check_vma=False)
```

```python
import jax
import jax.numpy as jnp
from jax import lax
from jax.experimental import pallas as pl
from jax.experimental.pallas import tpu as pltpu
from jax.sharding import Mesh, PartitionSpec as P

BF = jnp.bfloat16
F32 = jnp.float32
I32 = jnp.int32
TOK = 256
HEADS = 8
HD = 128
HALF = HD // 2
CTX = 16
CAP = 40
ROWS = CTX * CAP
PART = ROWS // 2
CUT = PART // 2
FEAT = 384
HID = 640
MARKS = 16
RINGX = 4
RIGHT = [(i, (i + 1) % RINGX) for i in range(RINGX)]
LEFT = [(i, (i - 1) % RINGX) for i in range(RINGX)]
SWAP = [(0, 1), (1, 0)]
MIB = 1 << 20

NT = (((1,), (1,)), ((), ()))
TN = (((0,), (0,)), ((), ()))


def vmem():
    return pl.BlockSpec(memory_space=pltpu.VMEM)


def anywhere():
    return pl.BlockSpec(memory_space=pl.ANY)


def in_hbm(value):
    return pltpu.with_memory_space_constraint(value, pltpu.HBM)


def call(kernel, outs, ins, scratch=(), flops=0, size=0, limit=32):
    return pl.pallas_call(
        kernel,
        out_shape=outs,
        in_specs=ins,
        out_specs=jax.tree.map(lambda o: vmem() if isinstance(o, jax.ShapeDtypeStruct) else anywhere(), outs),
        scratch_shapes=scratch,
        compiler_params=pltpu.CompilerParams(vmem_limit_bytes=limit * MIB),
        cost_estimate=pl.CostEstimate(flops=flops, bytes_accessed=size, transcendentals=0),
    )


def fetch(pairs, sems):
    copies = [pltpu.make_async_copy(src, dst, sems.at[i]) for i, (src, dst) in enumerate(pairs)]
    for copy in copies:
        copy.start()
    return copies


def mm(a, b, dims=(((1,), (0,)), ((), ()))):
    return lax.dot_general(a, b, dims, preferred_element_type=F32)


def onehot(slot):
    return lax.broadcasted_iota(I32, (ROWS, TOK), 0) == slot


def slots_of(ids):
    expert = lax.broadcasted_iota(I32, (CTX, TOK), 0)
    named = [ids[k : k + 1] == expert for k in range(2)]
    hits = jnp.where(named[0] | named[1], 1.0, 0.0).astype(BF)
    before = lax.broadcasted_iota(I32, (TOK, TOK), 0) < lax.broadcasted_iota(I32, (TOK, TOK), 1)
    rank = mm(hits, jnp.where(before, 1.0, 0.0).astype(BF))
    places = [jnp.sum(jnp.where(m, rank, 0.0), axis=0, keepdims=True).astype(I32) for m in named]
    return [ids[k : k + 1] * CAP + places[k] for k in range(2)]


def pack_kernel(ids_hbm, x_hbm, d_hbm, rows_ref, slots_hbm, ids_ref, x_ref, d_ref, slots_ref, sems):
    copies = fetch(((ids_hbm, ids_ref), (x_hbm, x_ref), (d_hbm, d_ref)), sems)
    copies[0].wait()
    slots = slots_of(ids_ref[...])
    slots_ref[0:1, :], slots_ref[1:2, :] = slots
    leaving = pltpu.make_async_copy(slots_ref, slots_hbm, sems.at[3])
    leaving.start()
    pick = jnp.where(onehot(slots[0]) | onehot(slots[1]), 1.0, 0.0).astype(BF)
    copies[1].wait()
    rows_ref[:, :FEAT] = mm(pick, x_ref[...]).astype(BF)
    copies[2].wait()
    rows_ref[:, FEAT:] = mm(pick, d_ref[...]).astype(BF)
    leaving.wait()


def combine_kernel(rows_ref, slots_hbm, weights_hbm, out_ref, slots_ref, weights_ref, sems):
    for copy in fetch(((slots_hbm, slots_ref), (weights_hbm, weights_ref)), sems):
        copy.wait()
    columns = jnp.concatenate([weights_ref[...], jnp.zeros((6, TOK), F32)], axis=0).T
    total = jnp.zeros((TOK, FEAT), F32)
    for k in range(2):
        pick = jnp.where(onehot(slots_ref[k : k + 1, :]), 1.0, 0.0).astype(BF)
        total += columns[:, k : k + 1] * mm(pick, rows_ref[...], TN)
    out_ref[...] = total.astype(BF)


def sums_of_decay(decay, doc):
    upto = lax.broadcasted_iota(I32, (TOK, TOK), 0) <= lax.broadcasted_iota(I32, (TOK, TOK), 1)
    cum = lax.dot_general(
        decay,
        jnp.where(upto, 1.0, 0.0),
        (((1,), (0,)), ((), ())),
        precision=lax.Precision.HIGHEST,
        preferred_element_type=F32,
    )
    both = jnp.concatenate([cum, jnp.broadcast_to(doc.astype(F32), (HEADS, TOK))], axis=0)
    return both, both.T


def weights_of(turned):
    cum, doc = turned[:, :HEADS], turned[:, HEADS:]
    first_w = jnp.where(doc == doc[0:1], jnp.exp(cum), 0.0)
    end_w = jnp.where(doc == doc[TOK - 1 :], jnp.exp(cum[TOK - 1 :] - cum), 0.0)
    return cum, doc, first_w, end_w


def state_kernel(*refs):
    sources, out_ref, (decay_ref, doc_ref, q_ref, k_ref, v_ref, g_ref), sems = refs[:6], refs[7], refs[8:14], refs[14]
    copies = fetch(tuple(zip(sources, refs[8:14])), sems)
    copies[0].wait()
    copies[1].wait()
    _, turned = sums_of_decay(decay_ref[...], doc_ref[...])
    cum_c, doc_c, first_w, end_w = weights_of(turned)
    total, first, last = cum_c[TOK - 1 :], doc_c[0:1], doc_c[TOK - 1 :]
    line = lax.broadcasted_iota(I32, (MARKS, HD), 0)
    for copy in copies[2:]:
        copy.wait()
    for h in range(HEADS):
        cols = slice(h * HD, (h + 1) * HD)
        keys_end = (end_w[:, h : h + 1] * k_ref[:, cols].astype(F32)).astype(BF)
        queries_first = (first_w[:, h : h + 1] * q_ref[:, cols].astype(F32)).astype(BF)
        state = mm(keys_end, v_ref[:, cols], TN).astype(BF)
        adjoint = mm(queries_first, g_ref[:, cols], TN).astype(BF)
        sum_h = jnp.broadcast_to(total[:, h : h + 1], (MARKS, HD))
        high = sum_h.astype(BF).astype(F32)
        mid = (sum_h - high).astype(BF).astype(F32)
        low = sum_h - high - mid
        marks = jnp.where(line == 0, high, jnp.where(line == 1, mid, jnp.where(line == 2, low, 0.0)))
        marks = jnp.where(line == 3, first[:, h : h + 1], jnp.where(line == 4, last[:, h : h + 1], marks))
        for part in range(2):
            lines = slice(part * HALF, (part + 1) * HALF)
            out_ref[2 * h + part, 0:HALF, :] = state[lines]
            out_ref[2 * h + part, HALF:HD, :] = adjoint[lines]
            out_ref[2 * h + part, HD:, :] = marks.astype(BF)


def scan_kernel(in_ref, out_ref):
    rates, live = [], []
    prev = jnp.full((1, HD), -1.0, F32)
    for b in range(CTX):
        marks = in_ref[b, HD:, :].astype(F32)
        first, last = marks[3:4], marks[4:5]
        rates.append(jnp.where(prev == last, jnp.exp(marks[0:1] + marks[1:2] + marks[2:3]), 0.0))
        live.append(prev == first)
        prev = last
    total = jnp.zeros((HALF, HD), F32)
    for b in range(CTX):
        out_ref[b, 0:HALF, :] = jnp.where(live[b], total, 0.0).astype(BF)
        total = rates[b] * total + in_ref[b, 0:HALF, :].astype(F32)
    total = jnp.zeros((HALF, HD), F32)
    for b in reversed(range(CTX)):
        out_ref[b, HALF:, :] = total.astype(BF)
        total = rates[b] * total + jnp.where(live[b], in_ref[b, HALF:HD, :].astype(F32), 0.0)


def attention_kernel(*refs):
    sources, carried_ref, (gq_ref, gk_ref, gv_ref), (decay_ref, doc_ref, q_ref, k_ref, v_ref, g_ref), sems = (
        refs[:6], refs[6], refs[7:10], refs[10:16], refs[16]
    )
    copies = fetch(tuple(zip(sources, refs[10:16])), sems)
    copies[0].wait()
    copies[1].wait()
    row, turned = sums_of_decay(decay_ref[...], doc_ref[...])
    cum_c, doc_c, first_w, end_w = weights_of(turned)
    seen = lax.broadcasted_iota(I32, (TOK, TOK), 0) >= lax.broadcasted_iota(I32, (TOK, TOK), 1)
    same = seen & (doc_c[:, 0:1] == row[HEADS : HEADS + 1])
    for copy in copies[2:]:
        copy.wait()
    for h in range(HEADS):
        cols = slice(h * HD, (h + 1) * HD)
        q, k, v, g = q_ref[:, cols], k_ref[:, cols], v_ref[:, cols], g_ref[:, cols]
        spread = jnp.where(same, cum_c[:, h : h + 1] - row[h : h + 1], -1e30)
        decay = jnp.exp(spread)
        weighted_do = (decay * mm(g, v, NT)).astype(BF)
        weighted_qk = (decay * mm(q, k, NT)).astype(BF)
        incoming = jnp.concatenate([carried_ref[2 * h, 0:HALF, :], carried_ref[2 * h + 1, 0:HALF, :]], axis=0)
        adjoint = jnp.concatenate([carried_ref[2 * h, HALF:, :], carried_ref[2 * h + 1, HALF:, :]], axis=0)
        start = first_w[:, h : h + 1]
        end = end_w[:, h : h + 1]
        gq_ref[:, cols] = (mm(weighted_do, k) + start * mm(g, incoming, NT)).astype(BF)
        gk_ref[:, cols] = (mm(weighted_do, q, TN) + end * mm(v, adjoint, NT)).astype(BF)
        gv_ref[:, cols] = (mm(weighted_qk, g, TN) + end * mm(k, adjoint)).astype(BF)


def feature_block(place, offset, sibling):
    core = place[1]
    core = 1 - core if sibling else core
    return pl.multiple_of((((place[0] + offset) % RINGX) * 2 + core) * FEAT, FEAT)


ORDER = ((0, 0), (0, 1), (-1, 0), (-1, 1), (1, 0), (1, 1), (2, 0), (2, 1))
ALL = len(ORDER) * FEAT
OUT_ORDER = (2, -1, 1, 0)


def split_kernel(rows, first, second, sems):
    pairs = [(rows.at[pl.ds(i * PART, PART), :], out) for i, out in enumerate((first, second))]
    for copy in fetch(pairs, sems):
        copy.wait()


def lay_out(chunks, xs, ds):
    moves = []
    for i, chunk in enumerate(chunks):
        side = pl.ds(i * FEAT, FEAT)
        moves.append(((chunk.at[:, pl.ds(FEAT, FEAT)], ds.at[:, side]), (chunk.at[:, pl.ds(0, FEAT)], xs.at[:, side])))
    return moves


def middle(gate, up, hid, mid_ref):
    s = 1.0 / (1.0 + jnp.exp(-gate))
    mid_ref[:, :HID] = (hid * up * s * (1.0 + gate * (1.0 - s))).astype(BF)
    mid_ref[:, HID:] = (hid * gate * s).astype(BF)


def expert_first_kernel(place, *refs):
    chunks, (wg, wu, wd) = refs[:8], refs[8:11]
    (mid_ref, far_ref, cat, down), (xs, ds, sems) = refs[-7:-3], refs[-3:]
    stages = ([], [], [])
    moves = lay_out(chunks, xs, ds)
    for i, (offset, sibling) in enumerate(ORDER):
        block = feature_block(place, offset, sibling)
        side = pl.ds(i * FEAT, FEAT)
        stages[0].extend([(wd.at[0, :, pl.ds(block, FEAT)], down.at[:, side]), moves[i][0]])
        stages[1].extend([(wg.at[0, pl.ds(block, FEAT), :], cat.at[side, pl.ds(0, HID)]), moves[i][1]])
        stages[2].append((wu.at[0, pl.ds(block, FEAT), :], cat.at[side, pl.ds(HID, HID)]))
    copies = fetch(stages[0] + stages[1] + stages[2], sems)

    def ready(n):
        for _ in range(n):
            copies.pop(0).wait()

    ready(len(stages[0]))
    hid = mm(ds[...], down[...], NT)
    ready(len(stages[1]))
    gate = mm(xs[...], cat[:, :HID])
    ready(len(stages[2]))
    up = mm(xs[...], cat[:, HID:])
    middle(gate, up, hid, mid_ref)
    far_ref[...] = out_block(mid_ref, cat, OUT_ORDER[0], 1).astype(BF)


def expert_second_kernel(*refs):
    chunks, (cat, down, mid_ref, far_ref, xs, ds, sems) = refs[:8], refs[8:]
    moves = lay_out(chunks, xs, ds)
    copies = fetch([m[0] for m in moves] + [m[1] for m in moves], sems)
    for copy in copies[:8]:
        copy.wait()
    hid = mm(ds[...], down[...], NT)
    for copy in copies[8:]:
        copy.wait()
    both = mm(xs[...], cat[...])
    middle(both[:, :HID], both[:, HID:], hid, mid_ref)
    far_ref[...] = out_block(mid_ref, cat, OUT_ORDER[0], 1).astype(BF)


def out_block(mid_ref, cat, offset, sibling):
    at = ORDER.index((offset, sibling)) * FEAT
    return mm(mid_ref[...], cat[at : at + FEAT, :], NT)


def expert_out_kernel(mid_ref, cat, far_ref, rest_ref):
    far_ref[...] = out_block(mid_ref, cat, OUT_ORDER[0], 0)
    for i, offset in enumerate(OUT_ORDER[1:]):
        rest_ref[i] = out_block(mid_ref, cat, offset, 1).astype(BF)


def far_kernel(mine, away, right_ref, left_ref):
    right_ref[...] = (mine[:CUT] + away[:CUT].astype(F32)).astype(BF)
    left_ref[...] = (mine[CUT:] + away[CUT:].astype(F32)).astype(BF)


def near_kernel(mid_ref, cat, away, via_right, via_left, left_ref, right_ref):
    left, right = [out_block(mid_ref, cat, offset, 0) + away[i].astype(F32) for i, offset in enumerate(OUT_ORDER[1:3])]
    left_ref[:CUT] = left[:CUT].astype(BF)
    left_ref[CUT:] = (left[CUT:] + via_left[...].astype(F32)).astype(BF)
    right_ref[:CUT] = (right[:CUT] + via_right[...].astype(F32)).astype(BF)
    right_ref[CUT:] = right[CUT:].astype(BF)


def here_kernel(mid_ref, cat, away, here_ref):
    here_ref[...] = out_block(mid_ref, cat, OUT_ORDER[3], 0) + away[2].astype(F32)


def sum_kernel(here0, left0, right0, here1, left1, right1, out_ref):
    for i, (here, left, right) in enumerate(((here0, left0, right0), (here1, left1, right1))):
        total = here[...] + left[...].astype(F32) + right[...].astype(F32)
        out_ref[i * PART : (i + 1) * PART] = total.astype(BF)


def local(
    queries, keys, values, out_grad, log_decay, doc_ids, moe_input, moe_cotangent, router_weights, expert_ids, w_gate, w_up, w_down
):
    S = jax.ShapeDtypeStruct
    place = jnp.stack([lax.axis_index("x"), lax.axis_index("core")]).astype(I32)
    smem = pl.BlockSpec(memory_space=pltpu.SMEM)
    block = S((PART, FEAT), BF)
    tie = lax.optimization_barrier

    def ring(value, way):
        return lax.ppermute(value, "x", way)

    def swap(value):
        return lax.ppermute(value, "core", SWAP)

    rows, slots = call(
        pack_kernel,
        (S((ROWS, 2 * FEAT), BF), pltpu.HBM((2, TOK), I32)),
        [anywhere()] * 3,
        [pltpu.VMEM((2, TOK), I32)] + [pltpu.VMEM((TOK, FEAT), BF)] * 2 + [pltpu.VMEM((2, TOK), I32), pltpu.SemaphoreType.DMA((4,))],
        flops=2 * ROWS * TOK * 2 * FEAT,
        size=2 * MIB,
        limit=6,
    )(in_hbm(expert_ids.T), in_hbm(moe_input), in_hbm(moe_cotangent))
    own = lax.all_to_all(rows.reshape(CTX, CAP, 2 * FEAT), "ctx", 0, 0, tiled=True).reshape(ROWS, 2 * FEAT)
    halves = call(
        split_kernel,
        (S((PART, 2 * FEAT), BF),) * 2,
        [anywhere()],
        [pltpu.SemaphoreType.DMA((2,))],
        size=2 * MIB,
        limit=4,
    )(own)
    left0, right0 = ring(halves[0], RIGHT), ring(halves[0], LEFT)

    branch = [in_hbm(a) for a in (log_decay, doc_ids.reshape(1, TOK), queries, keys, values, out_grad)]
    held = [pltpu.VMEM((HEADS, TOK), F32), pltpu.VMEM((1, TOK), I32)] + [pltpu.VMEM((TOK, HEADS * HD), BF)] * 4
    held += [pltpu.SemaphoreType.DMA((6,))]
    message = call(
        state_kernel,
        S((CTX, HD + MARKS, HD), BF),
        [anywhere()] * 7,
        held,
        flops=4 * HEADS * TOK * HD * HD,
        size=3 * MIB,
        limit=8,
    )(*branch, own)
    arrived = lax.all_to_all(message, "ctx", 0, 0, tiled=True)
    left0, right0, message, own1 = tie((left0, right0, message, halves[1]))
    far0, right1 = ring(left0, RIGHT), ring(own1, LEFT)
    early0 = [c for a in (halves[0], left0, right0) for c in (a, swap(a))]
    far0, right1, arrived, own1 = tie((far0, right1, arrived, own1))
    left1, far1 = ring(own1, RIGHT), ring(right1, LEFT)

    scanned = call(scan_kernel, S((CTX, HD, HD), BF), [vmem()], flops=MIB, size=MIB, limit=4)(arrived)
    wide = S((PART, 2 * HID), BF)
    side = [pltpu.VMEM((PART, ALL), BF)] * 2
    mid0, away0, cat, down = call(
        expert_first_kernel,
        (wide, block, S((ALL, 2 * HID), BF), S((HID, ALL), BF)),
        [smem] + [anywhere()] * 12,
        side + [pltpu.SemaphoreType.DMA((5 * len(ORDER),))],
        flops=7 * PART * HID * ALL,
        size=24 * MIB,
        limit=28,
    )(place, *early0, far0, swap(far0), *[in_hbm(w) for w in (w_gate, w_up, w_down)], scanned)

    def out_sums(mid, away_far):
        mine_far, rest = call(
            expert_out_kernel,
            (S((PART, FEAT), F32), S((RINGX - 1, PART, FEAT), BF)),
            [vmem()] * 2,
            flops=4 * PART * HID * RINGX * FEAT,
            size=6 * MIB,
            limit=14,
        )(mid, cat)
        part = S((CUT, FEAT), BF)
        return call(far_kernel, (part, part), [vmem()] * 2, size=2 * MIB, flops=MIB, limit=6)(mine_far, swap(away_far)), rest

    def near_sums(mid, rest, via):
        return call(
            near_kernel,
            (block, block),
            [vmem()] * 5,
            flops=2 * PART * HID * RINGX * FEAT,
            size=8 * MIB,
            limit=14,
        )(mid, cat, rest, *via)

    def here_sum(mid, rest):
        return call(
            here_kernel,
            S((PART, FEAT), F32),
            [vmem()] * 3,
            flops=PART * HID * RINGX * FEAT,
            size=6 * MIB,
            limit=14,
        )(mid, cat, rest)

    left1, far1, away0 = tie((left1, far1, away0))
    ends0, rest0 = out_sums(mid0, away0)
    own1_s = swap(own1)
    ends0, rest0, own1 = tie((ends0, rest0, own1))
    via0 = ring(ends0[0], RIGHT), ring(ends0[1], LEFT)
    rest0 = swap(rest0)
    mid1, away1 = call(
        expert_second_kernel,
        (wide, block),
        [anywhere()] * 8 + [vmem()] * 2,
        side + [pltpu.SemaphoreType.DMA((16,))],
        flops=7 * PART * HID * ALL,
        size=20 * MIB,
        limit=28,
    )(own1, own1_s, *[c for a in (left1, right1, far1) for c in (a, swap(a))], cat, down)
    via0, rest0, mid0, mid1 = tie((via0, rest0, mid0, mid1))
    near0 = near_sums(mid0, rest0, via0)
    near0, mid0, mid1 = tie((near0, mid0, mid1))
    here0 = here_sum(mid0, rest0)
    mid1, here0 = tie((mid1, here0))
    ends1, rest1 = out_sums(mid1, away1)
    ends1, rest1, mid1 = tie((ends1, rest1, mid1))
    via1 = ring(ends1[0], RIGHT), ring(ends1[1], LEFT)
    pieces0 = here0, ring(near0[1], RIGHT), ring(near0[0], LEFT)
    via1, pieces0 = tie((via1, pieces0))
    rest1 = swap(rest1)
    near1 = near_sums(mid1, rest1, via1)
    near1, mid1 = tie((near1, mid1))
    here1 = here_sum(mid1, rest1)
    here1, scanned = tie((here1, scanned))
    pieces = *pieces0, here1, ring(near1[1], RIGHT), ring(near1[0], LEFT)
    summed = call(sum_kernel, S((ROWS, FEAT), BF), [vmem()] * 6, size=4 * MIB, flops=MIB, limit=12)(*pieces)

    carried = lax.all_to_all(scanned, "ctx", 0, 0, tiled=True)
    grads = call(
        attention_kernel,
        (S((TOK, HEADS * HD), BF),) * 3,
        [anywhere()] * 6 + [vmem()],
        held,
        flops=16 * HEADS * TOK * TOK * HD,
        size=4 * MIB,
        limit=12,
    )(*branch, carried)

    back = lax.all_to_all(summed.reshape(CTX, CAP, FEAT), "ctx", 0, 0, tiled=True)
    grad_moe = call(
        combine_kernel,
        S((TOK, FEAT), BF),
        [vmem()] + [anywhere()] * 2,
        [pltpu.VMEM((2, TOK), I32), pltpu.VMEM((2, TOK), F32), pltpu.SemaphoreType.DMA((2,))],
        flops=4 * ROWS * TOK * FEAT,
        size=MIB,
        limit=8,
    )(back.reshape(ROWS, FEAT), in_hbm(slots), in_hbm(router_weights.T))
    return (*grads, grad_moe)


def solution(mesh):
    fine = Mesh(mesh.devices.reshape(CTX, RINGX, 2), ("ctx", "x", "core"))
    ep = ("x", "core")
    row = P("ctx", ep)
    in_specs = (row, row, row, row, P(ep, "ctx"), P("ctx"), row, row, P("ctx", None), P("ctx", None))
    in_specs += (P("ctx", None, ep), P("ctx", None, ep), P("ctx", ep, None))
    return jax.shard_map(local, mesh=fine, in_specs=in_specs, out_specs=(row,) * 4, check_vma=False)
```

```python
import jax
import jax.numpy as jnp
from jax import lax
from jax.experimental import pallas as pl
from jax.experimental.pallas import tpu as pltpu
from jax.sharding import Mesh, PartitionSpec as P

BF = jnp.bfloat16
F32 = jnp.float32
I32 = jnp.int32
TOK = 256
HEADS = 8
HD = 128
HALF = HD // 2
CTX = 16
CAP = 40
ROWS = CTX * CAP
CUT = ROWS // 2
FEAT = 384
HID = 640
MARKS = 16
RINGX = 4
RIGHT = [(i, (i + 1) % RINGX) for i in range(RINGX)]
LEFT = [(i, (i - 1) % RINGX) for i in range(RINGX)]
SWAP = [(0, 1), (1, 0)]
MIB = 1 << 20

NT = (((1,), (1,)), ((), ()))
TN = (((0,), (0,)), ((), ()))


def vmem():
    return pl.BlockSpec(memory_space=pltpu.VMEM)


def anywhere():
    return pl.BlockSpec(memory_space=pl.ANY)


def in_hbm(value):
    return pltpu.with_memory_space_constraint(value, pltpu.HBM)


def call(kernel, outs, ins, scratch=(), flops=0, size=0, limit=32):
    return pl.pallas_call(
        kernel,
        out_shape=outs,
        in_specs=ins,
        out_specs=jax.tree.map(lambda o: vmem() if isinstance(o, jax.ShapeDtypeStruct) else anywhere(), outs),
        scratch_shapes=scratch,
        compiler_params=pltpu.CompilerParams(vmem_limit_bytes=limit * MIB),
        cost_estimate=pl.CostEstimate(flops=flops, bytes_accessed=size, transcendentals=0),
    )


def fetch(pairs, sems):
    copies = [pltpu.make_async_copy(src, dst, sems.at[i]) for i, (src, dst) in enumerate(pairs)]
    for copy in copies:
        copy.start()
    return copies


def mm(a, b, dims=(((1,), (0,)), ((), ()))):
    return lax.dot_general(a, b, dims, preferred_element_type=F32)


def onehot(slot):
    return lax.broadcasted_iota(I32, (ROWS, TOK), 0) == slot


def slots_of(ids):
    expert = lax.broadcasted_iota(I32, (CTX, TOK), 0)
    named = [ids[k : k + 1] == expert for k in range(2)]
    hits = jnp.where(named[0] | named[1], 1.0, 0.0).astype(BF)
    before = lax.broadcasted_iota(I32, (TOK, TOK), 0) < lax.broadcasted_iota(I32, (TOK, TOK), 1)
    rank = mm(hits, jnp.where(before, 1.0, 0.0).astype(BF))
    places = [jnp.sum(jnp.where(m, rank, 0.0), axis=0, keepdims=True).astype(I32) for m in named]
    return [ids[k : k + 1] * CAP + places[k] for k in range(2)]


def pack_kernel(ids_hbm, x_hbm, d_hbm, rows_ref, slots_hbm, ids_ref, x_ref, d_ref, slots_ref, sems):
    copies = fetch(((ids_hbm, ids_ref), (x_hbm, x_ref), (d_hbm, d_ref)), sems)
    copies[0].wait()
    slots = slots_of(ids_ref[...])
    slots_ref[0:1, :], slots_ref[1:2, :] = slots
    leaving = pltpu.make_async_copy(slots_ref, slots_hbm, sems.at[3])
    leaving.start()
    pick = jnp.where(onehot(slots[0]) | onehot(slots[1]), 1.0, 0.0).astype(BF)
    copies[1].wait()
    rows_ref[:, :FEAT] = mm(pick, x_ref[...]).astype(BF)
    copies[2].wait()
    rows_ref[:, FEAT:] = mm(pick, d_ref[...]).astype(BF)
    leaving.wait()


def combine_kernel(rows_ref, slots_hbm, weights_hbm, out_ref, slots_ref, weights_ref, sems):
    for copy in fetch(((slots_hbm, slots_ref), (weights_hbm, weights_ref)), sems):
        copy.wait()
    columns = jnp.concatenate([weights_ref[...], jnp.zeros((6, TOK), F32)], axis=0).T
    total = jnp.zeros((TOK, FEAT), F32)
    for k in range(2):
        pick = jnp.where(onehot(slots_ref[k : k + 1, :]), 1.0, 0.0).astype(BF)
        total += columns[:, k : k + 1] * mm(pick, rows_ref[...], TN)
    out_ref[...] = total.astype(BF)


def sums_of_decay(decay, doc):
    upto = lax.broadcasted_iota(I32, (TOK, TOK), 0) <= lax.broadcasted_iota(I32, (TOK, TOK), 1)
    cum = lax.dot_general(
        decay,
        jnp.where(upto, 1.0, 0.0),
        (((1,), (0,)), ((), ())),
        precision=lax.Precision.HIGHEST,
        preferred_element_type=F32,
    )
    both = jnp.concatenate([cum, jnp.broadcast_to(doc.astype(F32), (HEADS, TOK))], axis=0)
    return both, both.T


def weights_of(turned):
    cum, doc = turned[:, :HEADS], turned[:, HEADS:]
    first_w = jnp.where(doc == doc[0:1], jnp.exp(cum), 0.0)
    end_w = jnp.where(doc == doc[TOK - 1 :], jnp.exp(cum[TOK - 1 :] - cum), 0.0)
    return cum, doc, first_w, end_w


def state_kernel(*refs):
    sources, out_ref, (decay_ref, doc_ref, q_ref, k_ref, v_ref, g_ref), sems = refs[:6], refs[7], refs[8:14], refs[14]
    copies = fetch(tuple(zip(sources, refs[8:14])), sems)
    copies[0].wait()
    copies[1].wait()
    _, turned = sums_of_decay(decay_ref[...], doc_ref[...])
    cum_c, doc_c, first_w, end_w = weights_of(turned)
    total, first, last = cum_c[TOK - 1 :], doc_c[0:1], doc_c[TOK - 1 :]
    line = lax.broadcasted_iota(I32, (MARKS, HD), 0)
    for copy in copies[2:]:
        copy.wait()
    for h in range(HEADS):
        cols = slice(h * HD, (h + 1) * HD)
        keys_end = (end_w[:, h : h + 1] * k_ref[:, cols].astype(F32)).astype(BF)
        queries_first = (first_w[:, h : h + 1] * q_ref[:, cols].astype(F32)).astype(BF)
        state = mm(keys_end, v_ref[:, cols], TN).astype(BF)
        adjoint = mm(queries_first, g_ref[:, cols], TN).astype(BF)
        sum_h = jnp.broadcast_to(total[:, h : h + 1], (MARKS, HD))
        high = sum_h.astype(BF).astype(F32)
        mid = (sum_h - high).astype(BF).astype(F32)
        low = sum_h - high - mid
        marks = jnp.where(line == 0, high, jnp.where(line == 1, mid, jnp.where(line == 2, low, 0.0)))
        marks = jnp.where(line == 3, first[:, h : h + 1], jnp.where(line == 4, last[:, h : h + 1], marks))
        for part in range(2):
            lines = slice(part * HALF, (part + 1) * HALF)
            out_ref[2 * h + part, 0:HALF, :] = state[lines]
            out_ref[2 * h + part, HALF:HD, :] = adjoint[lines]
            out_ref[2 * h + part, HD:, :] = marks.astype(BF)


def scan_kernel(in_ref, out_ref):
    rates, live = [], []
    prev = jnp.full((1, HD), -1.0, F32)
    for b in range(CTX):
        marks = in_ref[b, HD:, :].astype(F32)
        first, last = marks[3:4], marks[4:5]
        rates.append(jnp.where(prev == last, jnp.exp(marks[0:1] + marks[1:2] + marks[2:3]), 0.0))
        live.append(prev == first)
        prev = last
    total = jnp.zeros((HALF, HD), F32)
    for b in range(CTX):
        out_ref[b, 0:HALF, :] = jnp.where(live[b], total, 0.0).astype(BF)
        total = rates[b] * total + in_ref[b, 0:HALF, :].astype(F32)
    total = jnp.zeros((HALF, HD), F32)
    for b in reversed(range(CTX)):
        out_ref[b, HALF:, :] = total.astype(BF)
        total = rates[b] * total + jnp.where(live[b], in_ref[b, HALF:HD, :].astype(F32), 0.0)


def attention_kernel(*refs):
    sources, carried_ref, (gq_ref, gk_ref, gv_ref), (decay_ref, doc_ref, q_ref, k_ref, v_ref, g_ref), sems = (
        refs[:6], refs[6], refs[7:10], refs[10:16], refs[16]
    )
    copies = fetch(tuple(zip(sources, refs[10:16])), sems)
    copies[0].wait()
    copies[1].wait()
    row, turned = sums_of_decay(decay_ref[...], doc_ref[...])
    cum_c, doc_c, first_w, end_w = weights_of(turned)
    seen = lax.broadcasted_iota(I32, (TOK, TOK), 0) >= lax.broadcasted_iota(I32, (TOK, TOK), 1)
    same = seen & (doc_c[:, 0:1] == row[HEADS : HEADS + 1])
    for copy in copies[2:]:
        copy.wait()
    for h in range(HEADS):
        cols = slice(h * HD, (h + 1) * HD)
        q, k, v, g = q_ref[:, cols], k_ref[:, cols], v_ref[:, cols], g_ref[:, cols]
        spread = jnp.where(same, cum_c[:, h : h + 1] - row[h : h + 1], -1e30)
        decay = jnp.exp(spread)
        weighted_do = (decay * mm(g, v, NT)).astype(BF)
        weighted_qk = (decay * mm(q, k, NT)).astype(BF)
        incoming = jnp.concatenate([carried_ref[2 * h, 0:HALF, :], carried_ref[2 * h + 1, 0:HALF, :]], axis=0)
        adjoint = jnp.concatenate([carried_ref[2 * h, HALF:, :], carried_ref[2 * h + 1, HALF:, :]], axis=0)
        start = first_w[:, h : h + 1]
        end = end_w[:, h : h + 1]
        gq_ref[:, cols] = (mm(weighted_do, k) + start * mm(g, incoming, NT)).astype(BF)
        gk_ref[:, cols] = (mm(weighted_do, q, TN) + end * mm(v, adjoint, NT)).astype(BF)
        gv_ref[:, cols] = (mm(weighted_qk, g, TN) + end * mm(k, adjoint)).astype(BF)


def feature_block(place, offset, sibling):
    core = place[1]
    core = 1 - core if sibling else core
    return pl.multiple_of((((place[0] + offset) % RINGX) * 2 + core) * FEAT, FEAT)


ORDER = ((0, 0), (0, 1), (-1, 0), (-1, 1), (1, 0), (1, 1), (2, 0), (2, 1))
ALL = len(ORDER) * FEAT
OWN, EARLY = 2, 6
OUT_ORDER = (2, -1, 1, 0)


def forward_kernel(from_left, from_right, x_ref, d_ref, sems):
    pairs = ((from_left.at[:, pl.ds(0, FEAT)], x_ref), (from_right.at[:, pl.ds(FEAT, FEAT)], d_ref))
    for copy in fetch(pairs, sems):
        copy.wait()


def first_layer(place, blocks, chunks, weights, xs, ds, gate_up, down, sems, at=0):
    wg, wu, wd = weights
    stages = ([], [], [])
    for i, (offset, sibling) in enumerate(blocks):
        block = feature_block(place, offset, sibling)
        side, turned = pl.ds(i * FEAT, FEAT), pl.ds((at + i) * FEAT, FEAT)
        stages[0].append((wd.at[0, :, pl.ds(block, FEAT)], down.at[:, side]))
        stages[0].append((chunks[i].at[:, pl.ds(FEAT, FEAT)], ds.at[:, side]))
        stages[1].append((wg.at[0, pl.ds(block, FEAT), :], gate_up.at[turned, pl.ds(0, HID)]))
        stages[1].append((chunks[i].at[:, pl.ds(0, FEAT)], xs.at[:, side]))
        stages[2].append((wu.at[0, pl.ds(block, FEAT), :], gate_up.at[turned, pl.ds(HID, HID)]))
    return stages


def expert_own_kernel(place, a0, a1, wg, wu, wd, pre_hbm, hid_hbm, xs, ds, gate_up, down, pre, hid, sems, out_sems):
    stages = first_layer(place, ORDER[:OWN], (a0, a1), (wg, wu, wd), xs, ds, gate_up, down, sems)
    copies = fetch(stages[0] + stages[1] + stages[2], sems)

    def ready(n):
        for _ in range(n):
            copies.pop(0).wait()

    ready(len(stages[0]))
    hid[...] = mm(ds[...], down[...], NT)
    leaving = [pltpu.make_async_copy(hid, hid_hbm, out_sems.at[0]), pltpu.make_async_copy(pre, pre_hbm, out_sems.at[1])]
    leaving[0].start()
    ready(len(stages[1]))
    pre[:, :HID] = mm(xs[...], gate_up[:, :HID])
    ready(len(stages[2]))
    pre[:, HID:] = mm(xs[...], gate_up[:, HID:])
    leaving[1].start()
    for copy in leaving:
        copy.wait()


def expert_early_kernel(place, *refs):
    chunks, (wg, wu, wd, pre_hbm, hid_hbm) = refs[:4], refs[4:9]
    (pre, hid, cat, down_late), (xs, ds, down_w, sums, hids, sems) = refs[-10:-6], refs[-6:]
    stages = first_layer(place, ORDER[OWN:EARLY], chunks, (wg, wu, wd), xs, ds, cat, down_w, sems, at=OWN)
    stages[0].append((hid_hbm, hids))
    stages[1].append((pre_hbm.at[:, pl.ds(0, HID)], sums.at[:, pl.ds(0, HID)]))
    stages[2].append((pre_hbm.at[:, pl.ds(HID, HID)], sums.at[:, pl.ds(HID, HID)]))
    rest = []
    for i, (offset, sibling) in enumerate(ORDER):
        block = feature_block(place, offset, sibling)
        if i >= EARLY:
            rest.append((wd.at[0, :, pl.ds(block, FEAT)], down_late.at[:, pl.ds((i - EARLY) * FEAT, FEAT)]))
        if i >= EARLY or i < OWN:
            rest.append((wg.at[0, pl.ds(block, FEAT), :], cat.at[pl.ds(i * FEAT, FEAT), pl.ds(0, HID)]))
            rest.append((wu.at[0, pl.ds(block, FEAT), :], cat.at[pl.ds(i * FEAT, FEAT), pl.ds(HID, HID)]))
    copies = fetch(stages[0] + stages[1] + stages[2] + rest, sems)

    def ready(n):
        for _ in range(n):
            copies.pop(0).wait()

    lines = slice(OWN * FEAT, EARLY * FEAT)
    ready(len(stages[0]))
    hid[...] = hids[...] + mm(ds[...], down_w[...], NT)
    ready(len(stages[1]))
    pre[:, :HID] = sums[:, :HID] + mm(xs[...], cat[lines, :HID])
    ready(len(stages[2]))
    pre[:, HID:] = sums[:, HID:] + mm(xs[...], cat[lines, HID:])
    ready(len(rest))


def out_block(mid_ref, cat, offset, sibling):
    at = ORDER.index((offset, sibling)) * FEAT
    return mm(mid_ref[...], cat[at : at + FEAT, :], NT)


def expert_mid_kernel(pre, hid_ref, x0, d0, x1, d1, cat, down_late, mid_ref, far_ref):
    late = slice(EARLY * FEAT, None)
    hid = hid_ref[...] + mm(jnp.concatenate([d0[...], d1[...]], axis=1), down_late[...], NT)
    both = pre[...] + mm(jnp.concatenate([x0[...], x1[...]], axis=1), cat[late, :])
    gate, up = both[:, :HID], both[:, HID:]
    s = 1.0 / (1.0 + jnp.exp(-gate))
    mid_ref[:, :HID] = (hid * up * s * (1.0 + gate * (1.0 - s))).astype(BF)
    mid_ref[:, HID:] = (hid * gate * s).astype(BF)
    far_ref[...] = out_block(mid_ref, cat, OUT_ORDER[0], 1).astype(BF)


def expert_out_kernel(mid_ref, cat, far_ref, rest_ref):
    far_ref[...] = out_block(mid_ref, cat, OUT_ORDER[0], 0)
    for i, offset in enumerate(OUT_ORDER[1:]):
        rest_ref[i] = out_block(mid_ref, cat, offset, 1).astype(BF)


def expert_rest_kernel(mid_ref, cat, away, left_ref, right_ref, left_sum, right_sum, here_ref):
    left, right, here = [out_block(mid_ref, cat, offset, 0) + away[i].astype(F32) for i, offset in enumerate(OUT_ORDER[1:])]
    left_ref[...] = left[:CUT].astype(BF)
    left_sum[...] = left[CUT:]
    right_sum[...] = right[:CUT]
    right_ref[...] = right[CUT:].astype(BF)
    here_ref[...] = here


def far_kernel(mine, away, right_ref, left_ref):
    right_ref[...] = (mine[:CUT] + away[:CUT].astype(F32)).astype(BF)
    left_ref[...] = (mine[CUT:] + away[CUT:].astype(F32)).astype(BF)


def near_kernel(left_sum, right_sum, via_left, via_right, left_ref, right_ref):
    left_ref[...] = (left_sum[...] + via_left[...].astype(F32)).astype(BF)
    right_ref[...] = (right_sum[...] + via_right[...].astype(F32)).astype(BF)


def sum_kernel(here, from_right_a, from_right_b, from_left_a, from_left_b, out_ref):
    top = here[:CUT] + from_right_a[...].astype(F32) + from_left_b[...].astype(F32)
    out_ref[:CUT] = top.astype(BF)
    low = here[CUT:] + from_right_b[...].astype(F32) + from_left_a[...].astype(F32)
    out_ref[CUT:] = low.astype(BF)


def local(
    queries, keys, values, out_grad, log_decay, doc_ids, moe_input, moe_cotangent, router_weights, expert_ids, w_gate, w_up, w_down
):
    S = jax.ShapeDtypeStruct
    place = jnp.stack([lax.axis_index("x"), lax.axis_index("core")]).astype(I32)
    smem = pl.BlockSpec(memory_space=pltpu.SMEM)
    block = S((ROWS, FEAT), BF)
    tie = lax.optimization_barrier

    def ring(value, way):
        return lax.ppermute(value, "x", way)

    def swap(value):
        return lax.ppermute(value, "core", SWAP)

    rows, slots = call(
        pack_kernel,
        (S((ROWS, 2 * FEAT), BF), pltpu.HBM((2, TOK), I32)),
        [anywhere()] * 3,
        [pltpu.VMEM((2, TOK), I32)] + [pltpu.VMEM((TOK, FEAT), BF)] * 2 + [pltpu.VMEM((2, TOK), I32), pltpu.SemaphoreType.DMA((4,))],
        flops=2 * ROWS * TOK * 2 * FEAT,
        size=2 * MIB,
        limit=6,
    )(in_hbm(expert_ids.T), in_hbm(moe_input), in_hbm(moe_cotangent))
    own = lax.all_to_all(rows.reshape(CTX, CAP, 2 * FEAT), "ctx", 0, 0, tiled=True).reshape(ROWS, 2 * FEAT)
    from_left, from_right = ring(own, RIGHT), ring(own, LEFT)

    branch = [in_hbm(a) for a in (log_decay, doc_ids.reshape(1, TOK), queries, keys, values, out_grad)]
    held = [pltpu.VMEM((HEADS, TOK), F32), pltpu.VMEM((1, TOK), I32)] + [pltpu.VMEM((TOK, HEADS * HD), BF)] * 4
    held += [pltpu.SemaphoreType.DMA((6,))]
    message = call(
        state_kernel,
        S((CTX, HD + MARKS, HD), BF),
        [anywhere()] * 7,
        held,
        flops=4 * HEADS * TOK * HD * HD,
        size=3 * MIB,
        limit=8,
    )(*branch, own)
    arrived = lax.all_to_all(message, "ctx", 0, 0, tiled=True)
    weights = [in_hbm(w) for w in (w_gate, w_up, w_down)]
    own_s = swap(own)
    n = OWN * FEAT
    pre, hid = call(
        expert_own_kernel,
        (pltpu.HBM((ROWS, 2 * HID), F32), pltpu.HBM((ROWS, HID), F32)),
        [smem] + [anywhere()] * 5,
        [pltpu.VMEM((ROWS, n), BF)] * 2
        + [pltpu.VMEM((n, 2 * HID), BF), pltpu.VMEM((HID, n), BF), pltpu.VMEM((ROWS, 2 * HID), F32), pltpu.VMEM((ROWS, HID), F32)]
        + [pltpu.SemaphoreType.DMA((5 * OWN,)), pltpu.SemaphoreType.DMA((2,))],
        flops=6 * ROWS * HID * n,
        size=12 * MIB,
        limit=20,
    )(place, own, own_s, *weights)
    from_left, from_right, arrived, pre = tie((from_left, from_right, arrived, pre))

    x_far, d_far = call(
        forward_kernel,
        (block, block),
        [anywhere()] * 2,
        [pltpu.SemaphoreType.DMA((2,))],
        size=2 * MIB,
        limit=4,
    )(from_left, from_right)
    x_far, d_far = ring(x_far, RIGHT), ring(d_far, LEFT)
    early = [c for a in (from_left, from_right) for c in (a, swap(a))]

    scanned = call(scan_kernel, S((CTX, HD, HD), BF), [vmem()], flops=MIB, size=MIB, limit=4)(arrived)
    n = (EARLY - OWN) * FEAT
    pre, hid, cat, down_late = call(
        expert_early_kernel,
        (S((ROWS, 2 * HID), F32), S((ROWS, HID), F32), S((ALL, 2 * HID), BF), S((HID, ALL - EARLY * FEAT), BF)),
        [smem] + [anywhere()] * 10,
        [pltpu.VMEM((ROWS, n), BF)] * 2
        + [pltpu.VMEM((HID, n), BF), pltpu.VMEM((ROWS, 2 * HID), F32), pltpu.VMEM((ROWS, HID), F32)]
        + [pltpu.SemaphoreType.DMA((34,))],
        flops=6 * ROWS * HID * n,
        size=24 * MIB,
        limit=32,
    )(place, *early, *weights, in_hbm(pre), in_hbm(hid), scanned)
    x_far, d_far, pre = tie((x_far, d_far, pre))
    rest = (RINGX - 1, ROWS, FEAT)
    mid, away_far = call(
        expert_mid_kernel,
        (S((ROWS, 2 * HID), BF), block),
        [vmem()] * 8,
        flops=8 * ROWS * HID * 2 * FEAT,
        size=12 * MIB,
        limit=32,
    )(pre, hid, x_far, d_far, swap(x_far), swap(d_far), cat, down_late)
    away_far = swap(away_far)
    mine_far, away_rest = call(
        expert_out_kernel,
        (S((ROWS, FEAT), F32), S(rest, BF)),
        [vmem()] * 2,
        flops=4 * ROWS * HID * RINGX * FEAT,
        size=8 * MIB,
        limit=18,
    )(mid, cat)

    half = S((CUT, FEAT), BF)
    to_right, to_left = call(far_kernel, (half, half), [vmem()] * 2, size=2 * MIB, flops=MIB, limit=8)(mine_far, away_far)
    mid, away_rest, to_right, to_left = tie((mid, away_rest, to_right, to_left))
    away_rest = swap(away_rest)
    wide = S((CUT, FEAT), F32)
    left_a, right_a, left_sum, right_sum, here = call(
        expert_rest_kernel,
        (half, half, wide, wide, S((ROWS, FEAT), F32)),
        [vmem()] * 3,
        flops=3 * ROWS * HID * RINGX * FEAT,
        size=8 * MIB,
        limit=20,
    )(mid, cat, away_rest)
    via_right, via_left = ring(to_right, RIGHT), ring(to_left, LEFT)
    left_a, right_a = ring(left_a, LEFT), ring(right_a, RIGHT)
    here, scanned = tie((here, scanned))
    via_right, via_left, left_a, right_a = tie((via_right, via_left, left_a, right_a))
    left_b, right_b = call(near_kernel, (half, half), [vmem()] * 4, limit=6)(left_sum, right_sum, via_left, via_right)
    left_b, right_b = ring(left_b, LEFT), ring(right_b, RIGHT)
    summed = call(sum_kernel, block, [vmem()] * 5, size=4 * MIB, flops=MIB, limit=8)(here, left_a, left_b, right_a, right_b)
    carried = lax.all_to_all(scanned, "ctx", 0, 0, tiled=True)
    grads = call(
        attention_kernel,
        (S((TOK, HEADS * HD), BF),) * 3,
        [anywhere()] * 6 + [vmem()],
        held,
        flops=16 * HEADS * TOK * TOK * HD,
        size=4 * MIB,
        limit=12,
    )(*branch, carried)

    back = lax.all_to_all(summed.reshape(CTX, CAP, FEAT), "ctx", 0, 0, tiled=True)
    grad_moe = call(
        combine_kernel,
        S((TOK, FEAT), BF),
        [vmem()] + [anywhere()] * 2,
        [pltpu.VMEM((2, TOK), I32), pltpu.VMEM((2, TOK), F32), pltpu.SemaphoreType.DMA((2,))],
        flops=4 * ROWS * TOK * FEAT,
        size=MIB,
        limit=8,
    )(back.reshape(ROWS, FEAT), in_hbm(slots), in_hbm(router_weights.T))
    return (*grads, grad_moe)


def solution(mesh):
    fine = Mesh(mesh.devices.reshape(CTX, RINGX, 2), ("ctx", "x", "core"))
    ep = ("x", "core")
    row = P("ctx", ep)
    in_specs = (row, row, row, row, P(ep, "ctx"), P("ctx"), row, row, P("ctx", None), P("ctx", None))
    in_specs += (P("ctx", None, ep), P("ctx", None, ep), P("ctx", ep, None))
    return jax.shard_map(local, mesh=fine, in_specs=in_specs, out_specs=(row,) * 4, check_vma=False)
```

```python
import jax
import jax.numpy as jnp
from jax import lax
from jax.experimental import pallas as pl
from jax.experimental.pallas import tpu as pltpu
from jax.sharding import Mesh, PartitionSpec as P

BF = jnp.bfloat16
F32 = jnp.float32
I32 = jnp.int32
TOK = 256
HEADS = 8
HD = 128
HALF = HD // 2
CTX = 16
CAP = 40
ROWS = CTX * CAP
CUT = ROWS // 2
FEAT = 384
HID = 640
MARKS = 16
RINGX = 4
RIGHT = [(i, (i + 1) % RINGX) for i in range(RINGX)]
LEFT = [(i, (i - 1) % RINGX) for i in range(RINGX)]
SWAP = [(0, 1), (1, 0)]
MIB = 1 << 20

NT = (((1,), (1,)), ((), ()))
TN = (((0,), (0,)), ((), ()))


def vmem():
    return pl.BlockSpec(memory_space=pltpu.VMEM)


def anywhere():
    return pl.BlockSpec(memory_space=pl.ANY)


def in_hbm(value):
    return pltpu.with_memory_space_constraint(value, pltpu.HBM)


def call(kernel, outs, ins, scratch=(), flops=0, size=0, limit=32):
    return pl.pallas_call(
        kernel,
        out_shape=outs,
        in_specs=ins,
        out_specs=jax.tree.map(lambda o: vmem() if isinstance(o, jax.ShapeDtypeStruct) else anywhere(), outs),
        scratch_shapes=scratch,
        compiler_params=pltpu.CompilerParams(vmem_limit_bytes=limit * MIB),
        cost_estimate=pl.CostEstimate(flops=flops, bytes_accessed=size, transcendentals=0),
    )


def fetch(pairs, sems):
    copies = [pltpu.make_async_copy(src, dst, sems.at[i]) for i, (src, dst) in enumerate(pairs)]
    for copy in copies:
        copy.start()
    return copies


def mm(a, b, dims=(((1,), (0,)), ((), ()))):
    return lax.dot_general(a, b, dims, preferred_element_type=F32)


def onehot(slot):
    return lax.broadcasted_iota(I32, (ROWS, TOK), 0) == slot


def slots_of(ids):
    expert = lax.broadcasted_iota(I32, (CTX, TOK), 0)
    named = [ids[k : k + 1] == expert for k in range(2)]
    hits = jnp.where(named[0] | named[1], 1.0, 0.0).astype(BF)
    before = lax.broadcasted_iota(I32, (TOK, TOK), 0) < lax.broadcasted_iota(I32, (TOK, TOK), 1)
    rank = mm(hits, jnp.where(before, 1.0, 0.0).astype(BF))
    places = [jnp.sum(jnp.where(m, rank, 0.0), axis=0, keepdims=True).astype(I32) for m in named]
    return [ids[k : k + 1] * CAP + places[k] for k in range(2)]


def pack_kernel(ids_hbm, x_hbm, d_hbm, rows_ref, slots_hbm, ids_ref, x_ref, d_ref, slots_ref, sems):
    copies = fetch(((ids_hbm, ids_ref), (x_hbm, x_ref), (d_hbm, d_ref)), sems)
    copies[0].wait()
    slots = slots_of(ids_ref[...])
    slots_ref[0:1, :], slots_ref[1:2, :] = slots
    leaving = pltpu.make_async_copy(slots_ref, slots_hbm, sems.at[3])
    leaving.start()
    pick = jnp.where(onehot(slots[0]) | onehot(slots[1]), 1.0, 0.0).astype(BF)
    copies[1].wait()
    rows_ref[:, :FEAT] = mm(pick, x_ref[...]).astype(BF)
    copies[2].wait()
    rows_ref[:, FEAT:] = mm(pick, d_ref[...]).astype(BF)
    leaving.wait()


def combine_kernel(rows_ref, slots_hbm, weights_hbm, out_ref, slots_ref, weights_ref, sems):
    for copy in fetch(((slots_hbm, slots_ref), (weights_hbm, weights_ref)), sems):
        copy.wait()
    lines = [weights_ref[...], slots_ref[...].astype(F32), jnp.zeros((4, TOK), F32)]
    columns = jnp.concatenate(lines, axis=0).T
    slot = lax.broadcasted_iota(I32, (TOK, ROWS), 1)
    total = jnp.zeros((TOK, FEAT), F32)
    for k in range(2):
        pick = jnp.where(slot == columns[:, 2 + k : 3 + k].astype(I32), 1.0, 0.0).astype(BF)
        total += columns[:, k : k + 1] * mm(pick, rows_ref[...])
    out_ref[...] = total.astype(BF)


def sums_of_decay(decay, doc):
    upto = lax.broadcasted_iota(I32, (TOK, TOK), 0) <= lax.broadcasted_iota(I32, (TOK, TOK), 1)
    cum = lax.dot_general(
        decay,
        jnp.where(upto, 1.0, 0.0),
        (((1,), (0,)), ((), ())),
        precision=lax.Precision.HIGHEST,
        preferred_element_type=F32,
    )
    both = jnp.concatenate([cum, jnp.broadcast_to(doc.astype(F32), (HEADS, TOK))], axis=0)
    return both, both.T


def weights_of(turned):
    cum, doc = turned[:, :HEADS], turned[:, HEADS:]
    first_w = jnp.where(doc == doc[0:1], jnp.exp(cum), 0.0)
    end_w = jnp.where(doc == doc[TOK - 1 :], jnp.exp(cum[TOK - 1 :] - cum), 0.0)
    return cum, doc, first_w, end_w


def state_kernel(*refs):
    sources, out_ref, (decay_ref, doc_ref, q_ref, k_ref, v_ref, g_ref), sems = refs[:6], refs[7], refs[8:14], refs[14]
    copies = fetch(tuple(zip(sources, refs[8:14])), sems)
    copies[0].wait()
    copies[1].wait()
    _, turned = sums_of_decay(decay_ref[...], doc_ref[...])
    cum_c, doc_c, first_w, end_w = weights_of(turned)
    total, first, last = cum_c[TOK - 1 :], doc_c[0:1], doc_c[TOK - 1 :]
    line = lax.broadcasted_iota(I32, (MARKS, HD), 0)
    for copy in copies[2:]:
        copy.wait()
    for h in range(HEADS):
        cols = slice(h * HD, (h + 1) * HD)
        keys_end = (end_w[:, h : h + 1] * k_ref[:, cols].astype(F32)).astype(BF)
        queries_first = (first_w[:, h : h + 1] * q_ref[:, cols].astype(F32)).astype(BF)
        state = mm(keys_end, v_ref[:, cols], TN).astype(BF)
        adjoint = mm(queries_first, g_ref[:, cols], TN).astype(BF)
        sum_h = jnp.broadcast_to(total[:, h : h + 1], (MARKS, HD))
        high = sum_h.astype(BF).astype(F32)
        mid = (sum_h - high).astype(BF).astype(F32)
        low = sum_h - high - mid
        marks = jnp.where(line == 0, high, jnp.where(line == 1, mid, jnp.where(line == 2, low, 0.0)))
        marks = jnp.where(line == 3, first[:, h : h + 1], jnp.where(line == 4, last[:, h : h + 1], marks))
        for part in range(2):
            lines = slice(part * HALF, (part + 1) * HALF)
            out_ref[2 * h + part, 0:HALF, :] = state[lines]
            out_ref[2 * h + part, HALF:HD, :] = adjoint[lines]
            out_ref[2 * h + part, HD:, :] = marks.astype(BF)


def scan_kernel(in_ref, out_ref):
    rates, live = [], []
    prev = jnp.full((1, HD), -1.0, F32)
    for b in range(CTX):
        marks = in_ref[b, HD:, :].astype(F32)
        first, last = marks[3:4], marks[4:5]
        rates.append(jnp.where(prev == last, jnp.exp(marks[0:1] + marks[1:2] + marks[2:3]), 0.0))
        live.append(prev == first)
        prev = last
    total = jnp.zeros((HALF, HD), F32)
    for b in range(CTX):
        out_ref[b, 0:HALF, :] = jnp.where(live[b], total, 0.0).astype(BF)
        total = rates[b] * total + in_ref[b, 0:HALF, :].astype(F32)
    total = jnp.zeros((HALF, HD), F32)
    for b in reversed(range(CTX)):
        out_ref[b, HALF:, :] = total.astype(BF)
        total = rates[b] * total + jnp.where(live[b], in_ref[b, HALF:HD, :].astype(F32), 0.0)


def attention_kernel(*refs):
    sources, carried_ref, (gq_ref, gk_ref, gv_ref), (decay_ref, doc_ref, q_ref, k_ref, v_ref, g_ref), sems = (
        refs[:6], refs[6], refs[7:10], refs[10:16], refs[16]
    )
    copies = fetch(tuple(zip(sources, refs[10:16])), sems)
    copies[0].wait()
    copies[1].wait()
    row, turned = sums_of_decay(decay_ref[...], doc_ref[...])
    cum_c, doc_c, first_w, end_w = weights_of(turned)
    seen = lax.broadcasted_iota(I32, (TOK, TOK), 0) >= lax.broadcasted_iota(I32, (TOK, TOK), 1)
    same = seen & (doc_c[:, 0:1] == row[HEADS : HEADS + 1])
    for copy in copies[2:]:
        copy.wait()
    for h in range(HEADS):
        cols = slice(h * HD, (h + 1) * HD)
        q, k, v, g = q_ref[:, cols], k_ref[:, cols], v_ref[:, cols], g_ref[:, cols]
        spread = jnp.where(same, cum_c[:, h : h + 1] - row[h : h + 1], -1e30)
        decay = jnp.exp(spread)
        weighted_do = (decay * mm(g, v, NT)).astype(BF)
        weighted_qk = (decay * mm(q, k, NT)).astype(BF)
        incoming = jnp.concatenate([carried_ref[2 * h, 0:HALF, :], carried_ref[2 * h + 1, 0:HALF, :]], axis=0)
        adjoint = jnp.concatenate([carried_ref[2 * h, HALF:, :], carried_ref[2 * h + 1, HALF:, :]], axis=0)
        start = first_w[:, h : h + 1]
        end = end_w[:, h : h + 1]
        gq_ref[:, cols] = (mm(weighted_do, k) + start * mm(g, incoming, NT)).astype(BF)
        gk_ref[:, cols] = (mm(weighted_do, q, TN) + end * mm(v, adjoint, NT)).astype(BF)
        gv_ref[:, cols] = (mm(weighted_qk, g, TN) + end * mm(k, adjoint)).astype(BF)


def feature_block(place, offset, sibling):
    core = place[1]
    core = 1 - core if sibling else core
    return pl.multiple_of((((place[0] + offset) % RINGX) * 2 + core) * FEAT, FEAT)


ORDER = ((0, 0), (0, 1), (-1, 0), (-1, 1), (1, 0), (1, 1), (2, 0), (2, 1))
ALL = len(ORDER) * FEAT
OWN, EARLY = 2, 6
OUT_ORDER = (2, -1, 1, 0)


def split_kernel(rows, x_ref, d_ref, sems):
    for copy in fetch(((rows.at[:, pl.ds(0, FEAT)], x_ref), (rows.at[:, pl.ds(FEAT, FEAT)], d_ref)), sems):
        copy.wait()


def first_layer(place, blocks, chunks, weights, xs, ds, gate_up, down, sems, at=0):
    wg, wu, wd = weights
    stages = ([], [], [])
    for i, (offset, sibling) in enumerate(blocks):
        block = feature_block(place, offset, sibling)
        side, turned = pl.ds(i * FEAT, FEAT), pl.ds((at + i) * FEAT, FEAT)
        stages[0].append((wd.at[0, :, pl.ds(block, FEAT)], down.at[:, side]))
        stages[0].append((chunks[i][1], ds.at[:, side]))
        stages[1].append((wg.at[0, pl.ds(block, FEAT), :], gate_up.at[turned, pl.ds(0, HID)]))
        stages[1].append((chunks[i][0], xs.at[:, side]))
        stages[2].append((wu.at[0, pl.ds(block, FEAT), :], gate_up.at[turned, pl.ds(HID, HID)]))
    return stages


def expert_own_kernel(place, x0, d0, x1, d1, wg, wu, wd, pre_hbm, hid_hbm, xs, ds, gate_up, down, pre, hid, sems, out_sems):
    stages = first_layer(place, ORDER[:OWN], ((x0, d0), (x1, d1)), (wg, wu, wd), xs, ds, gate_up, down, sems)
    copies = fetch(stages[0] + stages[1] + stages[2], sems)

    def ready(n):
        for _ in range(n):
            copies.pop(0).wait()

    ready(len(stages[0]))
    hid[...] = mm(ds[...], down[...], NT)
    leaving = [pltpu.make_async_copy(hid, hid_hbm, out_sems.at[0]), pltpu.make_async_copy(pre, pre_hbm, out_sems.at[1])]
    leaving[0].start()
    ready(len(stages[1]))
    pre[:, :HID] = mm(xs[...], gate_up[:, :HID])
    ready(len(stages[2]))
    pre[:, HID:] = mm(xs[...], gate_up[:, HID:])
    leaving[1].start()
    for copy in leaving:
        copy.wait()


def expert_early_kernel(place, *refs):
    chunks, (wg, wu, wd, pre_hbm, hid_hbm) = list(zip(refs[0:8:2], refs[1:8:2])), refs[8:13]
    (pre, hid, cat, down_late), (xs, ds, down_w, sums, hids, sems) = refs[-10:-6], refs[-6:]
    stages = first_layer(place, ORDER[OWN:EARLY], chunks, (wg, wu, wd), xs, ds, cat, down_w, sems, at=OWN)
    stages[0].append((hid_hbm, hids))
    stages[1].append((pre_hbm.at[:, pl.ds(0, HID)], sums.at[:, pl.ds(0, HID)]))
    stages[2].append((pre_hbm.at[:, pl.ds(HID, HID)], sums.at[:, pl.ds(HID, HID)]))
    rest = []
    for i, (offset, sibling) in enumerate(ORDER):
        block = feature_block(place, offset, sibling)
        if i >= EARLY:
            rest.append((wd.at[0, :, pl.ds(block, FEAT)], down_late.at[:, pl.ds((i - EARLY) * FEAT, FEAT)]))
        if i >= EARLY or i < OWN:
            rest.append((wg.at[0, pl.ds(block, FEAT), :], cat.at[pl.ds(i * FEAT, FEAT), pl.ds(0, HID)]))
            rest.append((wu.at[0, pl.ds(block, FEAT), :], cat.at[pl.ds(i * FEAT, FEAT), pl.ds(HID, HID)]))
    copies = fetch(stages[0] + stages[1] + stages[2] + rest, sems)

    def ready(n):
        for _ in range(n):
            copies.pop(0).wait()

    lines = slice(OWN * FEAT, EARLY * FEAT)
    ready(len(stages[0]))
    hid[...] = hids[...] + mm(ds[...], down_w[...], NT)
    ready(len(stages[1]))
    pre[:, :HID] = sums[:, :HID] + mm(xs[...], cat[lines, :HID])
    ready(len(stages[2]))
    pre[:, HID:] = sums[:, HID:] + mm(xs[...], cat[lines, HID:])
    ready(len(rest))


def out_block(mid_ref, cat, offset, sibling):
    at = ORDER.index((offset, sibling)) * FEAT
    return mm(mid_ref[...], cat[at : at + FEAT, :], NT)


def expert_mid_kernel(pre, hid_ref, x0, d0, x1, d1, cat, down_late, mid_ref, far_ref):
    late = slice(EARLY * FEAT, None)
    hid = hid_ref[...] + mm(jnp.concatenate([d0[...], d1[...]], axis=1), down_late[...], NT)
    both = pre[...] + mm(jnp.concatenate([x0[...], x1[...]], axis=1), cat[late, :])
    gate, up = both[:, :HID], both[:, HID:]
    s = 1.0 / (1.0 + jnp.exp(-gate))
    mid_ref[:, :HID] = (hid * up * s * (1.0 + gate * (1.0 - s))).astype(BF)
    mid_ref[:, HID:] = (hid * gate * s).astype(BF)
    far_ref[...] = out_block(mid_ref, cat, OUT_ORDER[0], 1).astype(BF)


def expert_out_kernel(mid_ref, cat, far_ref, rest_ref):
    far_ref[...] = out_block(mid_ref, cat, OUT_ORDER[0], 0)
    for i, offset in enumerate(OUT_ORDER[1:]):
        rest_ref[i] = out_block(mid_ref, cat, offset, 1).astype(BF)


def expert_rest_kernel(mid_ref, cat, rest_ref):
    for i, offset in enumerate(OUT_ORDER[1:]):
        rest_ref[i] = out_block(mid_ref, cat, offset, 0)


def far_kernel(mine, away, right_ref, left_ref):
    right_ref[...] = (mine[:CUT] + away[:CUT].astype(F32)).astype(BF)
    left_ref[...] = (mine[CUT:] + away[CUT:].astype(F32)).astype(BF)


def near_kernel(mine, away, via_right, via_left, left_ref, right_ref, here_ref):
    left_ref[:CUT] = (mine[0, :CUT] + away[0, :CUT].astype(F32)).astype(BF)
    left_ref[CUT:] = (mine[0, CUT:] + away[0, CUT:].astype(F32) + via_left[...].astype(F32)).astype(BF)
    right_ref[:CUT] = (mine[1, :CUT] + away[1, :CUT].astype(F32) + via_right[...].astype(F32)).astype(BF)
    right_ref[CUT:] = (mine[1, CUT:] + away[1, CUT:].astype(F32)).astype(BF)
    here_ref[...] = mine[2] + away[2].astype(F32)


def local(
    queries, keys, values, out_grad, log_decay, doc_ids, moe_input, moe_cotangent, router_weights, expert_ids, w_gate, w_up, w_down
):
    S = jax.ShapeDtypeStruct
    place = jnp.stack([lax.axis_index("x"), lax.axis_index("core")]).astype(I32)
    smem = pl.BlockSpec(memory_space=pltpu.SMEM)
    block = S((ROWS, FEAT), BF)
    tie = lax.optimization_barrier

    def ring(value, way):
        return lax.ppermute(value, "x", way)

    def swap(value):
        return lax.ppermute(value, "core", SWAP)

    rows, slots = call(
        pack_kernel,
        (S((ROWS, 2 * FEAT), BF), pltpu.HBM((2, TOK), I32)),
        [anywhere()] * 3,
        [pltpu.VMEM((2, TOK), I32)] + [pltpu.VMEM((TOK, FEAT), BF)] * 2 + [pltpu.VMEM((2, TOK), I32), pltpu.SemaphoreType.DMA((4,))],
        flops=2 * ROWS * TOK * 2 * FEAT,
        size=2 * MIB,
        limit=6,
    )(in_hbm(expert_ids.T), in_hbm(moe_input), in_hbm(moe_cotangent))
    own = lax.all_to_all(rows.reshape(CTX, CAP, 2 * FEAT), "ctx", 0, 0, tiled=True).reshape(ROWS, 2 * FEAT)
    x_own, d_own = call(
        split_kernel, (block, block), [anywhere()], [pltpu.SemaphoreType.DMA((2,))], size=2 * MIB, limit=4
    )(own)
    x_left, d_right = ring(x_own, RIGHT), ring(d_own, LEFT)

    branch = [in_hbm(a) for a in (log_decay, doc_ids.reshape(1, TOK), queries, keys, values, out_grad)]
    held = [pltpu.VMEM((HEADS, TOK), F32), pltpu.VMEM((1, TOK), I32)] + [pltpu.VMEM((TOK, HEADS * HD), BF)] * 4
    held += [pltpu.SemaphoreType.DMA((6,))]
    message = call(
        state_kernel,
        S((CTX, HD + MARKS, HD), BF),
        [anywhere()] * 7,
        held,
        flops=4 * HEADS * TOK * HD * HD,
        size=3 * MIB,
        limit=8,
    )(*branch, own)
    d_next, x_next, message = tie((d_own, x_own, message))
    d_left, x_right = ring(d_next, RIGHT), ring(x_next, LEFT)
    arrived = lax.all_to_all(message, "ctx", 0, 0, tiled=True)
    weights = [in_hbm(w) for w in (w_gate, w_up, w_down)]
    n = OWN * FEAT
    pre, hid = call(
        expert_own_kernel,
        (pltpu.HBM((ROWS, 2 * HID), F32), pltpu.HBM((ROWS, HID), F32)),
        [smem] + [anywhere()] * 7,
        [pltpu.VMEM((ROWS, n), BF)] * 2
        + [pltpu.VMEM((n, 2 * HID), BF), pltpu.VMEM((HID, n), BF), pltpu.VMEM((ROWS, 2 * HID), F32), pltpu.VMEM((ROWS, HID), F32)]
        + [pltpu.SemaphoreType.DMA((5 * OWN,)), pltpu.SemaphoreType.DMA((2,))],
        flops=6 * ROWS * HID * n,
        size=12 * MIB,
        limit=20,
    )(place, x_own, d_own, swap(x_own), swap(d_own), *weights)
    x_left, d_right, pre = tie((x_left, d_right, pre))
    x_far, d_far = ring(x_left, RIGHT), ring(d_right, LEFT)
    d_left, x_right, arrived = tie((d_left, x_right, arrived))
    early = [c for x, d in ((x_left, d_left), (x_right, d_right)) for c in (x, d, swap(x), swap(d))]

    scanned = call(scan_kernel, S((CTX, HD, HD), BF), [vmem()], flops=MIB, size=MIB, limit=4)(arrived)
    n = (EARLY - OWN) * FEAT
    pre, hid, cat, down_late = call(
        expert_early_kernel,
        (S((ROWS, 2 * HID), F32), S((ROWS, HID), F32), S((ALL, 2 * HID), BF), S((HID, ALL - EARLY * FEAT), BF)),
        [smem] + [anywhere()] * 14,
        [pltpu.VMEM((ROWS, n), BF)] * 2
        + [pltpu.VMEM((HID, n), BF), pltpu.VMEM((ROWS, 2 * HID), F32), pltpu.VMEM((ROWS, HID), F32)]
        + [pltpu.SemaphoreType.DMA((34,))],
        flops=6 * ROWS * HID * n,
        size=24 * MIB,
        limit=32,
    )(place, *early, *weights, in_hbm(pre), in_hbm(hid), scanned)
    x_far, d_far, pre = tie((x_far, d_far, pre))
    rest = (RINGX - 1, ROWS, FEAT)
    mid, away_far = call(
        expert_mid_kernel,
        (S((ROWS, 2 * HID), BF), block),
        [vmem()] * 8,
        flops=8 * ROWS * HID * 2 * FEAT,
        size=12 * MIB,
        limit=32,
    )(pre, hid, x_far, d_far, swap(x_far), swap(d_far), cat, down_late)
    away_far = swap(away_far)
    mine_far, away_rest = call(
        expert_out_kernel,
        (S((ROWS, FEAT), F32), S(rest, BF)),
        [vmem()] * 2,
        flops=4 * ROWS * HID * RINGX * FEAT,
        size=8 * MIB,
        limit=18,
    )(mid, cat)

    half = S((CUT, FEAT), BF)
    to_right, to_left = call(far_kernel, (half, half), [vmem()] * 2, size=2 * MIB, flops=MIB, limit=8)(mine_far, away_far)
    mid, away_rest, to_right, to_left = tie((mid, away_rest, to_right, to_left))
    away_rest = swap(away_rest)
    mine_rest = call(
        expert_rest_kernel,
        S(rest, F32),
        [vmem()] * 2,
        flops=3 * ROWS * HID * RINGX * FEAT,
        size=8 * MIB,
        limit=18,
    )(mid, cat)
    via_right, via_left = ring(to_right, RIGHT), ring(to_left, LEFT)
    to_left, to_right, here = call(
        near_kernel, (block, block, S((ROWS, FEAT), F32)), [vmem()] * 4, size=5 * MIB, flops=MIB, limit=16
    )(mine_rest, away_rest, via_right, via_left)
    summed = (here + ring(to_right, RIGHT).astype(F32) + ring(to_left, LEFT).astype(F32)).astype(BF)
    carried = lax.all_to_all(scanned, "ctx", 0, 0, tiled=True)
    grads = call(
        attention_kernel,
        (S((TOK, HEADS * HD), BF),) * 3,
        [anywhere()] * 6 + [vmem()],
        held,
        flops=16 * HEADS * TOK * TOK * HD,
        size=4 * MIB,
        limit=12,
    )(*branch, carried)

    back = lax.all_to_all(summed.reshape(CTX, CAP, FEAT), "ctx", 0, 0, tiled=True)
    grad_moe = call(
        combine_kernel,
        S((TOK, FEAT), BF),
        [vmem()] + [anywhere()] * 2,
        [pltpu.VMEM((2, TOK), I32), pltpu.VMEM((2, TOK), F32), pltpu.SemaphoreType.DMA((2,))],
        flops=4 * ROWS * TOK * FEAT,
        size=MIB,
        limit=8,
    )(back.reshape(ROWS, FEAT), in_hbm(slots), in_hbm(router_weights.T))
    return (*grads, grad_moe)


def solution(mesh):
    fine = Mesh(mesh.devices.reshape(CTX, RINGX, 2), ("ctx", "x", "core"))
    ep = ("x", "core")
    row = P("ctx", ep)
    in_specs = (row, row, row, row, P(ep, "ctx"), P("ctx"), row, row, P("ctx", None), P("ctx", None))
    in_specs += (P("ctx", None, ep), P("ctx", None, ep), P("ctx", ep, None))
    return jax.shard_map(local, mesh=fine, in_specs=in_specs, out_specs=(row,) * 4, check_vma=False)
```

```python
import jax
import jax.numpy as jnp
from jax import lax
from jax.experimental import pallas as pl
from jax.experimental.pallas import tpu as pltpu
from jax.sharding import Mesh, PartitionSpec as P

BF = jnp.bfloat16
F32 = jnp.float32
I32 = jnp.int32
TOK = 256
HEADS = 8
HD = 128
HALF = HD // 2
CTX = 16
CAP = 40
ROWS = CTX * CAP
CUT = ROWS // 2
FEAT = 384
HID = 640
MARKS = 16
RINGX = 4
RIGHT = [(i, (i + 1) % RINGX) for i in range(RINGX)]
LEFT = [(i, (i - 1) % RINGX) for i in range(RINGX)]
SWAP = [(0, 1), (1, 0)]
MIB = 1 << 20

NT = (((1,), (1,)), ((), ()))
TN = (((0,), (0,)), ((), ()))


def vmem():
    return pl.BlockSpec(memory_space=pltpu.VMEM)


def anywhere():
    return pl.BlockSpec(memory_space=pl.ANY)


def in_hbm(value):
    return pltpu.with_memory_space_constraint(value, pltpu.HBM)


def call(kernel, outs, ins, scratch=(), flops=0, size=0, limit=32):
    return pl.pallas_call(
        kernel,
        out_shape=outs,
        in_specs=ins,
        out_specs=jax.tree.map(lambda o: vmem() if isinstance(o, jax.ShapeDtypeStruct) else anywhere(), outs),
        scratch_shapes=scratch,
        compiler_params=pltpu.CompilerParams(vmem_limit_bytes=limit * MIB),
        cost_estimate=pl.CostEstimate(flops=flops, bytes_accessed=size, transcendentals=0),
    )


def fetch(pairs, sems):
    copies = [pltpu.make_async_copy(src, dst, sems.at[i]) for i, (src, dst) in enumerate(pairs)]
    for copy in copies:
        copy.start()
    return copies


def mm(a, b, dims=(((1,), (0,)), ((), ()))):
    return lax.dot_general(a, b, dims, preferred_element_type=F32)


def onehot(slot):
    return lax.broadcasted_iota(I32, (ROWS, TOK), 0) == slot


def slots_of(ids):
    expert = lax.broadcasted_iota(I32, (CTX, TOK), 0)
    named = [ids[k : k + 1] == expert for k in range(2)]
    hits = jnp.where(named[0] | named[1], 1.0, 0.0).astype(BF)
    before = lax.broadcasted_iota(I32, (TOK, TOK), 0) < lax.broadcasted_iota(I32, (TOK, TOK), 1)
    rank = mm(hits, jnp.where(before, 1.0, 0.0).astype(BF))
    places = [jnp.sum(jnp.where(m, rank, 0.0), axis=0, keepdims=True).astype(I32) for m in named]
    return [ids[k : k + 1] * CAP + places[k] for k in range(2)]


def pack_kernel(ids_hbm, x_hbm, d_hbm, rows_ref, slots_hbm, ids_ref, x_ref, d_ref, slots_ref, sems):
    copies = fetch(((ids_hbm, ids_ref), (x_hbm, x_ref), (d_hbm, d_ref)), sems)
    copies[0].wait()
    slots = slots_of(ids_ref[...])
    slots_ref[0:1, :], slots_ref[1:2, :] = slots
    leaving = pltpu.make_async_copy(slots_ref, slots_hbm, sems.at[3])
    leaving.start()
    pick = jnp.where(onehot(slots[0]) | onehot(slots[1]), 1.0, 0.0).astype(BF)
    copies[1].wait()
    rows_ref[:, :FEAT] = mm(pick, x_ref[...]).astype(BF)
    copies[2].wait()
    rows_ref[:, FEAT:] = mm(pick, d_ref[...]).astype(BF)
    leaving.wait()


def combine_kernel(rows_ref, slots_ref, weights_ref, out_ref):
    columns = jnp.concatenate([weights_ref[...], jnp.zeros((6, TOK), F32)], axis=0).T
    total = jnp.zeros((TOK, FEAT), F32)
    for k in range(2):
        pick = jnp.where(onehot(slots_ref[k : k + 1, :]), 1.0, 0.0).astype(BF)
        total += columns[:, k : k + 1] * mm(pick, rows_ref[...], TN)
    out_ref[...] = total.astype(BF)


def sums_of_decay(decay, doc):
    upto = lax.broadcasted_iota(I32, (TOK, TOK), 0) <= lax.broadcasted_iota(I32, (TOK, TOK), 1)
    cum = lax.dot_general(
        decay,
        jnp.where(upto, 1.0, 0.0),
        (((1,), (0,)), ((), ())),
        precision=lax.Precision.HIGHEST,
        preferred_element_type=F32,
    )
    both = jnp.concatenate([cum, jnp.broadcast_to(doc.astype(F32), (HEADS, TOK))], axis=0)
    return both, both.T


def weights_of(turned):
    cum, doc = turned[:, :HEADS], turned[:, HEADS:]
    first_w = jnp.where(doc == doc[0:1], jnp.exp(cum), 0.0)
    end_w = jnp.where(doc == doc[TOK - 1 :], jnp.exp(cum[TOK - 1 :] - cum), 0.0)
    return cum, doc, first_w, end_w


def state_kernel(*refs):
    sources, out_ref, (decay_ref, doc_ref, q_ref, k_ref, v_ref, g_ref), sems = refs[:6], refs[7], refs[8:14], refs[14]
    copies = fetch(tuple(zip(sources, refs[8:14])), sems)
    copies[0].wait()
    copies[1].wait()
    _, turned = sums_of_decay(decay_ref[...], doc_ref[...])
    cum_c, doc_c, first_w, end_w = weights_of(turned)
    total, first, last = cum_c[TOK - 1 :], doc_c[0:1], doc_c[TOK - 1 :]
    line = lax.broadcasted_iota(I32, (MARKS, HD), 0)
    for copy in copies[2:]:
        copy.wait()
    for h in range(HEADS):
        cols = slice(h * HD, (h + 1) * HD)
        keys_end = (end_w[:, h : h + 1] * k_ref[:, cols].astype(F32)).astype(BF)
        queries_first = (first_w[:, h : h + 1] * q_ref[:, cols].astype(F32)).astype(BF)
        state = mm(keys_end, v_ref[:, cols], TN).astype(BF)
        adjoint = mm(queries_first, g_ref[:, cols], TN).astype(BF)
        sum_h = jnp.broadcast_to(total[:, h : h + 1], (MARKS, HD))
        high = sum_h.astype(BF).astype(F32)
        mid = (sum_h - high).astype(BF).astype(F32)
        low = sum_h - high - mid
        marks = jnp.where(line == 0, high, jnp.where(line == 1, mid, jnp.where(line == 2, low, 0.0)))
        marks = jnp.where(line == 3, first[:, h : h + 1], jnp.where(line == 4, last[:, h : h + 1], marks))
        for part in range(2):
            lines = slice(part * HALF, (part + 1) * HALF)
            out_ref[2 * h + part, 0:HALF, :] = state[lines]
            out_ref[2 * h + part, HALF:HD, :] = adjoint[lines]
            out_ref[2 * h + part, HD:, :] = marks.astype(BF)


def scan_kernel(in_ref, out_ref):
    rates, live = [], []
    prev = jnp.full((1, HD), -1.0, F32)
    for b in range(CTX):
        marks = in_ref[b, HD:, :].astype(F32)
        first, last = marks[3:4], marks[4:5]
        rates.append(jnp.where(prev == last, jnp.exp(marks[0:1] + marks[1:2] + marks[2:3]), 0.0))
        live.append(prev == first)
        prev = last
    total = jnp.zeros((HALF, HD), F32)
    for b in range(CTX):
        out_ref[b, 0:HALF, :] = jnp.where(live[b], total, 0.0).astype(BF)
        total = rates[b] * total + in_ref[b, 0:HALF, :].astype(F32)
    total = jnp.zeros((HALF, HD), F32)
    for b in reversed(range(CTX)):
        out_ref[b, HALF:, :] = total.astype(BF)
        total = rates[b] * total + jnp.where(live[b], in_ref[b, HALF:HD, :].astype(F32), 0.0)


def attention_kernel(*refs):
    sources, carried_ref, (gq_ref, gk_ref, gv_ref), (decay_ref, doc_ref, q_ref, k_ref, v_ref, g_ref), sems = (
        refs[:6], refs[6], refs[7:10], refs[10:16], refs[16]
    )
    copies = fetch(tuple(zip(sources, refs[10:16])), sems)
    copies[0].wait()
    copies[1].wait()
    row, turned = sums_of_decay(decay_ref[...], doc_ref[...])
    cum_c, doc_c, first_w, end_w = weights_of(turned)
    seen = lax.broadcasted_iota(I32, (TOK, TOK), 0) >= lax.broadcasted_iota(I32, (TOK, TOK), 1)
    same = seen & (doc_c[:, 0:1] == row[HEADS : HEADS + 1])
    for copy in copies[2:]:
        copy.wait()
    for h in range(HEADS):
        cols = slice(h * HD, (h + 1) * HD)
        q, k, v, g = q_ref[:, cols], k_ref[:, cols], v_ref[:, cols], g_ref[:, cols]
        spread = jnp.where(same, cum_c[:, h : h + 1] - row[h : h + 1], -1e30)
        decay = jnp.exp(spread)
        weighted_do = (decay * mm(g, v, NT)).astype(BF)
        weighted_qk = (decay * mm(q, k, NT)).astype(BF)
        incoming = jnp.concatenate([carried_ref[2 * h, 0:HALF, :], carried_ref[2 * h + 1, 0:HALF, :]], axis=0)
        adjoint = jnp.concatenate([carried_ref[2 * h, HALF:, :], carried_ref[2 * h + 1, HALF:, :]], axis=0)
        start = first_w[:, h : h + 1]
        end = end_w[:, h : h + 1]
        gq_ref[:, cols] = (mm(weighted_do, k) + start * mm(g, incoming, NT)).astype(BF)
        gk_ref[:, cols] = (mm(weighted_do, q, TN) + end * mm(v, adjoint, NT)).astype(BF)
        gv_ref[:, cols] = (mm(weighted_qk, g, TN) + end * mm(k, adjoint)).astype(BF)


def feature_block(place, offset, sibling):
    core = place[1]
    core = 1 - core if sibling else core
    return pl.multiple_of((((place[0] + offset) % RINGX) * 2 + core) * FEAT, FEAT)


ORDER = ((0, 0), (0, 1), (-1, 0), (-1, 1), (1, 0), (1, 1), (2, 0), (2, 1))
ALL = len(ORDER) * FEAT
OWN, EARLY = 2, 6
OUT_ORDER = (2, -1, 1, 0)


def forward_kernel(from_left, from_right, x_ref, d_ref, sems):
    pairs = ((from_left.at[:, pl.ds(0, FEAT)], x_ref), (from_right.at[:, pl.ds(FEAT, FEAT)], d_ref))
    for copy in fetch(pairs, sems):
        copy.wait()


def first_layer(place, blocks, chunks, weights, xs, ds, gate_up, down, sems, at=0):
    wg, wu, wd = weights
    stages = ([], [], [])
    for i, (offset, sibling) in enumerate(blocks):
        block = feature_block(place, offset, sibling)
        side, turned = pl.ds(i * FEAT, FEAT), pl.ds((at + i) * FEAT, FEAT)
        stages[0].append((wd.at[0, :, pl.ds(block, FEAT)], down.at[:, side]))
        stages[0].append((chunks[i].at[:, pl.ds(FEAT, FEAT)], ds.at[:, side]))
        stages[1].append((wg.at[0, pl.ds(block, FEAT), :], gate_up.at[turned, pl.ds(0, HID)]))
        stages[1].append((chunks[i].at[:, pl.ds(0, FEAT)], xs.at[:, side]))
        stages[2].append((wu.at[0, pl.ds(block, FEAT), :], gate_up.at[turned, pl.ds(HID, HID)]))
    return stages


def expert_own_kernel(place, a0, a1, wg, wu, wd, pre_hbm, hid_hbm, xs, ds, gate_up, down, pre, hid, sems, out_sems):
    stages = first_layer(place, ORDER[:OWN], (a0, a1), (wg, wu, wd), xs, ds, gate_up, down, sems)
    copies = fetch(stages[0] + stages[1] + stages[2], sems)

    def ready(n):
        for _ in range(n):
            copies.pop(0).wait()

    ready(len(stages[0]))
    hid[...] = mm(ds[...], down[...], NT)
    leaving = [pltpu.make_async_copy(hid, hid_hbm, out_sems.at[0]), pltpu.make_async_copy(pre, pre_hbm, out_sems.at[1])]
    leaving[0].start()
    ready(len(stages[1]))
    pre[:, :HID] = mm(xs[...], gate_up[:, :HID])
    ready(len(stages[2]))
    pre[:, HID:] = mm(xs[...], gate_up[:, HID:])
    leaving[1].start()
    for copy in leaving:
        copy.wait()


def expert_early_kernel(place, *refs):
    chunks, (wg, wu, wd, pre_hbm, hid_hbm) = refs[:4], refs[4:9]
    (pre, hid, cat, down_late), (xs, ds, down_w, sums, hids, sems) = refs[-10:-6], refs[-6:]
    stages = first_layer(place, ORDER[OWN:EARLY], chunks, (wg, wu, wd), xs, ds, cat, down_w, sems, at=OWN)
    stages[0].append((hid_hbm, hids))
    stages[1].append((pre_hbm.at[:, pl.ds(0, HID)], sums.at[:, pl.ds(0, HID)]))
    stages[2].append((pre_hbm.at[:, pl.ds(HID, HID)], sums.at[:, pl.ds(HID, HID)]))
    rest = []
    for i, (offset, sibling) in enumerate(ORDER):
        block = feature_block(place, offset, sibling)
        if i >= EARLY:
            rest.append((wd.at[0, :, pl.ds(block, FEAT)], down_late.at[:, pl.ds((i - EARLY) * FEAT, FEAT)]))
        if i >= EARLY or i < OWN:
            rest.append((wg.at[0, pl.ds(block, FEAT), :], cat.at[pl.ds(i * FEAT, FEAT), pl.ds(0, HID)]))
            rest.append((wu.at[0, pl.ds(block, FEAT), :], cat.at[pl.ds(i * FEAT, FEAT), pl.ds(HID, HID)]))
    copies = fetch(stages[0] + stages[1] + stages[2] + rest, sems)

    def ready(n):
        for _ in range(n):
            copies.pop(0).wait()

    lines = slice(OWN * FEAT, EARLY * FEAT)
    ready(len(stages[0]))
    hid[...] = hids[...] + mm(ds[...], down_w[...], NT)
    ready(len(stages[1]))
    pre[:, :HID] = sums[:, :HID] + mm(xs[...], cat[lines, :HID])
    ready(len(stages[2]))
    pre[:, HID:] = sums[:, HID:] + mm(xs[...], cat[lines, HID:])
    ready(len(rest))


def out_block(mid_ref, cat, offset, sibling):
    at = ORDER.index((offset, sibling)) * FEAT
    return mm(mid_ref[...], cat[at : at + FEAT, :], NT)


def expert_mid_kernel(pre, hid_ref, x0, d0, x1, d1, cat, down_late, mid_ref, far_ref):
    late = slice(EARLY * FEAT, None)
    hid = hid_ref[...] + mm(jnp.concatenate([d0[...], d1[...]], axis=1), down_late[...], NT)
    both = pre[...] + mm(jnp.concatenate([x0[...], x1[...]], axis=1), cat[late, :])
    gate, up = both[:, :HID], both[:, HID:]
    s = 1.0 / (1.0 + jnp.exp(-gate))
    mid_ref[:, :HID] = (hid * up * s * (1.0 + gate * (1.0 - s))).astype(BF)
    mid_ref[:, HID:] = (hid * gate * s).astype(BF)
    far_ref[...] = out_block(mid_ref, cat, OUT_ORDER[0], 1).astype(BF)


def expert_out_kernel(mid_ref, cat, far_ref, rest_ref):
    far_ref[...] = out_block(mid_ref, cat, OUT_ORDER[0], 0)
    for i, offset in enumerate(OUT_ORDER[1:]):
        rest_ref[i] = out_block(mid_ref, cat, offset, 1).astype(BF)


def expert_rest_kernel(mid_ref, cat, rest_ref):
    for i, offset in enumerate(OUT_ORDER[1:]):
        rest_ref[i] = out_block(mid_ref, cat, offset, 0)


def far_kernel(mine, away, right_ref, left_ref):
    right_ref[...] = (mine[:CUT] + away[:CUT].astype(F32)).astype(BF)
    left_ref[...] = (mine[CUT:] + away[CUT:].astype(F32)).astype(BF)


def near_kernel(mine, away, via_right, via_left, left_ref, right_ref, here_ref):
    left_ref[:CUT] = (mine[0, :CUT] + away[0, :CUT].astype(F32)).astype(BF)
    left_ref[CUT:] = (mine[0, CUT:] + away[0, CUT:].astype(F32) + via_left[...].astype(F32)).astype(BF)
    right_ref[:CUT] = (mine[1, :CUT] + away[1, :CUT].astype(F32) + via_right[...].astype(F32)).astype(BF)
    right_ref[CUT:] = (mine[1, CUT:] + away[1, CUT:].astype(F32)).astype(BF)
    here_ref[...] = mine[2] + away[2].astype(F32)


def local(
    queries, keys, values, out_grad, log_decay, doc_ids, moe_input, moe_cotangent, router_weights, expert_ids, w_gate, w_up, w_down
):
    S = jax.ShapeDtypeStruct
    place = jnp.stack([lax.axis_index("x"), lax.axis_index("core")]).astype(I32)
    smem = pl.BlockSpec(memory_space=pltpu.SMEM)
    block = S((ROWS, FEAT), BF)
    tie = lax.optimization_barrier

    def ring(value, way):
        return lax.ppermute(value, "x", way)

    def swap(value):
        return lax.ppermute(value, "core", SWAP)

    rows, slots = call(
        pack_kernel,
        (S((ROWS, 2 * FEAT), BF), pltpu.HBM((2, TOK), I32)),
        [anywhere()] * 3,
        [pltpu.VMEM((2, TOK), I32)] + [pltpu.VMEM((TOK, FEAT), BF)] * 2 + [pltpu.VMEM((2, TOK), I32), pltpu.SemaphoreType.DMA((4,))],
        flops=2 * ROWS * TOK * 2 * FEAT,
        size=2 * MIB,
        limit=6,
    )(in_hbm(expert_ids.T), in_hbm(moe_input), in_hbm(moe_cotangent))
    own = lax.all_to_all(rows.reshape(CTX, CAP, 2 * FEAT), "ctx", 0, 0, tiled=True).reshape(ROWS, 2 * FEAT)
    from_left, from_right = ring(own, RIGHT), ring(own, LEFT)

    branch = [in_hbm(a) for a in (log_decay, doc_ids.reshape(1, TOK), queries, keys, values, out_grad)]
    held = [pltpu.VMEM((HEADS, TOK), F32), pltpu.VMEM((1, TOK), I32)] + [pltpu.VMEM((TOK, HEADS * HD), BF)] * 4
    held += [pltpu.SemaphoreType.DMA((6,))]
    message = call(
        state_kernel,
        S((CTX, HD + MARKS, HD), BF),
        [anywhere()] * 7,
        held,
        flops=4 * HEADS * TOK * HD * HD,
        size=3 * MIB,
        limit=8,
    )(*branch, own)
    arrived = lax.all_to_all(message, "ctx", 0, 0, tiled=True)
    weights = [in_hbm(w) for w in (w_gate, w_up, w_down)]
    own_s = swap(own)
    n = OWN * FEAT
    pre, hid = call(
        expert_own_kernel,
        (pltpu.HBM((ROWS, 2 * HID), F32), pltpu.HBM((ROWS, HID), F32)),
        [smem] + [anywhere()] * 5,
        [pltpu.VMEM((ROWS, n), BF)] * 2
        + [pltpu.VMEM((n, 2 * HID), BF), pltpu.VMEM((HID, n), BF), pltpu.VMEM((ROWS, 2 * HID), F32), pltpu.VMEM((ROWS, HID), F32)]
        + [pltpu.SemaphoreType.DMA((5 * OWN,)), pltpu.SemaphoreType.DMA((2,))],
        flops=6 * ROWS * HID * n,
        size=12 * MIB,
        limit=20,
    )(place, own, own_s, *weights)
    from_left, from_right, arrived, pre = tie((from_left, from_right, arrived, pre))

    x_far, d_far = call(
        forward_kernel,
        (block, block),
        [anywhere()] * 2,
        [pltpu.SemaphoreType.DMA((2,))],
        size=2 * MIB,
        limit=4,
    )(from_left, from_right)
    x_far, d_far = ring(x_far, RIGHT), ring(d_far, LEFT)
    early = [c for a in (from_left, from_right) for c in (a, swap(a))]

    scanned = call(scan_kernel, S((CTX, HD, HD), BF), [vmem()], flops=MIB, size=MIB, limit=4)(arrived)
    n = (EARLY - OWN) * FEAT
    pre, hid, cat, down_late = call(
        expert_early_kernel,
        (S((ROWS, 2 * HID), F32), S((ROWS, HID), F32), S((ALL, 2 * HID), BF), S((HID, ALL - EARLY * FEAT), BF)),
        [smem] + [anywhere()] * 10,
        [pltpu.VMEM((ROWS, n), BF)] * 2
        + [pltpu.VMEM((HID, n), BF), pltpu.VMEM((ROWS, 2 * HID), F32), pltpu.VMEM((ROWS, HID), F32)]
        + [pltpu.SemaphoreType.DMA((34,))],
        flops=6 * ROWS * HID * n,
        size=24 * MIB,
        limit=32,
    )(place, *early, *weights, in_hbm(pre), in_hbm(hid), scanned)
    x_far, d_far, pre = tie((x_far, d_far, pre))
    rest = (RINGX - 1, ROWS, FEAT)
    mid, away_far = call(
        expert_mid_kernel,
        (S((ROWS, 2 * HID), BF), block),
        [vmem()] * 8,
        flops=8 * ROWS * HID * 2 * FEAT,
        size=12 * MIB,
        limit=32,
    )(pre, hid, x_far, d_far, swap(x_far), swap(d_far), cat, down_late)
    away_far = swap(away_far)
    mine_far, away_rest = call(
        expert_out_kernel,
        (S((ROWS, FEAT), F32), S(rest, BF)),
        [vmem()] * 2,
        flops=4 * ROWS * HID * RINGX * FEAT,
        size=8 * MIB,
        limit=18,
    )(mid, cat)

    half = S((CUT, FEAT), BF)
    to_right, to_left = call(far_kernel, (half, half), [vmem()] * 2, size=2 * MIB, flops=MIB, limit=8)(mine_far, away_far)
    mid, away_rest, to_right, to_left = tie((mid, away_rest, to_right, to_left))
    away_rest = swap(away_rest)
    mine_rest = call(
        expert_rest_kernel,
        S(rest, F32),
        [vmem()] * 2,
        flops=3 * ROWS * HID * RINGX * FEAT,
        size=8 * MIB,
        limit=18,
    )(mid, cat)
    mine_rest, scanned = tie((mine_rest, scanned))
    via_right, via_left = ring(to_right, RIGHT), ring(to_left, LEFT)
    to_left, to_right, here = call(
        near_kernel, (block, block, S((ROWS, FEAT), F32)), [vmem()] * 4, size=5 * MIB, flops=MIB, limit=16
    )(mine_rest, away_rest, via_right, via_left)
    summed = (here + ring(to_right, RIGHT).astype(F32) + ring(to_left, LEFT).astype(F32)).astype(BF)
    carried = lax.all_to_all(scanned, "ctx", 0, 0, tiled=True)
    grads = call(
        attention_kernel,
        (S((TOK, HEADS * HD), BF),) * 3,
        [anywhere()] * 6 + [vmem()],
        held,
        flops=16 * HEADS * TOK * TOK * HD,
        size=4 * MIB,
        limit=12,
    )(*branch, carried)

    back = lax.all_to_all(summed.reshape(CTX, CAP, FEAT), "ctx", 0, 0, tiled=True)
    grad_moe = call(
        combine_kernel,
        S((TOK, FEAT), BF),
        [vmem()] * 3,
        flops=4 * ROWS * TOK * FEAT,
        size=MIB,
        limit=8,
    )(back.reshape(ROWS, FEAT), slots, router_weights.T)
    return (*grads, grad_moe)


def solution(mesh):
    fine = Mesh(mesh.devices.reshape(CTX, RINGX, 2), ("ctx", "x", "core"))
    ep = ("x", "core")
    row = P("ctx", ep)
    in_specs = (row, row, row, row, P(ep, "ctx"), P("ctx"), row, row, P("ctx", None), P("ctx", None))
    in_specs += (P("ctx", None, ep), P("ctx", None, ep), P("ctx", ep, None))
    return jax.shard_map(local, mesh=fine, in_specs=in_specs, out_specs=(row,) * 4, check_vma=False)
```

```python
import jax
import jax.numpy as jnp
from jax import lax
from jax.experimental import pallas as pl
from jax.experimental.pallas import tpu as pltpu
from jax.sharding import Mesh, PartitionSpec as P

BF = jnp.bfloat16
F32 = jnp.float32
I32 = jnp.int32
TOK = 256
HEADS = 8
HD = 128
HALF = HD // 2
CTX = 16
CAP = 40
ROWS = CTX * CAP
CUT = ROWS // 2
FEAT = 384
HID = 640
MARKS = 16
RINGX = 4
RIGHT = [(i, (i + 1) % RINGX) for i in range(RINGX)]
LEFT = [(i, (i - 1) % RINGX) for i in range(RINGX)]
SWAP = [(0, 1), (1, 0)]
MIB = 1 << 20

NT = (((1,), (1,)), ((), ()))
TN = (((0,), (0,)), ((), ()))


def vmem():
    return pl.BlockSpec(memory_space=pltpu.VMEM)


def anywhere():
    return pl.BlockSpec(memory_space=pl.ANY)


def in_hbm(value):
    return pltpu.with_memory_space_constraint(value, pltpu.HBM)


def call(kernel, outs, ins, scratch=(), flops=0, size=0, limit=32):
    return pl.pallas_call(
        kernel,
        out_shape=outs,
        in_specs=ins,
        out_specs=jax.tree.map(lambda o: vmem() if isinstance(o, jax.ShapeDtypeStruct) else anywhere(), outs),
        scratch_shapes=scratch,
        compiler_params=pltpu.CompilerParams(vmem_limit_bytes=limit * MIB),
        cost_estimate=pl.CostEstimate(flops=flops, bytes_accessed=size, transcendentals=0),
    )


def fetch(pairs, sems):
    copies = [pltpu.make_async_copy(src, dst, sems.at[i]) for i, (src, dst) in enumerate(pairs)]
    for copy in copies:
        copy.start()
    return copies


def mm(a, b, dims=(((1,), (0,)), ((), ()))):
    return lax.dot_general(a, b, dims, preferred_element_type=F32)


def onehot(slot):
    return lax.broadcasted_iota(I32, (ROWS, TOK), 0) == slot


def slots_of(ids):
    expert = lax.broadcasted_iota(I32, (CTX, TOK), 0)
    named = [ids[k : k + 1] == expert for k in range(2)]
    hits = jnp.where(named[0] | named[1], 1.0, 0.0).astype(BF)
    before = lax.broadcasted_iota(I32, (TOK, TOK), 0) < lax.broadcasted_iota(I32, (TOK, TOK), 1)
    rank = mm(hits, jnp.where(before, 1.0, 0.0).astype(BF))
    places = [jnp.sum(jnp.where(m, rank, 0.0), axis=0, keepdims=True).astype(I32) for m in named]
    return [ids[k : k + 1] * CAP + places[k] for k in range(2)]


def pack_kernel(ids_hbm, x_hbm, d_hbm, rows_ref, slots_hbm, ids_ref, x_ref, d_ref, slots_ref, sems):
    copies = fetch(((ids_hbm, ids_ref), (x_hbm, x_ref), (d_hbm, d_ref)), sems)
    copies[0].wait()
    slots = slots_of(ids_ref[...])
    slots_ref[0:1, :], slots_ref[1:2, :] = slots
    leaving = pltpu.make_async_copy(slots_ref, slots_hbm, sems.at[3])
    leaving.start()
    pick = jnp.where(onehot(slots[0]) | onehot(slots[1]), 1.0, 0.0).astype(BF)
    copies[1].wait()
    rows_ref[:, :FEAT] = mm(pick, x_ref[...]).astype(BF)
    copies[2].wait()
    rows_ref[:, FEAT:] = mm(pick, d_ref[...]).astype(BF)
    leaving.wait()


def combine_kernel(rows_ref, slots_ref, weights_ref, out_ref):
    columns = jnp.concatenate([weights_ref[...], jnp.zeros((6, TOK), F32)], axis=0).T
    total = jnp.zeros((TOK, FEAT), F32)
    for k in range(2):
        pick = jnp.where(onehot(slots_ref[k : k + 1, :]), 1.0, 0.0).astype(BF)
        total += columns[:, k : k + 1] * mm(pick, rows_ref[...], TN)
    out_ref[...] = total.astype(BF)


def sums_of_decay(decay, doc):
    upto = lax.broadcasted_iota(I32, (TOK, TOK), 0) <= lax.broadcasted_iota(I32, (TOK, TOK), 1)
    cum = lax.dot_general(
        decay,
        jnp.where(upto, 1.0, 0.0),
        (((1,), (0,)), ((), ())),
        precision=lax.Precision.HIGHEST,
        preferred_element_type=F32,
    )
    both = jnp.concatenate([cum, jnp.broadcast_to(doc.astype(F32), (HEADS, TOK))], axis=0)
    return both, both.T


def weights_of(turned):
    cum, doc = turned[:, :HEADS], turned[:, HEADS:]
    first_w = jnp.where(doc == doc[0:1], jnp.exp(cum), 0.0)
    end_w = jnp.where(doc == doc[TOK - 1 :], jnp.exp(cum[TOK - 1 :] - cum), 0.0)
    return cum, doc, first_w, end_w


def state_kernel(*refs):
    sources, out_ref, (decay_ref, doc_ref, q_ref, k_ref, v_ref, g_ref), sems = refs[:6], refs[7], refs[8:14], refs[14]
    copies = fetch(tuple(zip(sources, refs[8:14])), sems)
    copies[0].wait()
    copies[1].wait()
    _, turned = sums_of_decay(decay_ref[...], doc_ref[...])
    cum_c, doc_c, first_w, end_w = weights_of(turned)
    total, first, last = cum_c[TOK - 1 :], doc_c[0:1], doc_c[TOK - 1 :]
    line = lax.broadcasted_iota(I32, (MARKS, HD), 0)
    for copy in copies[2:]:
        copy.wait()
    for h in range(HEADS):
        cols = slice(h * HD, (h + 1) * HD)
        keys_end = (end_w[:, h : h + 1] * k_ref[:, cols].astype(F32)).astype(BF)
        queries_first = (first_w[:, h : h + 1] * q_ref[:, cols].astype(F32)).astype(BF)
        state = mm(keys_end, v_ref[:, cols], TN).astype(BF)
        adjoint = mm(queries_first, g_ref[:, cols], TN).astype(BF)
        sum_h = jnp.broadcast_to(total[:, h : h + 1], (MARKS, HD))
        high = sum_h.astype(BF).astype(F32)
        mid = (sum_h - high).astype(BF).astype(F32)
        low = sum_h - high - mid
        marks = jnp.where(line == 0, high, jnp.where(line == 1, mid, jnp.where(line == 2, low, 0.0)))
        marks = jnp.where(line == 3, first[:, h : h + 1], jnp.where(line == 4, last[:, h : h + 1], marks))
        for part in range(2):
            lines = slice(part * HALF, (part + 1) * HALF)
            out_ref[2 * h + part, 0:HALF, :] = state[lines]
            out_ref[2 * h + part, HALF:HD, :] = adjoint[lines]
            out_ref[2 * h + part, HD:, :] = marks.astype(BF)


def scan_kernel(in_ref, out_ref):
    rates, live = [], []
    prev = jnp.full((1, HD), -1.0, F32)
    for b in range(CTX):
        marks = in_ref[b, HD:, :].astype(F32)
        first, last = marks[3:4], marks[4:5]
        rates.append(jnp.where(prev == last, jnp.exp(marks[0:1] + marks[1:2] + marks[2:3]), 0.0))
        live.append(prev == first)
        prev = last
    total = jnp.zeros((HALF, HD), F32)
    for b in range(CTX):
        out_ref[b, 0:HALF, :] = jnp.where(live[b], total, 0.0).astype(BF)
        total = rates[b] * total + in_ref[b, 0:HALF, :].astype(F32)
    total = jnp.zeros((HALF, HD), F32)
    for b in reversed(range(CTX)):
        out_ref[b, HALF:, :] = total.astype(BF)
        total = rates[b] * total + jnp.where(live[b], in_ref[b, HALF:HD, :].astype(F32), 0.0)


def attention_kernel(*refs):
    sources, carried_ref, (gq_ref, gk_ref, gv_ref), (decay_ref, doc_ref, q_ref, k_ref, v_ref, g_ref), sems = (
        refs[:6], refs[6], refs[7:10], refs[10:16], refs[16]
    )
    copies = fetch(tuple(zip(sources, refs[10:16])), sems)
    copies[0].wait()
    copies[1].wait()
    row, turned = sums_of_decay(decay_ref[...], doc_ref[...])
    cum_c, doc_c, first_w, end_w = weights_of(turned)
    seen = lax.broadcasted_iota(I32, (TOK, TOK), 0) >= lax.broadcasted_iota(I32, (TOK, TOK), 1)
    same = seen & (doc_c[:, 0:1] == row[HEADS : HEADS + 1])
    for copy in copies[2:]:
        copy.wait()
    for h in range(HEADS):
        cols = slice(h * HD, (h + 1) * HD)
        q, k, v, g = q_ref[:, cols], k_ref[:, cols], v_ref[:, cols], g_ref[:, cols]
        spread = jnp.where(same, cum_c[:, h : h + 1] - row[h : h + 1], -1e30)
        decay = jnp.exp(spread)
        weighted_do = (decay * mm(g, v, NT)).astype(BF)
        weighted_qk = (decay * mm(q, k, NT)).astype(BF)
        incoming = jnp.concatenate([carried_ref[2 * h, 0:HALF, :], carried_ref[2 * h + 1, 0:HALF, :]], axis=0)
        adjoint = jnp.concatenate([carried_ref[2 * h, HALF:, :], carried_ref[2 * h + 1, HALF:, :]], axis=0)
        start = first_w[:, h : h + 1]
        end = end_w[:, h : h + 1]
        gq_ref[:, cols] = (mm(weighted_do, k) + start * mm(g, incoming, NT)).astype(BF)
        gk_ref[:, cols] = (mm(weighted_do, q, TN) + end * mm(v, adjoint, NT)).astype(BF)
        gv_ref[:, cols] = (mm(weighted_qk, g, TN) + end * mm(k, adjoint)).astype(BF)


def feature_block(place, offset, sibling):
    core = place[1]
    core = 1 - core if sibling else core
    return pl.multiple_of((((place[0] + offset) % RINGX) * 2 + core) * FEAT, FEAT)


ORDER = ((0, 0), (0, 1), (-1, 0), (-1, 1), (1, 0), (1, 1), (2, 0), (2, 1))
ALL = len(ORDER) * FEAT
OWN, EARLY = 2, 6
OUT_ORDER = (2, -1, 1, 0)


def forward_kernel(from_left, from_right, x_ref, d_ref, sems):
    pairs = ((from_left.at[:, pl.ds(0, FEAT)], x_ref), (from_right.at[:, pl.ds(FEAT, FEAT)], d_ref))
    for copy in fetch(pairs, sems):
        copy.wait()


def first_layer(place, blocks, chunks, weights, xs, ds, gate_up, down, sems, at=0):
    wg, wu, wd = weights
    stages = ([], [], [])
    for i, (offset, sibling) in enumerate(blocks):
        block = feature_block(place, offset, sibling)
        side, turned = pl.ds(i * FEAT, FEAT), pl.ds((at + i) * FEAT, FEAT)
        stages[0].append((wd.at[0, :, pl.ds(block, FEAT)], down.at[:, side]))
        stages[0].append((chunks[i].at[:, pl.ds(FEAT, FEAT)], ds.at[:, side]))
        stages[1].append((wg.at[0, pl.ds(block, FEAT), :], gate_up.at[turned, pl.ds(0, HID)]))
        stages[1].append((chunks[i].at[:, pl.ds(0, FEAT)], xs.at[:, side]))
        stages[2].append((wu.at[0, pl.ds(block, FEAT), :], gate_up.at[turned, pl.ds(HID, HID)]))
    return stages


def expert_own_kernel(place, a0, a1, wg, wu, wd, pre_hbm, hid_hbm, xs, ds, gate_up, down, pre, hid, sems, out_sems):
    stages = first_layer(place, ORDER[:OWN], (a0, a1), (wg, wu, wd), xs, ds, gate_up, down, sems)
    copies = fetch(stages[0] + stages[1] + stages[2], sems)

    def ready(n):
        for _ in range(n):
            copies.pop(0).wait()

    ready(len(stages[0]))
    hid[...] = mm(ds[...], down[...], NT)
    leaving = [pltpu.make_async_copy(hid, hid_hbm, out_sems.at[0]), pltpu.make_async_copy(pre, pre_hbm, out_sems.at[1])]
    leaving[0].start()
    ready(len(stages[1]))
    pre[:, :HID] = mm(xs[...], gate_up[:, :HID])
    ready(len(stages[2]))
    pre[:, HID:] = mm(xs[...], gate_up[:, HID:])
    leaving[1].start()
    for copy in leaving:
        copy.wait()


def expert_early_kernel(place, *refs):
    chunks, (wg, wu, wd, pre_hbm, hid_hbm) = refs[:4], refs[4:9]
    (pre, hid, cat, down_late), (xs, ds, down_w, sums, hids, sems) = refs[-10:-6], refs[-6:]
    stages = first_layer(place, ORDER[OWN:EARLY], chunks, (wg, wu, wd), xs, ds, cat, down_w, sems, at=OWN)
    stages[0].append((hid_hbm, hids))
    stages[1].append((pre_hbm.at[:, pl.ds(0, HID)], sums.at[:, pl.ds(0, HID)]))
    stages[2].append((pre_hbm.at[:, pl.ds(HID, HID)], sums.at[:, pl.ds(HID, HID)]))
    rest = []
    for i, (offset, sibling) in enumerate(ORDER):
        block = feature_block(place, offset, sibling)
        if i >= EARLY:
            rest.append((wd.at[0, :, pl.ds(block, FEAT)], down_late.at[:, pl.ds((i - EARLY) * FEAT, FEAT)]))
        if i >= EARLY or i < OWN:
            rest.append((wg.at[0, pl.ds(block, FEAT), :], cat.at[pl.ds(i * FEAT, FEAT), pl.ds(0, HID)]))
            rest.append((wu.at[0, pl.ds(block, FEAT), :], cat.at[pl.ds(i * FEAT, FEAT), pl.ds(HID, HID)]))
    copies = fetch(stages[0] + stages[1] + stages[2] + rest, sems)

    def ready(n):
        for _ in range(n):
            copies.pop(0).wait()

    lines = slice(OWN * FEAT, EARLY * FEAT)
    ready(len(stages[0]))
    hid[...] = hids[...] + mm(ds[...], down_w[...], NT)
    ready(len(stages[1]))
    pre[:, :HID] = sums[:, :HID] + mm(xs[...], cat[lines, :HID])
    ready(len(stages[2]))
    pre[:, HID:] = sums[:, HID:] + mm(xs[...], cat[lines, HID:])
    ready(len(rest))


def out_block(mid_ref, cat, offset, sibling):
    at = ORDER.index((offset, sibling)) * FEAT
    return mm(mid_ref[...], cat[at : at + FEAT, :], NT)


def expert_far_kernel(pre, hid, x, d, cat, down_late, pre_ref, hid_ref):
    hid_ref[...] = hid[...] + mm(d[...], down_late[:, :FEAT], NT)
    pre_ref[...] = pre[...] + mm(x[...], cat[EARLY * FEAT : (EARLY + 1) * FEAT, :])


def expert_mid_kernel(pre, hid_ref, x, d, cat, down_late, mid_ref, far_ref):
    hid = hid_ref[...] + mm(d[...], down_late[:, FEAT:], NT)
    both = pre[...] + mm(x[...], cat[(EARLY + 1) * FEAT :, :])
    gate, up = both[:, :HID], both[:, HID:]
    s = 1.0 / (1.0 + jnp.exp(-gate))
    mid_ref[:, :HID] = (hid * up * s * (1.0 + gate * (1.0 - s))).astype(BF)
    mid_ref[:, HID:] = (hid * gate * s).astype(BF)
    far_ref[...] = out_block(mid_ref, cat, OUT_ORDER[0], 1).astype(BF)


def expert_out_kernel(mid_ref, cat, far_ref, rest_ref):
    far_ref[...] = out_block(mid_ref, cat, OUT_ORDER[0], 0)
    for i, offset in enumerate(OUT_ORDER[1:]):
        rest_ref[i] = out_block(mid_ref, cat, offset, 1).astype(BF)


def expert_rest_kernel(mid_ref, cat, rest_ref):
    for i, offset in enumerate(OUT_ORDER[1:]):
        rest_ref[i] = out_block(mid_ref, cat, offset, 0)


def far_kernel(mine, away, right_ref, left_ref):
    right_ref[...] = (mine[:CUT] + away[:CUT].astype(F32)).astype(BF)
    left_ref[...] = (mine[CUT:] + away[CUT:].astype(F32)).astype(BF)


def near_kernel(mine, away, via_right, via_left, left_ref, right_ref, here_ref):
    left_ref[:CUT] = (mine[0, :CUT] + away[0, :CUT].astype(F32)).astype(BF)
    left_ref[CUT:] = (mine[0, CUT:] + away[0, CUT:].astype(F32) + via_left[...].astype(F32)).astype(BF)
    right_ref[:CUT] = (mine[1, :CUT] + away[1, :CUT].astype(F32) + via_right[...].astype(F32)).astype(BF)
    right_ref[CUT:] = (mine[1, CUT:] + away[1, CUT:].astype(F32)).astype(BF)
    here_ref[...] = mine[2] + away[2].astype(F32)


def local(
    queries, keys, values, out_grad, log_decay, doc_ids, moe_input, moe_cotangent, router_weights, expert_ids, w_gate, w_up, w_down
):
    S = jax.ShapeDtypeStruct
    place = jnp.stack([lax.axis_index("x"), lax.axis_index("core")]).astype(I32)
    smem = pl.BlockSpec(memory_space=pltpu.SMEM)
    block = S((ROWS, FEAT), BF)
    tie = lax.optimization_barrier

    def ring(value, way):
        return lax.ppermute(value, "x", way)

    def swap(value):
        return lax.ppermute(value, "core", SWAP)

    rows, slots = call(
        pack_kernel,
        (S((ROWS, 2 * FEAT), BF), pltpu.HBM((2, TOK), I32)),
        [anywhere()] * 3,
        [pltpu.VMEM((2, TOK), I32)] + [pltpu.VMEM((TOK, FEAT), BF)] * 2 + [pltpu.VMEM((2, TOK), I32), pltpu.SemaphoreType.DMA((4,))],
        flops=2 * ROWS * TOK * 2 * FEAT,
        size=2 * MIB,
        limit=6,
    )(in_hbm(expert_ids.T), in_hbm(moe_input), in_hbm(moe_cotangent))
    own = lax.all_to_all(rows.reshape(CTX, CAP, 2 * FEAT), "ctx", 0, 0, tiled=True).reshape(ROWS, 2 * FEAT)
    from_left, from_right = ring(own, RIGHT), ring(own, LEFT)

    branch = [in_hbm(a) for a in (log_decay, doc_ids.reshape(1, TOK), queries, keys, values, out_grad)]
    held = [pltpu.VMEM((HEADS, TOK), F32), pltpu.VMEM((1, TOK), I32)] + [pltpu.VMEM((TOK, HEADS * HD), BF)] * 4
    held += [pltpu.SemaphoreType.DMA((6,))]
    message = call(
        state_kernel,
        S((CTX, HD + MARKS, HD), BF),
        [anywhere()] * 7,
        held,
        flops=4 * HEADS * TOK * HD * HD,
        size=3 * MIB,
        limit=8,
    )(*branch, own)
    arrived = lax.all_to_all(message, "ctx", 0, 0, tiled=True)
    weights = [in_hbm(w) for w in (w_gate, w_up, w_down)]
    own_s = swap(own)
    n = OWN * FEAT
    pre, hid = call(
        expert_own_kernel,
        (pltpu.HBM((ROWS, 2 * HID), F32), pltpu.HBM((ROWS, HID), F32)),
        [smem] + [anywhere()] * 5,
        [pltpu.VMEM((ROWS, n), BF)] * 2
        + [pltpu.VMEM((n, 2 * HID), BF), pltpu.VMEM((HID, n), BF), pltpu.VMEM((ROWS, 2 * HID), F32), pltpu.VMEM((ROWS, HID), F32)]
        + [pltpu.SemaphoreType.DMA((5 * OWN,)), pltpu.SemaphoreType.DMA((2,))],
        flops=6 * ROWS * HID * n,
        size=12 * MIB,
        limit=20,
    )(place, own, own_s, *weights)
    from_left, from_right, arrived, pre = tie((from_left, from_right, arrived, pre))

    x_far, d_far = call(
        forward_kernel,
        (block, block),
        [anywhere()] * 2,
        [pltpu.SemaphoreType.DMA((2,))],
        size=2 * MIB,
        limit=4,
    )(from_left, from_right)
    x_far, d_far, from_left, from_right = tie((x_far, d_far, from_left, from_right))
    x_far, d_far = ring(x_far, RIGHT), ring(d_far, LEFT)
    early = [c for a in (from_left, from_right) for c in (a, swap(a))]

    scanned = call(scan_kernel, S((CTX, HD, HD), BF), [vmem()], flops=MIB, size=MIB, limit=4)(arrived)
    n = (EARLY - OWN) * FEAT
    pre, hid, cat, down_late = call(
        expert_early_kernel,
        (S((ROWS, 2 * HID), F32), S((ROWS, HID), F32), S((ALL, 2 * HID), BF), S((HID, ALL - EARLY * FEAT), BF)),
        [smem] + [anywhere()] * 10,
        [pltpu.VMEM((ROWS, n), BF)] * 2
        + [pltpu.VMEM((HID, n), BF), pltpu.VMEM((ROWS, 2 * HID), F32), pltpu.VMEM((ROWS, HID), F32)]
        + [pltpu.SemaphoreType.DMA((34,))],
        flops=6 * ROWS * HID * n,
        size=24 * MIB,
        limit=32,
    )(place, *early, *weights, in_hbm(pre), in_hbm(hid), scanned)
    x_far, d_far, pre = tie((x_far, d_far, pre))
    rest = (RINGX - 1, ROWS, FEAT)
    x_swapped, d_swapped = swap(x_far), swap(d_far)
    pre, hid = call(
        expert_far_kernel,
        (S((ROWS, 2 * HID), F32), S((ROWS, HID), F32)),
        [vmem()] * 6,
        flops=6 * ROWS * HID * FEAT,
        size=10 * MIB,
        limit=24,
    )(pre, hid, x_far, d_far, cat, down_late)
    mid, away_far = call(
        expert_mid_kernel,
        (S((ROWS, 2 * HID), BF), block),
        [vmem()] * 6,
        flops=8 * ROWS * HID * 2 * FEAT,
        size=12 * MIB,
        limit=30,
    )(pre, hid, x_swapped, d_swapped, cat, down_late)
    away_far = swap(away_far)
    mine_far, away_rest = call(
        expert_out_kernel,
        (S((ROWS, FEAT), F32), S(rest, BF)),
        [vmem()] * 2,
        flops=4 * ROWS * HID * RINGX * FEAT,
        size=8 * MIB,
        limit=18,
    )(mid, cat)

    half = S((CUT, FEAT), BF)
    to_right, to_left = call(far_kernel, (half, half), [vmem()] * 2, size=2 * MIB, flops=MIB, limit=8)(mine_far, away_far)
    mid, away_rest, to_right, to_left = tie((mid, away_rest, to_right, to_left))
    away_rest = swap(away_rest)
    mine_rest = call(
        expert_rest_kernel,
        S(rest, F32),
        [vmem()] * 2,
        flops=3 * ROWS * HID * RINGX * FEAT,
        size=8 * MIB,
        limit=18,
    )(mid, cat)
    mine_rest, scanned = tie((mine_rest, scanned))
    via_right, via_left = ring(to_right, RIGHT), ring(to_left, LEFT)
    to_left, to_right, here = call(
        near_kernel, (block, block, S((ROWS, FEAT), F32)), [vmem()] * 4, size=5 * MIB, flops=MIB, limit=16
    )(mine_rest, away_rest, via_right, via_left)
    summed = (here + ring(to_right, RIGHT).astype(F32) + ring(to_left, LEFT).astype(F32)).astype(BF)
    carried = lax.all_to_all(scanned, "ctx", 0, 0, tiled=True)
    grads = call(
        attention_kernel,
        (S((TOK, HEADS * HD), BF),) * 3,
        [anywhere()] * 6 + [vmem()],
        held,
        flops=16 * HEADS * TOK * TOK * HD,
        size=4 * MIB,
        limit=12,
    )(*branch, carried)

    back = lax.all_to_all(summed.reshape(CTX, CAP, FEAT), "ctx", 0, 0, tiled=True)
    grad_moe = call(
        combine_kernel,
        S((TOK, FEAT), BF),
        [vmem()] * 3,
        flops=4 * ROWS * TOK * FEAT,
        size=MIB,
        limit=8,
    )(back.reshape(ROWS, FEAT), slots, router_weights.T)
    return (*grads, grad_moe)


def solution(mesh):
    fine = Mesh(mesh.devices.reshape(CTX, RINGX, 2), ("ctx", "x", "core"))
    ep = ("x", "core")
    row = P("ctx", ep)
    in_specs = (row, row, row, row, P(ep, "ctx"), P("ctx"), row, row, P("ctx", None), P("ctx", None))
    in_specs += (P("ctx", None, ep), P("ctx", None, ep), P("ctx", ep, None))
    return jax.shard_map(local, mesh=fine, in_specs=in_specs, out_specs=(row,) * 4, check_vma=False)
```

```python
import jax
import jax.numpy as jnp
from jax import lax
from jax.experimental import pallas as pl
from jax.experimental.pallas import tpu as pltpu
from jax.sharding import Mesh, PartitionSpec as P

BF = jnp.bfloat16
F32 = jnp.float32
I32 = jnp.int32
TOK = 256
HEADS = 8
HD = 128
HALF = HD // 2
CTX = 16
CAP = 40
ROWS = CTX * CAP
CUT = ROWS // 2
FEAT = 384
HID = 640
MARKS = 16
RINGX = 4
RIGHT = [(i, (i + 1) % RINGX) for i in range(RINGX)]
LEFT = [(i, (i - 1) % RINGX) for i in range(RINGX)]
SWAP = [(0, 1), (1, 0)]
MIB = 1 << 20

NT = (((1,), (1,)), ((), ()))
TN = (((0,), (0,)), ((), ()))


def vmem():
    return pl.BlockSpec(memory_space=pltpu.VMEM)


def anywhere():
    return pl.BlockSpec(memory_space=pl.ANY)


def in_hbm(value):
    return pltpu.with_memory_space_constraint(value, pltpu.HBM)


def call(kernel, outs, ins, scratch=(), flops=0, size=0, limit=32):
    return pl.pallas_call(
        kernel,
        out_shape=outs,
        in_specs=ins,
        out_specs=jax.tree.map(lambda o: vmem() if isinstance(o, jax.ShapeDtypeStruct) else anywhere(), outs),
        scratch_shapes=scratch,
        compiler_params=pltpu.CompilerParams(vmem_limit_bytes=limit * MIB),
        cost_estimate=pl.CostEstimate(flops=flops, bytes_accessed=size, transcendentals=0),
    )


def fetch(pairs, sems):
    copies = [pltpu.make_async_copy(src, dst, sems.at[i]) for i, (src, dst) in enumerate(pairs)]
    for copy in copies:
        copy.start()
    return copies


def mm(a, b, dims=(((1,), (0,)), ((), ()))):
    return lax.dot_general(a, b, dims, preferred_element_type=F32)


def onehot(slot):
    return lax.broadcasted_iota(I32, (ROWS, TOK), 0) == slot


def slots_of(ids):
    expert = lax.broadcasted_iota(I32, (CTX, TOK), 0)
    named = [ids[k : k + 1] == expert for k in range(2)]
    hits = jnp.where(named[0] | named[1], 1.0, 0.0).astype(BF)
    before = lax.broadcasted_iota(I32, (TOK, TOK), 0) < lax.broadcasted_iota(I32, (TOK, TOK), 1)
    rank = mm(hits, jnp.where(before, 1.0, 0.0).astype(BF))
    places = [jnp.sum(jnp.where(m, rank, 0.0), axis=0, keepdims=True).astype(I32) for m in named]
    return [ids[k : k + 1] * CAP + places[k] for k in range(2)]


def pack_kernel(ids_hbm, x_hbm, d_hbm, rows_ref, slots_hbm, ids_ref, x_ref, d_ref, slots_ref, sems):
    copies = fetch(((ids_hbm, ids_ref), (x_hbm, x_ref), (d_hbm, d_ref)), sems)
    copies[0].wait()
    slots = slots_of(ids_ref[...])
    slots_ref[0:1, :], slots_ref[1:2, :] = slots
    leaving = pltpu.make_async_copy(slots_ref, slots_hbm, sems.at[3])
    leaving.start()
    pick = jnp.where(onehot(slots[0]) | onehot(slots[1]), 1.0, 0.0).astype(BF)
    copies[1].wait()
    rows_ref[:, :FEAT] = mm(pick, x_ref[...]).astype(BF)
    copies[2].wait()
    rows_ref[:, FEAT:] = mm(pick, d_ref[...]).astype(BF)
    leaving.wait()


def combine_kernel(rows_ref, slots_ref, weights_ref, out_ref):
    columns = jnp.concatenate([weights_ref[...], jnp.zeros((6, TOK), F32)], axis=0).T
    total = jnp.zeros((TOK, FEAT), F32)
    for k in range(2):
        pick = jnp.where(onehot(slots_ref[k : k + 1, :]), 1.0, 0.0).astype(BF)
        total += columns[:, k : k + 1] * mm(pick, rows_ref[...], TN)
    out_ref[...] = total.astype(BF)


def sums_of_decay(decay, doc):
    upto = lax.broadcasted_iota(I32, (TOK, TOK), 0) <= lax.broadcasted_iota(I32, (TOK, TOK), 1)
    cum = lax.dot_general(
        decay,
        jnp.where(upto, 1.0, 0.0),
        (((1,), (0,)), ((), ())),
        precision=lax.Precision.HIGHEST,
        preferred_element_type=F32,
    )
    both = jnp.concatenate([cum, jnp.broadcast_to(doc.astype(F32), (HEADS, TOK))], axis=0)
    return both, both.T


def weights_of(turned):
    cum, doc = turned[:, :HEADS], turned[:, HEADS:]
    first_w = jnp.where(doc == doc[0:1], jnp.exp(cum), 0.0)
    end_w = jnp.where(doc == doc[TOK - 1 :], jnp.exp(cum[TOK - 1 :] - cum), 0.0)
    return cum, doc, first_w, end_w


def state_kernel(*refs):
    sources, out_ref, (decay_ref, doc_ref, q_ref, k_ref, v_ref, g_ref), sems = refs[:6], refs[7], refs[8:14], refs[14]
    copies = fetch(tuple(zip(sources, refs[8:14])), sems)
    copies[0].wait()
    copies[1].wait()
    _, turned = sums_of_decay(decay_ref[...], doc_ref[...])
    cum_c, doc_c, first_w, end_w = weights_of(turned)
    total, first, last = cum_c[TOK - 1 :], doc_c[0:1], doc_c[TOK - 1 :]
    line = lax.broadcasted_iota(I32, (MARKS, HD), 0)
    for copy in copies[2:]:
        copy.wait()
    for h in range(HEADS):
        cols = slice(h * HD, (h + 1) * HD)
        keys_end = (end_w[:, h : h + 1] * k_ref[:, cols].astype(F32)).astype(BF)
        queries_first = (first_w[:, h : h + 1] * q_ref[:, cols].astype(F32)).astype(BF)
        state = mm(keys_end, v_ref[:, cols], TN).astype(BF)
        adjoint = mm(queries_first, g_ref[:, cols], TN).astype(BF)
        sum_h = jnp.broadcast_to(total[:, h : h + 1], (MARKS, HD))
        high = sum_h.astype(BF).astype(F32)
        mid = (sum_h - high).astype(BF).astype(F32)
        low = sum_h - high - mid
        marks = jnp.where(line == 0, high, jnp.where(line == 1, mid, jnp.where(line == 2, low, 0.0)))
        marks = jnp.where(line == 3, first[:, h : h + 1], jnp.where(line == 4, last[:, h : h + 1], marks))
        for part in range(2):
            lines = slice(part * HALF, (part + 1) * HALF)
            out_ref[2 * h + part, 0:HALF, :] = state[lines]
            out_ref[2 * h + part, HALF:HD, :] = adjoint[lines]
            out_ref[2 * h + part, HD:, :] = marks.astype(BF)


def scan_kernel(in_ref, out_ref):
    rates, live = [], []
    prev = jnp.full((1, HD), -1.0, F32)
    for b in range(CTX):
        marks = in_ref[b, HD:, :].astype(F32)
        first, last = marks[3:4], marks[4:5]
        rates.append(jnp.where(prev == last, jnp.exp(marks[0:1] + marks[1:2] + marks[2:3]), 0.0))
        live.append(prev == first)
        prev = last
    total = jnp.zeros((HALF, HD), F32)
    for b in range(CTX):
        out_ref[b, 0:HALF, :] = jnp.where(live[b], total, 0.0).astype(BF)
        total = rates[b] * total + in_ref[b, 0:HALF, :].astype(F32)
    total = jnp.zeros((HALF, HD), F32)
    for b in reversed(range(CTX)):
        out_ref[b, HALF:, :] = total.astype(BF)
        total = rates[b] * total + jnp.where(live[b], in_ref[b, HALF:HD, :].astype(F32), 0.0)


def attention_kernel(*refs):
    sources, carried_ref, (gq_ref, gk_ref, gv_ref), (decay_ref, doc_ref, q_ref, k_ref, v_ref, g_ref), sems = (
        refs[:6], refs[6], refs[7:10], refs[10:16], refs[16]
    )
    copies = fetch(tuple(zip(sources, refs[10:16])), sems)
    copies[0].wait()
    copies[1].wait()
    row, turned = sums_of_decay(decay_ref[...], doc_ref[...])
    cum_c, doc_c, first_w, end_w = weights_of(turned)
    seen = lax.broadcasted_iota(I32, (TOK, TOK), 0) >= lax.broadcasted_iota(I32, (TOK, TOK), 1)
    same = seen & (doc_c[:, 0:1] == row[HEADS : HEADS + 1])
    for copy in copies[2:]:
        copy.wait()
    for h in range(HEADS):
        cols = slice(h * HD, (h + 1) * HD)
        q, k, v, g = q_ref[:, cols], k_ref[:, cols], v_ref[:, cols], g_ref[:, cols]
        spread = jnp.where(same, cum_c[:, h : h + 1] - row[h : h + 1], -1e30)
        decay = jnp.exp(spread)
        weighted_do = (decay * mm(g, v, NT)).astype(BF)
        weighted_qk = (decay * mm(q, k, NT)).astype(BF)
        incoming = jnp.concatenate([carried_ref[2 * h, 0:HALF, :], carried_ref[2 * h + 1, 0:HALF, :]], axis=0)
        adjoint = jnp.concatenate([carried_ref[2 * h, HALF:, :], carried_ref[2 * h + 1, HALF:, :]], axis=0)
        start = first_w[:, h : h + 1]
        end = end_w[:, h : h + 1]
        gq_ref[:, cols] = (mm(weighted_do, k) + start * mm(g, incoming, NT)).astype(BF)
        gk_ref[:, cols] = (mm(weighted_do, q, TN) + end * mm(v, adjoint, NT)).astype(BF)
        gv_ref[:, cols] = (mm(weighted_qk, g, TN) + end * mm(k, adjoint)).astype(BF)


def feature_block(place, offset, sibling):
    core = place[1]
    core = 1 - core if sibling else core
    return pl.multiple_of((((place[0] + offset) % RINGX) * 2 + core) * FEAT, FEAT)


ORDER = ((0, 0), (0, 1), (-1, 0), (-1, 1), (1, 0), (1, 1), (2, 0), (2, 1))
ALL = len(ORDER) * FEAT
OWN, EARLY = 2, 6
OUT_ORDER = (2, -1, 1, 0)


def forward_kernel(from_left, from_right, x_ref, d_ref, sems):
    pairs = ((from_left.at[:, pl.ds(0, FEAT)], x_ref), (from_right.at[:, pl.ds(FEAT, FEAT)], d_ref))
    for copy in fetch(pairs, sems):
        copy.wait()


def first_layer(place, blocks, chunks, weights, xs, ds, gate_up, down, sems, at=0):
    wg, wu, wd = weights
    stages = ([], [], [])
    for i, (offset, sibling) in enumerate(blocks):
        block = feature_block(place, offset, sibling)
        side, turned = pl.ds(i * FEAT, FEAT), pl.ds((at + i) * FEAT, FEAT)
        stages[0].append((wd.at[0, :, pl.ds(block, FEAT)], down.at[:, side]))
        stages[0].append((chunks[i].at[:, pl.ds(FEAT, FEAT)], ds.at[:, side]))
        stages[1].append((wg.at[0, pl.ds(block, FEAT), :], gate_up.at[turned, pl.ds(0, HID)]))
        stages[1].append((chunks[i].at[:, pl.ds(0, FEAT)], xs.at[:, side]))
        stages[2].append((wu.at[0, pl.ds(block, FEAT), :], gate_up.at[turned, pl.ds(HID, HID)]))
    return stages


def expert_own_kernel(place, a0, a1, wg, wu, wd, pre_hbm, hid_hbm, xs, ds, gate_up, down, pre, hid, sems, out_sems):
    stages = first_layer(place, ORDER[:OWN], (a0, a1), (wg, wu, wd), xs, ds, gate_up, down, sems)
    copies = fetch(stages[0] + stages[1] + stages[2], sems)

    def ready(n):
        for _ in range(n):
            copies.pop(0).wait()

    ready(len(stages[0]))
    hid[...] = mm(ds[...], down[...], NT)
    leaving = [pltpu.make_async_copy(hid, hid_hbm, out_sems.at[0]), pltpu.make_async_copy(pre, pre_hbm, out_sems.at[1])]
    leaving[0].start()
    ready(len(stages[1]))
    pre[:, :HID] = mm(xs[...], gate_up[:, :HID])
    ready(len(stages[2]))
    pre[:, HID:] = mm(xs[...], gate_up[:, HID:])
    leaving[1].start()
    for copy in leaving:
        copy.wait()


def expert_early_kernel(place, *refs):
    chunks, (wg, wu, wd, pre_hbm, hid_hbm) = refs[:4], refs[4:9]
    (pre, hid, cat, down_late), (xs, ds, down_w, sums, hids, sems) = refs[-10:-6], refs[-6:]
    stages = first_layer(place, ORDER[OWN:EARLY], chunks, (wg, wu, wd), xs, ds, cat, down_w, sems, at=OWN)
    stages[0].append((hid_hbm, hids))
    stages[1].append((pre_hbm.at[:, pl.ds(0, HID)], sums.at[:, pl.ds(0, HID)]))
    stages[2].append((pre_hbm.at[:, pl.ds(HID, HID)], sums.at[:, pl.ds(HID, HID)]))
    rest = []
    for i, (offset, sibling) in enumerate(ORDER):
        block = feature_block(place, offset, sibling)
        if i >= EARLY:
            rest.append((wd.at[0, :, pl.ds(block, FEAT)], down_late.at[:, pl.ds((i - EARLY) * FEAT, FEAT)]))
        if i >= EARLY or i < OWN:
            rest.append((wg.at[0, pl.ds(block, FEAT), :], cat.at[pl.ds(i * FEAT, FEAT), pl.ds(0, HID)]))
            rest.append((wu.at[0, pl.ds(block, FEAT), :], cat.at[pl.ds(i * FEAT, FEAT), pl.ds(HID, HID)]))
    copies = fetch(stages[0] + stages[1] + stages[2] + rest, sems)

    def ready(n):
        for _ in range(n):
            copies.pop(0).wait()

    lines = slice(OWN * FEAT, EARLY * FEAT)
    ready(len(stages[0]))
    hid[...] = hids[...] + mm(ds[...], down_w[...], NT)
    ready(len(stages[1]))
    pre[:, :HID] = sums[:, :HID] + mm(xs[...], cat[lines, :HID])
    ready(len(stages[2]))
    pre[:, HID:] = sums[:, HID:] + mm(xs[...], cat[lines, HID:])
    ready(len(rest))


def out_block(mid_ref, cat, offset, sibling):
    at = ORDER.index((offset, sibling)) * FEAT
    return mm(mid_ref[...], cat[at : at + FEAT, :], NT)


def expert_far_kernel(pre, hid, x, d, cat, down_late, pre_ref, hid_ref):
    hid_ref[...] = hid[...] + mm(d[...], down_late[:, :FEAT], NT)
    pre_ref[...] = pre[...] + mm(x[...], cat[EARLY * FEAT : (EARLY + 1) * FEAT, :])


def expert_mid_kernel(pre, hid_ref, x, d, cat, down_late, mid_ref, far_ref):
    hid = hid_ref[...] + mm(d[...], down_late[:, FEAT:], NT)
    both = pre[...] + mm(x[...], cat[(EARLY + 1) * FEAT :, :])
    gate, up = both[:, :HID], both[:, HID:]
    s = 1.0 / (1.0 + jnp.exp(-gate))
    mid_ref[:, :HID] = (hid * up * s * (1.0 + gate * (1.0 - s))).astype(BF)
    mid_ref[:, HID:] = (hid * gate * s).astype(BF)
    far_ref[...] = out_block(mid_ref, cat, OUT_ORDER[0], 1).astype(BF)


def expert_out_kernel(mid_ref, cat, far_ref, rest_ref):
    far_ref[...] = out_block(mid_ref, cat, OUT_ORDER[0], 0)
    for i, offset in enumerate(OUT_ORDER[1:]):
        rest_ref[i] = out_block(mid_ref, cat, offset, 1).astype(BF)


def expert_rest_kernel(mid_ref, cat, rest_ref):
    for i, offset in enumerate(OUT_ORDER[1:]):
        rest_ref[i] = out_block(mid_ref, cat, offset, 0)


def far_kernel(mine, away, right_ref, left_ref):
    right_ref[...] = (mine[:CUT] + away[:CUT].astype(F32)).astype(BF)
    left_ref[...] = (mine[CUT:] + away[CUT:].astype(F32)).astype(BF)


def near_kernel(mine, away, via_right, via_left, left_ref, right_ref, here_ref):
    left_ref[:CUT] = (mine[0, :CUT] + away[0, :CUT].astype(F32)).astype(BF)
    left_ref[CUT:] = (mine[0, CUT:] + away[0, CUT:].astype(F32) + via_left[...].astype(F32)).astype(BF)
    right_ref[:CUT] = (mine[1, :CUT] + away[1, :CUT].astype(F32) + via_right[...].astype(F32)).astype(BF)
    right_ref[CUT:] = (mine[1, CUT:] + away[1, CUT:].astype(F32)).astype(BF)
    here_ref[...] = mine[2] + away[2].astype(F32)


def local(
    queries, keys, values, out_grad, log_decay, doc_ids, moe_input, moe_cotangent, router_weights, expert_ids, w_gate, w_up, w_down
):
    S = jax.ShapeDtypeStruct
    place = jnp.stack([lax.axis_index("x"), lax.axis_index("core")]).astype(I32)
    smem = pl.BlockSpec(memory_space=pltpu.SMEM)
    block = S((ROWS, FEAT), BF)
    tie = lax.optimization_barrier

    def ring(value, way):
        return lax.ppermute(value, "x", way)

    def swap(value):
        return lax.ppermute(value, "core", SWAP)

    rows, slots = call(
        pack_kernel,
        (S((ROWS, 2 * FEAT), BF), pltpu.HBM((2, TOK), I32)),
        [anywhere()] * 3,
        [pltpu.VMEM((2, TOK), I32)] + [pltpu.VMEM((TOK, FEAT), BF)] * 2 + [pltpu.VMEM((2, TOK), I32), pltpu.SemaphoreType.DMA((4,))],
        flops=2 * ROWS * TOK * 2 * FEAT,
        size=2 * MIB,
        limit=6,
    )(in_hbm(expert_ids.T), in_hbm(moe_input), in_hbm(moe_cotangent))
    own = lax.all_to_all(rows.reshape(CTX, CAP, 2 * FEAT), "ctx", 0, 0, tiled=True).reshape(ROWS, 2 * FEAT)
    from_left, from_right = ring(own, RIGHT), ring(own, LEFT)

    branch = [in_hbm(a) for a in (log_decay, doc_ids.reshape(1, TOK), queries, keys, values, out_grad)]
    held = [pltpu.VMEM((HEADS, TOK), F32), pltpu.VMEM((1, TOK), I32)] + [pltpu.VMEM((TOK, HEADS * HD), BF)] * 4
    held += [pltpu.SemaphoreType.DMA((6,))]
    message = call(
        state_kernel,
        S((CTX, HD + MARKS, HD), BF),
        [anywhere()] * 7,
        held,
        flops=4 * HEADS * TOK * HD * HD,
        size=3 * MIB,
        limit=8,
    )(*branch, own)
    arrived = lax.all_to_all(message, "ctx", 0, 0, tiled=True)
    weights = [in_hbm(w) for w in (w_gate, w_up, w_down)]
    own_s = swap(own)
    n = OWN * FEAT
    pre, hid = call(
        expert_own_kernel,
        (pltpu.HBM((ROWS, 2 * HID), F32), pltpu.HBM((ROWS, HID), F32)),
        [smem] + [anywhere()] * 5,
        [pltpu.VMEM((ROWS, n), BF)] * 2
        + [pltpu.VMEM((n, 2 * HID), BF), pltpu.VMEM((HID, n), BF), pltpu.VMEM((ROWS, 2 * HID), F32), pltpu.VMEM((ROWS, HID), F32)]
        + [pltpu.SemaphoreType.DMA((5 * OWN,)), pltpu.SemaphoreType.DMA((2,))],
        flops=6 * ROWS * HID * n,
        size=12 * MIB,
        limit=20,
    )(place, own, own_s, *weights)
    from_left, from_right, arrived, pre = tie((from_left, from_right, arrived, pre))

    x_far, d_far = call(
        forward_kernel,
        (block, block),
        [anywhere()] * 2,
        [pltpu.SemaphoreType.DMA((2,))],
        size=2 * MIB,
        limit=4,
    )(from_left, from_right)
    x_far, d_far = ring(x_far, RIGHT), ring(d_far, LEFT)
    early = [c for a in (from_left, from_right) for c in (a, swap(a))]

    scanned = call(scan_kernel, S((CTX, HD, HD), BF), [vmem()], flops=MIB, size=MIB, limit=4)(arrived)
    n = (EARLY - OWN) * FEAT
    pre, hid, cat, down_late = call(
        expert_early_kernel,
        (S((ROWS, 2 * HID), F32), S((ROWS, HID), F32), S((ALL, 2 * HID), BF), S((HID, ALL - EARLY * FEAT), BF)),
        [smem] + [anywhere()] * 10,
        [pltpu.VMEM((ROWS, n), BF)] * 2
        + [pltpu.VMEM((HID, n), BF), pltpu.VMEM((ROWS, 2 * HID), F32), pltpu.VMEM((ROWS, HID), F32)]
        + [pltpu.SemaphoreType.DMA((34,))],
        flops=6 * ROWS * HID * n,
        size=24 * MIB,
        limit=32,
    )(place, *early, *weights, in_hbm(pre), in_hbm(hid), scanned)
    x_far, d_far, pre = tie((x_far, d_far, pre))
    rest = (RINGX - 1, ROWS, FEAT)
    x_swapped, d_swapped = swap(x_far), swap(d_far)
    pre, hid = call(
        expert_far_kernel,
        (S((ROWS, 2 * HID), F32), S((ROWS, HID), F32)),
        [vmem()] * 6,
        flops=6 * ROWS * HID * FEAT,
        size=10 * MIB,
        limit=24,
    )(pre, hid, x_far, d_far, cat, down_late)
    mid, away_far = call(
        expert_mid_kernel,
        (S((ROWS, 2 * HID), BF), block),
        [vmem()] * 6,
        flops=8 * ROWS * HID * 2 * FEAT,
        size=12 * MIB,
        limit=30,
    )(pre, hid, x_swapped, d_swapped, cat, down_late)
    away_far = swap(away_far)
    mine_far, away_rest = call(
        expert_out_kernel,
        (S((ROWS, FEAT), F32), S(rest, BF)),
        [vmem()] * 2,
        flops=4 * ROWS * HID * RINGX * FEAT,
        size=8 * MIB,
        limit=18,
    )(mid, cat)

    half = S((CUT, FEAT), BF)
    to_right, to_left = call(far_kernel, (half, half), [vmem()] * 2, size=2 * MIB, flops=MIB, limit=8)(mine_far, away_far)
    mid, away_rest, to_right, to_left = tie((mid, away_rest, to_right, to_left))
    away_rest = swap(away_rest)
    mine_rest = call(
        expert_rest_kernel,
        S(rest, F32),
        [vmem()] * 2,
        flops=3 * ROWS * HID * RINGX * FEAT,
        size=8 * MIB,
        limit=18,
    )(mid, cat)
    mine_rest, scanned = tie((mine_rest, scanned))
    via_right, via_left = ring(to_right, RIGHT), ring(to_left, LEFT)
    to_left, to_right, here = call(
        near_kernel, (block, block, S((ROWS, FEAT), F32)), [vmem()] * 4, size=5 * MIB, flops=MIB, limit=16
    )(mine_rest, away_rest, via_right, via_left)
    summed = (here + ring(to_right, RIGHT).astype(F32) + ring(to_left, LEFT).astype(F32)).astype(BF)
    carried = lax.all_to_all(scanned, "ctx", 0, 0, tiled=True)
    grads = call(
        attention_kernel,
        (S((TOK, HEADS * HD), BF),) * 3,
        [anywhere()] * 6 + [vmem()],
        held,
        flops=16 * HEADS * TOK * TOK * HD,
        size=4 * MIB,
        limit=12,
    )(*branch, carried)

    back = lax.all_to_all(summed.reshape(CTX, CAP, FEAT), "ctx", 0, 0, tiled=True)
    grad_moe = call(
        combine_kernel,
        S((TOK, FEAT), BF),
        [vmem()] * 3,
        flops=4 * ROWS * TOK * FEAT,
        size=MIB,
        limit=8,
    )(back.reshape(ROWS, FEAT), slots, router_weights.T)
    return (*grads, grad_moe)


def solution(mesh):
    fine = Mesh(mesh.devices.reshape(CTX, RINGX, 2), ("ctx", "x", "core"))
    ep = ("x", "core")
    row = P("ctx", ep)
    in_specs = (row, row, row, row, P(ep, "ctx"), P("ctx"), row, row, P("ctx", None), P("ctx", None))
    in_specs += (P("ctx", None, ep), P("ctx", None, ep), P("ctx", ep, None))
    return jax.shard_map(local, mesh=fine, in_specs=in_specs, out_specs=(row,) * 4, check_vma=False)
```
